256 devices in a mesh: feat: 64 (over z, y, core), sect: 4 (over x).
Axes of the slice: x: 4, y: 4, z: 8, core: 2. Of those that a mesh axis runs over, the one named last changes fastest.
Arguments:
- table: bfloat16 [32768, 1024], P('feat'), may hold values from -6 to 6
- hop2_owner: int32 [102400, 1], P(('feat', 'sect')), may hold values from 0 to 63; in each aligned block of 400 rows (0 to 399, 400 to 799, ...) at most 12 rows name the same one
- hop2_row: int32 [102400], P(('feat', 'sect')), may hold values from 0 to 511
- hop2_weight: int32 [102400], P(('feat', 'sect')), may hold values from 1 to 32
- hop1_feats: bfloat16 [5120, 1024], P(('feat', 'sect')), may hold values from -24 to 24
- hop1_weight: int32 [5120], P(('feat', 'sect')), may hold values from 1 to 32
- target_feats: bfloat16 [256, 1024], P('feat'), may hold values from -6 to 6
- cotangent: bfloat16 [256, 1024], P('feat'), may hold values from -6 to 6
- layer_one: bfloat16 [1024, 3072], P('feat'), may hold values from -0.1875 to 0.1875
- layer_two: bfloat16 [1024, 3072], replicated, may hold values from -0.1875 to 0.1875
Outputs:
- embedding: bfloat16 [256, 1024], P(('feat', 'sect'))
- grads: float32 [1024, 3072], P(('feat', 'sect'))
The draws below stay inside these ranges and needn't reach their ends.
Inputs may be any that keep to these rules, and one draw needn't show every extreme that they name: `hop2_owner`: among the 400 rows of one device no shard is named more than 12 times.
All inputs are finite; a program needn't handle non-finite values.
Results may differ from the reference program's by a relative error of at most 0.0095.
Values may be sent and summed in bfloat16 or wider, within the bound.
A program may use at most 128 MiB of HBM per device.

```python
import math
import jax
import jax.numpy as jnp
import numpy as np
from jax import lax

D = 1024
K1 = 20
K2 = 20
TGT_DEV = 4
ROWS_DEV = 512
KS = 5
HOP1_DEV = 20
HOP2_DEV = 400
CAP = 12
TARGETS = 256
HOP1 = 5120
HOP2 = 102400
PINS = 32768
N_FEAT = 64
N_SECT = 4


def with_ends(entries, stream_key, least, top_value):
    extent = entries.shape
    index_at = [jax.random.randint(jax.random.fold_in(stream_key, axis), (), 0, extent[axis]) for axis in range(len(extent))]
    entries = entries.at[tuple(index_at)].set(least)
    longest = extent.index(max(extent))
    index_at[longest] = (index_at[longest] + 1) % extent[longest]
    return entries.at[tuple(index_at)].set(top_value)


def strengthened(array, stream_key, source, target, blocks, factor):
    owner, partner = [(jnp.arange(array.shape[dim]) // (array.shape[dim] // blocks)).reshape([-1 if axis == dim else 1 for axis in range(array.ndim)]) for dim in (source, target)]
    chosen = jax.random.permutation(stream_key, blocks)[partner]
    strong = (owner == chosen) | (owner == (partner + blocks // 2) % blocks)
    return jnp.where(strong, factor * array, array)


def level_of(stream_key, shape, pieces, least, high):
    level, own = 1.0, jax.random.fold_in(stream_key, 6)
    for position, parts in pieces:
        draws = jnp.exp(jax.random.uniform(jax.random.fold_in(own, position), (parts,), jnp.float32, least / len(pieces), high / len(pieces)))
        level = level * jnp.repeat(draws, shape[position] // parts).reshape([-1 if axis == position else 1 for axis in range(len(shape))])
    return level


def shared_out(own_key, own, number, rows, count, top, most, lean):
    order = jax.random.permutation(own_key, count)
    packed, usual = shares(count, rows * top, most, lean, True), shares(count, rows * top, most, lean, False)
    places = jnp.arange(count)

    def named(sizes, rotation):
        used = int((sizes > 0).sum())
        fixed = max(1, used // 4)
        moved = fixed + (places - fixed + rotation * (used - fixed)) % max(1, count - fixed)
        return jnp.zeros((count,), jnp.int32).at[order[jnp.where(places < fixed, places, moved)]].set(jnp.asarray(sizes, jnp.int32))

    sizes = jnp.where(number % 4 == 0, named(packed, number // 4), named(usual, number - number // 4 - 1))
    mixed = jax.random.permutation(jax.random.fold_in(own, 3), count)
    donor, sink = mixed[0:count // 2 * 2:2], mixed[1:count // 2 * 2:2]
    margin = jnp.minimum(sizes[donor] - 1, most - sizes[sink]) // 2
    margin = jnp.where((donor == order[0]) | (sink == order[0]) | (sizes[sink] == 0), 0, jnp.maximum(margin, 0))
    moved = jax.random.randint(jax.random.fold_in(own, 4), (count // 2,), 0, 1 << 20) % (margin + 1)
    sizes = sizes.at[donor].add(-moved).at[sink].add(moved)
    members = jnp.searchsorted(jnp.cumsum(sizes), jnp.arange(rows * top), side="right").astype(jnp.int32)
    grid = members.reshape(top, rows).T
    grid = grid[jax.random.permutation(jax.random.fold_in(own, 1), rows)]
    rotation = jax.random.randint(jax.random.fold_in(own, 2), (rows, 1), 0, top)
    return jnp.take_along_axis(grid, (jnp.arange(top)[None, :] + rotation) % top, axis=1)


def shares(amount, total, bound, slope, full):
    weights = [(1 << 20) // math.isqrt(standing ** slope) + 1 for standing in range(1, amount + 1)]
    largest = bound if full else min(bound, max(-(-total // amount), total * weights[0] // sum(weights)))
    least = 1 if total - largest >= amount - 1 else 0
    counts, spare = [largest] + [least] * (amount - 1), total - largest - least * (amount - 1)
    while spare > 0:
        candidates = [i for i in range(1, amount) if counts[i] < largest] or [i for i in range(1, amount) if counts[i] < bound]
        mass, left = sum([weights[i] for i in candidates]), spare
        for i in candidates:
            extra = min(bound - counts[i], max(1, left * weights[i] // mass), spare)
            counts[i] = counts[i] + extra
            spare = spare - extra
    return np.array(counts)


def scatter_about(key, extent, deviation, reach, shards=(), held_as=jnp.bfloat16):
    loudness = level_of(key, extent, shards, -0.22, 0.18) if shards else 1.0
    array = jax.random.normal(key, extent, jnp.float32) * deviation * loudness
    return jnp.minimum(jnp.maximum(array, -reach), reach).astype(held_as)


def noise_with(rng, extent, scale, bound, shards, heavy, kind=jnp.bfloat16):
    values = scale * jax.random.normal(rng, extent, jnp.float32)
    if shards:
        values = values * level_of(rng, extent, shards, -0.22, 0.18)
    return jnp.clip(strengthened(values, jax.random.fold_in(rng, 3), *heavy), -bound, bound).astype(kind)


def setup_inputs(seed: int = 0) -> dict:
    key_of = jax.random.split(jax.random.key(seed), 11)
    table = scatter_about(key_of[0], (PINS, D), 1.0, 6.0, ((0, 64),))
    hop2_owner_keys = jax.random.split(jax.random.fold_in(key_of[1], 1), HOP2 // HOP2_DEV)
    hop2_owner_turns = jax.random.permutation(jax.random.fold_in(key_of[1], 3), HOP2 // HOP2_DEV)
    hop2_owner = jax.vmap(lambda own, number: shared_out(jax.random.fold_in(key_of[1], 2), own, number, HOP2_DEV, N_FEAT, 1, CAP, 2))(hop2_owner_keys, hop2_owner_turns).reshape((HOP2, 1))
    hop2_row = with_ends(jax.random.randint(key_of[2], (HOP2,), 0, ROWS_DEV), jax.random.fold_in(key_of[2], 1), 0, ROWS_DEV - 1).astype(jnp.int32)
    hop2_weight = with_ends(jax.random.randint(key_of[3], (HOP2,), 1, 33), jax.random.fold_in(key_of[3], 1), 1, 32).astype(jnp.int32)
    hop1_feats = noise_with(key_of[4], (HOP1, D), 1.0, 24.0, ((0, 256),), (0, 1, 256, 6.0))
    hop1_weight = with_ends(jax.random.randint(key_of[5], (HOP1,), 1, 33), jax.random.fold_in(key_of[5], 1), 1, 32).astype(jnp.int32)
    target_feats = scatter_about(key_of[6], (TARGETS, D), 1.0, 6.0, ((0, 64),))
    cotangent = scatter_about(key_of[7], (TARGETS, D), 1.0, 6.0, ((0, 64),))
    layer_one = scatter_about(key_of[8], (D, 3 * D), D ** -0.5, 0.1875, ((0, 64),))
    layer_two = scatter_about(key_of[9], (D, 3 * D), D ** -0.5, 0.1875)
    return {"table": table, "hop2_owner": hop2_owner, "hop2_row": hop2_row, "hop2_weight": hop2_weight, "hop1_feats": hop1_feats, "hop1_weight": hop1_weight, "target_feats": target_feats, "cotangent": cotangent, "layer_one": layer_one, "layer_two": layer_two}


EPS = 1e-05

def act(values):
    return values * jax.nn.sigmoid(values)

def act_slope(values):
    sig = jax.nn.sigmoid(values)
    return sig * (1.0 + values * (1.0 - sig))

def reorder(values):
    width = values.shape[-1]
    shaped = values.reshape(N_FEAT, N_SECT, TGT_DEV, KS, width)
    return shaped.transpose(0, 2, 1, 3, 4).reshape(TARGETS, K1, width)

def restore(values):
    width = values.shape[-1]
    shaped = values.reshape(N_FEAT, TGT_DEV, N_SECT, KS, width)
    return shaped.transpose(0, 2, 1, 3, 4).reshape(HOP1, width)

def reference(table, hop2_owner, hop2_row, hop2_weight, hop1_feats, hop1_weight, target_feats, cotangent, layer_one, layer_two):
    f32 = jnp.float32
    bf16 = jnp.bfloat16
    q_one = layer_one[:, :D]
    w_self = layer_one[:, D:2 * D]
    w_nbr = layer_one[:, 2 * D:]
    q_two = layer_two[:, :D]
    v_self = layer_two[:, D:2 * D]
    v_nbr = layer_two[:, 2 * D:]
    blocks = N_FEAT * N_SECT
    owner_b = hop2_owner[:, 0].reshape(blocks, HOP2_DEV)
    row_b = hop2_row.reshape(blocks, HOP2_DEV)
    weight_b = hop2_weight.reshape(blocks, HOP1_DEV, K2)

    def fetch(owner, row):
        ids = (owner * ROWS_DEV + row).astype(jnp.int32)
        return jnp.take(table, ids, axis=0)

    def pool(args):
        owner, row, weight = args
        fetched = fetch(owner, row)
        pre = jnp.dot(fetched, q_one, preferred_element_type=f32)
        trans = act(pre).reshape(HOP1_DEV, K2, D)
        imp = weight.astype(f32)
        return (lax.optimization_barrier(jnp.sum(imp[:, :, None] * trans, axis=1)) / lax.optimization_barrier(jnp.sum(imp, axis=1))[:, None]).astype(bf16)
    nbr1 = lax.map(pool, (owner_b, row_b, weight_b)).reshape(HOP1, D)
    pre1 = jnp.dot(hop1_feats, w_self, preferred_element_type=f32) + jnp.dot(nbr1, w_nbr, preferred_element_type=f32)
    gated1 = act(pre1)
    scale1 = lax.rsqrt(lax.optimization_barrier(jnp.mean(gated1 * gated1, axis=-1)) + EPS)
    norm1 = gated1 * scale1[:, None]
    h_one = norm1.astype(bf16)
    pre_hop1 = jnp.dot(h_one, q_two, preferred_element_type=f32)
    imp1 = reorder(hop1_weight.astype(f32)[:, None])[:, :, 0]
    pre_t = reorder(pre_hop1)
    total = lax.optimization_barrier(jnp.sum(imp1, axis=1))
    nbr2 = (lax.optimization_barrier(jnp.sum(imp1[:, :, None] * act(pre_t), axis=1)) / total[:, None]).astype(bf16)
    pre2 = jnp.dot(target_feats, v_self, preferred_element_type=f32) + jnp.dot(nbr2, v_nbr, preferred_element_type=f32)
    gated2 = act(pre2)
    scale2 = lax.rsqrt(lax.optimization_barrier(jnp.mean(gated2 * gated2, axis=-1)) + EPS)
    norm2 = gated2 * scale2[:, None]
    embedding = norm2.astype(bf16)
    cot = cotangent.astype(f32)
    dg2 = scale2[:, None] * (cot - norm2 * lax.optimization_barrier(jnp.mean(cot * norm2, axis=-1, keepdims=True)))
    back2 = (dg2 * act_slope(pre2)).astype(bf16)
    back_nbr2 = jnp.dot(back2, v_nbr.T, preferred_element_type=f32)
    coef1 = imp1 / total[:, None]
    back_t = (back_nbr2[:, None, :] * coef1[:, :, None] * act_slope(pre_t)).astype(bf16)
    back_hop1 = restore(back_t)
    back_h1 = jnp.dot(back_hop1, q_two.T, preferred_element_type=f32)
    dg1 = scale1[:, None] * (back_h1 - norm1 * lax.optimization_barrier(jnp.mean(back_h1 * norm1, axis=-1, keepdims=True)))
    back1 = (dg1 * act_slope(pre1)).astype(bf16)
    grad_self = jnp.dot(hop1_feats.T, back1, preferred_element_type=f32)
    grad_nbr = jnp.dot(nbr1.T, back1, preferred_element_type=f32)
    back_nbr1 = jnp.dot(back1, w_nbr.T, preferred_element_type=f32).reshape(blocks, HOP1_DEV, D)

    def back_step(acc, args):
        owner, row, weight, dnode = args
        fetched = fetch(owner, row)
        pre = jnp.dot(fetched, q_one, preferred_element_type=f32).reshape(HOP1_DEV, K2, D)
        imp = weight.astype(f32)
        coef = imp / lax.optimization_barrier(jnp.sum(imp, axis=1))[:, None]
        dfetch = (dnode[:, None, :] * coef[:, :, None] * act_slope(pre)).reshape(HOP2_DEV, D).astype(bf16)
        return (acc + jnp.dot(fetched.T, dfetch, preferred_element_type=f32), None)
    grad_q, unused = lax.scan(back_step, jnp.zeros((D, D), f32), (owner_b, row_b, weight_b, back_nbr1))
    return (embedding, jnp.concatenate([grad_q, grad_self, grad_nbr], axis=1))
```

```python
import functools
import jax
import jax.numpy as jnp
from jax import lax
from jax.experimental import pallas as pl
from jax.experimental.pallas import tpu as pltpu

MESH = pl.DeviceIdType.MESH
NZ, NY, NC, NX = 8, 4, 2, 4


def coords():
    feat = lax.axis_index("feat")
    sect = lax.axis_index("sect")
    return feat // (NY * NC), (feat // NC) % NY, feat % NC, sect


def device_at(z, y, c, x):
    return ((z * NY + y) * NC + c, x)


def row_pick(first, parity, width):
    half = width // 2
    m = lax.broadcasted_iota(jnp.int32, (half, width), 0)
    lane = lax.broadcasted_iota(jnp.int32, (half, width), 1)
    a, b, z, i = m // 128, (m // 32) % 4, (m // 4) % 8, m % 4
    y, x = (b, a) if first == "x" else (a, b)
    return (lane == z * 128 + y * 32 + parity * 16 + x * 4 + i).astype(jnp.bfloat16)


def dot(a, b):
    return lax.dot_general(a, b, (((1,), (0,)), ((), ())), preferred_element_type=jnp.float32)


def dot_nt(a, b):
    return lax.dot_general(a, b, (((1,), (1,)), ((), ())), preferred_element_type=jnp.float32)


def grads_kernel(
    x_ref, b_ref, s_ref, out_ref,
    x_o, b_o, s_o, xt, ht, nt, send1, recv1, acc1, send2, recv2, acc2, pk, pk16, recv3,
    p_send, p_recv, s1, r1, s2, r2, s3, r3,
):
    f32, bf16 = jnp.float32, jnp.bfloat16
    z, y, c, x = coords()
    partner = device_at(z, y, 1 - c, x)
    xs = [device_at(z, y, c, (x + k) % NX) for k in range(NX)]
    ys = [device_at(z, (y + k) % NY, c, x) for k in range(NY)]
    zs = [device_at((z + k) % NZ, y, c, x) for k in range(NZ)]
    barrier = pltpu.get_barrier_semaphore()
    for dev in [partner] + xs[1:] + ys[1:] + zs[1:]:
        pl.semaphore_signal(barrier, inc=1, device_id=dev, device_id_type=MESH)
    pl.semaphore_wait(barrier, 1 + NX - 1 + NY - 1 + NZ - 1)

    swaps = []
    for n, (src, dst) in enumerate([(x_ref, x_o), (s_ref, s_o), (b_ref, b_o)]):
        copy = pltpu.make_async_remote_copy(
            src_ref=src, dst_ref=dst, send_sem=p_send.at[n], recv_sem=p_recv.at[n], device_id=partner, device_id_type=MESH)
        copy.start()
        swaps.append(copy)
    picks = [row_pick("x", c, 1024), row_pick("y", c, 1024)]
    rows = x_ref.shape[0]
    for part in range(2):
        xt[part, :, 0:rows] = dot_nt(picks[part], x_ref[...]).astype(bf16)
        ht[part, :, 0:32] = dot_nt(picks[part], s_ref[0]).astype(bf16)
        nt[part, :, 0:32] = dot_nt(picks[part], s_ref[1]).astype(bf16)
    swaps[0].wait_recv()
    swaps[1].wait_recv()
    for part in range(2):
        xt[part, :, 512:512 + rows] = dot_nt(picks[part], x_o[...]).astype(bf16)
        ht[part, :, 32:64] = dot_nt(picks[part], s_o[0]).astype(bf16)
        nt[part, :, 32:64] = dot_nt(picks[part], s_o[1]).astype(bf16)
    swaps[2].wait_recv()

    def block(part, k):
        at = lax.rem((x if part == 0 else y) + k, 4)
        rws = pl.ds(pl.multiple_of(at * 128, 128), 128)
        cols = slice(512 * part, 512 * part + 512)
        q = dot(xt[part, rws, 0:rows], b_ref[:, cols]) + dot(xt[part, rws, 512:512 + rows], b_o[:, cols])
        back = jnp.concatenate([s_ref[2][:, cols], s_o[2][:, cols]], axis=0)
        return q, dot(ht[part, rws, :], back), dot(nt[part, rws, :], back)

    first = {}
    for k in (2, 1, 3, 0):
        for part in range(2):
            vals = block(part, k)
            for n, v in enumerate(vals):
                if k == 0:
                    acc1[part, :, 512 * n:512 * n + 512] = v
                else:
                    send1[part, k - 1, :, 512 * n:512 * n + 512] = v.astype(bf16)
            if k:
                copy = pltpu.make_async_remote_copy(
                    src_ref=send1.at[part, k - 1], dst_ref=recv1.at[part, k - 1], send_sem=s1.at[part, k - 1],
                    recv_sem=r1.at[part, k - 1], device_id=(xs, ys)[part][k], device_id_type=MESH)
                copy.start()
                first[part, k] = copy
    second = {}
    for part in range(2):
        for k in (1, 3, 2):
            first[part, k].wait_recv()
        total = acc1[part]
        for k in range(3):
            total = total + recv1[part, k].astype(f32)
        acc1[part] = total
        for k in (2, 1, 3):
            at = lax.rem((y if part == 0 else x) + k, 4)
            send2[part, k - 1] = acc1[part, pl.ds(pl.multiple_of(at * 32, 32), 32), :].astype(bf16)
            copy = pltpu.make_async_remote_copy(
                src_ref=send2.at[part, k - 1], dst_ref=recv2.at[part, k - 1], send_sem=s2.at[part, k - 1],
                recv_sem=r2.at[part, k - 1], device_id=(ys, xs)[part][k], device_id_type=MESH)
            copy.start()
            second[part, k] = copy
    for part in range(2):
        for k in (1, 3, 2):
            second[part, k].wait_recv()
        own = y if part == 0 else x
        total = acc1[part, pl.ds(pl.multiple_of(own * 32, 32), 32), :]
        for k in range(3):
            total = total + recv2[part, k].astype(f32)
        acc2[...] = total
        for zz in range(NZ):
            for h in range(2):
                q = 2 * part + h
                pk[zz, 4 * q:4 * q + 4, :] = acc2[4 * zz:4 * zz + 4, 768 * h:768 * h + 768]
    pk16[...] = pk[...].astype(bf16)
    third = []
    for k in range(1, NZ):
        copy = pltpu.make_async_remote_copy(
            src_ref=pk16.at[lax.rem(z + k, NZ)], dst_ref=recv3.at[k - 1], send_sem=s3.at[k - 1], recv_sem=r3.at[k - 1],
            device_id=zs[k], device_id_type=MESH)
        copy.start()
        third.append(copy)
    total = pk[z]
    for k in range(NZ - 1):
        third[k].wait_recv()
        total = total + recv3[k].astype(f32)
    pk[0] = total
    for part in range(2):
        for n in range(3):
            for piece in range(2):
                col = 512 * n + 256 * piece
                q = 2 * part + col // 768
                out_ref[:, 1024 * n + 512 * part + 256 * piece:1024 * n + 512 * part + 256 * piece + 256] = (
                    pk[0, 4 * q:4 * q + 4, col % 768:col % 768 + 256])
    for copy in swaps + list(first.values()) + list(second.values()) + third:
        copy.wait_send()


def grads_call(fetched, back_fetch, hop1, nbr1, back1):
    bf16, f32 = jnp.bfloat16, jnp.float32
    rows, width = fetched.shape
    small = jnp.pad(jnp.stack([hop1, nbr1, back1]), ((0, 0), (0, 32 - hop1.shape[0]), (0, 0)))
    dma = pltpu.SemaphoreType.DMA
    return pl.pallas_call(
        grads_kernel,
        out_shape=jax.ShapeDtypeStruct((4, 3 * width), f32),
        in_specs=[pl.BlockSpec(memory_space=pltpu.VMEM)] * 3,
        out_specs=pl.BlockSpec(memory_space=pltpu.VMEM),
        scratch_shapes=[
            pltpu.VMEM((rows, width), bf16), pltpu.VMEM((rows, width), bf16), pltpu.VMEM((3, 32, width), bf16),
            pltpu.VMEM((2, 512, 1024), bf16), pltpu.VMEM((2, 512, 64), bf16), pltpu.VMEM((2, 512, 64), bf16),
            pltpu.VMEM((2, 3, 128, 1536), bf16), pltpu.VMEM((2, 3, 128, 1536), bf16), pltpu.VMEM((2, 128, 1536), f32),
            pltpu.VMEM((2, 3, 32, 1536), bf16), pltpu.VMEM((2, 3, 32, 1536), bf16), pltpu.VMEM((32, 1536), f32),
            pltpu.VMEM((8, 16, 768), f32), pltpu.VMEM((8, 16, 768), bf16), pltpu.VMEM((7, 16, 768), bf16),
            dma((3,)), dma((3,)), dma((2, 3)), dma((2, 3)), dma((2, 3)), dma((2, 3)), dma((7,)), dma((7,)),
        ],
        compiler_params=pltpu.CompilerParams(collective_id=3, has_side_effects=True, vmem_limit_bytes=50 * 1024 * 1024),
        name="grads_scatter",
    )(fetched, back_fetch, small)


from jax.sharding import PartitionSpec as P

EPS = 1e-05


def act(values):
    return values * jax.nn.sigmoid(values)


def act_slope(values):
    sig = jax.nn.sigmoid(values)
    return sig * (1.0 + values * (1.0 - sig))


def contract_rows(left, right):
    return lax.dot_general(
        left, right, (((0,), (0,)), ((), ())), preferred_element_type=jnp.float32
    )


def contract_cols(left, right):
    return lax.dot_general(
        left, right, (((1,), (1,)), ((), ())), preferred_element_type=jnp.float32
    )


def on_device(
    table,
    hop2_owner,
    hop2_row,
    hop2_weight,
    hop1_feats,
    hop1_weight,
    target_feats,
    cotangent,
    layer_one,
    layer_two,
):
    f32 = jnp.float32
    bf16 = jnp.bfloat16
    width = table.shape[1]
    owners = lax.axis_size("feat")
    sections = lax.axis_size("sect")
    section = lax.axis_index("sect")
    count2 = hop2_row.shape[0]
    count1 = hop1_feats.shape[0]
    fanout = count2 // count1
    targets_dev = target_feats.shape[0]
    per_target = count1 // targets_dev
    capacity = 2 * count2 // owners
    owner = hop2_owner[:, 0]
    onehot = (owner[:, None] == jnp.arange(owners, dtype=jnp.int32)[None, :]).astype(jnp.int32)
    ranks = jnp.cumsum(onehot, axis=0)
    slot = jnp.sum(onehot * ranks, axis=1) - 1
    placed = owner * capacity + slot
    requests = (
        jnp.zeros((owners * capacity,), jnp.int32)
        .at[placed]
        .set(hop2_row)
        .reshape(owners, capacity)
    )
    found = jnp.take(
        table, lax.all_to_all(requests, "feat", split_axis=0, concat_axis=0, tiled=True), axis=0
    )
    replies = lax.all_to_all(found, "feat", split_axis=0, concat_axis=0, tiled=True)
    fetched = jnp.take(replies.reshape(owners * capacity, width), placed, axis=0)
    piece = lax.all_gather(layer_one, "feat", axis=0, tiled=True)
    cols_fetch = fetched
    cols_self = hop1_feats
    acc_fetch = jnp.dot(cols_fetch, piece[:, :width], preferred_element_type=f32)
    acc_self = jnp.dot(cols_self, piece[:, width : 2 * width], preferred_element_type=f32)
    nbr_weight = piece[:, 2 * width :]
    imp2 = hop2_weight.astype(f32).reshape(count1, fanout)
    total2 = jnp.sum(imp2, axis=1)
    trans2 = act(acc_fetch).reshape(count1, fanout, width)
    nbr1 = (jnp.sum(imp2[:, :, None] * trans2, axis=1) / total2[:, None]).astype(bf16)
    pre1 = acc_self + jnp.dot(nbr1, nbr_weight, preferred_element_type=f32)
    gated1 = act(pre1)
    scale1 = lax.rsqrt(jnp.mean(gated1 * gated1, axis=-1) + EPS)
    norm1 = gated1 * scale1[:, None]
    h_one = norm1.astype(bf16)
    q_two = layer_two[:, :width]
    v_self = layer_two[:, width : 2 * width]
    v_nbr = layer_two[:, 2 * width :]
    pre_hop1 = jnp.dot(h_one, q_two, preferred_element_type=f32)
    imp1 = hop1_weight.astype(f32).reshape(targets_dev, per_target)
    trans1 = act(pre_hop1).reshape(targets_dev, per_target, width)
    numer = jnp.sum(imp1[:, :, None] * trans1, axis=1)
    partial_total = jnp.sum(imp1, axis=1)
    share = targets_dev // sections
    numer_all, total_all = lax.psum((numer, partial_total), "sect")
    nbr2 = (numer_all / total_all[:, None]).astype(bf16)
    pre2 = jnp.dot(target_feats, v_self, preferred_element_type=f32) + jnp.dot(
        nbr2, v_nbr, preferred_element_type=f32
    )
    gated2 = act(pre2)
    scale2 = lax.rsqrt(jnp.mean(gated2 * gated2, axis=-1) + EPS)
    norm2 = gated2 * scale2[:, None]
    cot = cotangent.astype(f32)
    dg2 = scale2[:, None] * (cot - norm2 * jnp.mean(cot * norm2, axis=-1, keepdims=True))
    back2 = (dg2 * act_slope(pre2)).astype(bf16)
    emb_all = norm2.astype(bf16)
    back_nbr2 = contract_cols(back2, v_nbr)
    embedding = lax.dynamic_slice_in_dim(emb_all, section * share, share, 0)
    coef1 = imp1 / total_all[:, None]
    slope1 = act_slope(pre_hop1.reshape(targets_dev, per_target, width))
    back_hop1 = (
        (back_nbr2[:, None, :] * coef1[:, :, None] * slope1).reshape(count1, width).astype(bf16)
    )
    back_h1 = contract_cols(back_hop1, q_two)
    dg1 = scale1[:, None] * (back_h1 - norm1 * jnp.mean(back_h1 * norm1, axis=-1, keepdims=True))
    back1 = (dg1 * act_slope(pre1)).astype(bf16)
    back_nbr1 = contract_cols(back1, nbr_weight)
    coef2 = imp2 / total2[:, None]
    slope2 = act_slope(acc_fetch.reshape(count1, fanout, width))
    back_fetch = (
        (back_nbr1[:, None, :] * coef2[:, :, None] * slope2).reshape(count2, width).astype(bf16)
    )
    grads = grads_call(fetched, back_fetch, hop1_feats, nbr1, back1)
    return (embedding, grads)


def solution(mesh):
    return jax.shard_map(
        on_device,
        mesh=mesh,
        in_specs=(
            P("feat", None),
            P(("feat", "sect"), None),
            P(("feat", "sect")),
            P(("feat", "sect")),
            P(("feat", "sect"), None),
            P(("feat", "sect")),
            P("feat", None),
            P("feat", None),
            P("feat", None),
            P(),
        ),
        out_specs=(P(("feat", "sect"), None), P(("feat", "sect"), None)),
        check_vma=False,
    )
```

```python
import functools
import jax
import jax.numpy as jnp
from jax import lax
from jax.experimental import pallas as pl
from jax.experimental.pallas import tpu as pltpu

MESH = pl.DeviceIdType.MESH
NZ, NY, NC, NX = 8, 4, 2, 4


def coords():
    feat = lax.axis_index("feat")
    sect = lax.axis_index("sect")
    return feat // (NY * NC), (feat // NC) % NY, feat % NC, sect


def device_at(z, y, c, x):
    return ((z * NY + y) * NC + c, x)


def row_pick(first, parity, width):
    half = width // 2
    m = lax.broadcasted_iota(jnp.int32, (half, width), 0)
    lane = lax.broadcasted_iota(jnp.int32, (half, width), 1)
    a, b, z, i = m // 128, (m // 32) % 4, (m // 4) % 8, m % 4
    y, x = (b, a) if first == "x" else (a, b)
    return (lane == z * 128 + y * 32 + parity * 16 + x * 4 + i).astype(jnp.bfloat16)


def dot(a, b):
    return lax.dot_general(a, b, (((1,), (0,)), ((), ())), preferred_element_type=jnp.float32)


def dot_nt(a, b):
    return lax.dot_general(a, b, (((1,), (1,)), ((), ())), preferred_element_type=jnp.float32)


def grads_kernel(
    x_ref, b_ref, s_ref, out_ref,
    x_o, b_o, s_o, xt, ht, nt, send1, recv1, acc1, send2, recv2, acc2, pk, pk16, recv3,
    p_send, p_recv, s1, r1, s2, r2, s3, r3,
):
    f32, bf16 = jnp.float32, jnp.bfloat16
    z, y, c, x = coords()
    partner = device_at(z, y, 1 - c, x)
    xs = [device_at(z, y, c, (x + k) % NX) for k in range(NX)]
    ys = [device_at(z, (y + k) % NY, c, x) for k in range(NY)]
    zs = [device_at((z + k) % NZ, y, c, x) for k in range(NZ)]
    barrier = pltpu.get_barrier_semaphore()
    for dev in [partner] + xs[1:] + ys[1:] + zs[1:]:
        pl.semaphore_signal(barrier, inc=1, device_id=dev, device_id_type=MESH)
    pl.semaphore_wait(barrier, 1 + NX - 1 + NY - 1 + NZ - 1)

    swaps = []
    for n, (src, dst) in enumerate([(x_ref, x_o), (s_ref, s_o), (b_ref, b_o)]):
        copy = pltpu.make_async_remote_copy(
            src_ref=src, dst_ref=dst, send_sem=p_send.at[n], recv_sem=p_recv.at[n], device_id=partner, device_id_type=MESH)
        copy.start()
        swaps.append(copy)
    picks = [row_pick("x", c, 1024), row_pick("y", c, 1024)]
    rows = x_ref.shape[0]
    for part in range(2):
        xt[part, :, 0:rows] = dot_nt(picks[part], x_ref[...]).astype(bf16)
        ht[part, :, 0:32] = dot_nt(picks[part], s_ref[0]).astype(bf16)
        nt[part, :, 0:32] = dot_nt(picks[part], s_ref[1]).astype(bf16)
    swaps[0].wait_recv()
    swaps[1].wait_recv()
    for part in range(2):
        xt[part, :, 512:512 + rows] = dot_nt(picks[part], x_o[...]).astype(bf16)
        ht[part, :, 32:64] = dot_nt(picks[part], s_o[0]).astype(bf16)
        nt[part, :, 32:64] = dot_nt(picks[part], s_o[1]).astype(bf16)
    swaps[2].wait_recv()

    def block(part, k):
        at = lax.rem((x if part == 0 else y) + k, 4)
        rws = pl.ds(pl.multiple_of(at * 128, 128), 128)
        cols = slice(512 * part, 512 * part + 512)
        q = dot(xt[part, rws, 0:rows], b_ref[:, cols]) + dot(xt[part, rws, 512:512 + rows], b_o[:, cols])
        back = jnp.concatenate([s_ref[2][:, cols], s_o[2][:, cols]], axis=0)
        return q, dot(ht[part, rws, :], back), dot(nt[part, rws, :], back)

    first = {}
    for k in (2, 1, 3, 0):
        for part in range(2):
            vals = block(part, k)
            for n, v in enumerate(vals):
                if k == 0:
                    acc1[part, :, 512 * n:512 * n + 512] = v
                else:
                    send1[part, k - 1, :, 512 * n:512 * n + 512] = v.astype(bf16)
            if k:
                copy = pltpu.make_async_remote_copy(
                    src_ref=send1.at[part, k - 1], dst_ref=recv1.at[part, k - 1], send_sem=s1.at[part, k - 1],
                    recv_sem=r1.at[part, k - 1], device_id=(xs, ys)[part][k], device_id_type=MESH)
                copy.start()
                first[part, k] = copy
    second = {}
    for part in range(2):
        for k in (1, 3, 2):
            first[part, k].wait_recv()
        total = acc1[part]
        for k in range(3):
            total = total + recv1[part, k].astype(f32)
        acc1[part] = total
        for k in (2, 1, 3):
            at = lax.rem((y if part == 0 else x) + k, 4)
            send2[part, k - 1] = acc1[part, pl.ds(pl.multiple_of(at * 32, 32), 32), :].astype(bf16)
            copy = pltpu.make_async_remote_copy(
                src_ref=send2.at[part, k - 1], dst_ref=recv2.at[part, k - 1], send_sem=s2.at[part, k - 1],
                recv_sem=r2.at[part, k - 1], device_id=(ys, xs)[part][k], device_id_type=MESH)
            copy.start()
            second[part, k] = copy
    for part in range(2):
        for k in (1, 3, 2):
            second[part, k].wait_recv()
        own = y if part == 0 else x
        total = acc1[part, pl.ds(pl.multiple_of(own * 32, 32), 32), :]
        for k in range(3):
            total = total + recv2[part, k].astype(f32)
        acc2[...] = total
        for zz in range(NZ):
            for h in range(2):
                q = 2 * part + h
                pk[zz, 4 * q:4 * q + 4, :] = acc2[4 * zz:4 * zz + 4, 768 * h:768 * h + 768]
    pk16[...] = pk[...].astype(bf16)
    third = []
    for k in range(1, NZ):
        copy = pltpu.make_async_remote_copy(
            src_ref=pk16.at[lax.rem(z + k, NZ)], dst_ref=recv3.at[k - 1], send_sem=s3.at[k - 1], recv_sem=r3.at[k - 1],
            device_id=zs[k], device_id_type=MESH)
        copy.start()
        third.append(copy)
    total = pk[z]
    for k in range(NZ - 1):
        third[k].wait_recv()
        total = total + recv3[k].astype(f32)
    pk[0] = total
    for part in range(2):
        for n in range(3):
            for piece in range(2):
                col = 512 * n + 256 * piece
                q = 2 * part + col // 768
                out_ref[:, 1024 * n + 512 * part + 256 * piece:1024 * n + 512 * part + 256 * piece + 256] = (
                    pk[0, 4 * q:4 * q + 4, col % 768:col % 768 + 256])
    for copy in swaps + list(first.values()) + list(second.values()) + third:
        copy.wait_send()


def grads_call(fetched, back_fetch, hop1, nbr1, back1):
    bf16, f32 = jnp.bfloat16, jnp.float32
    rows, width = fetched.shape
    small = jnp.pad(jnp.stack([hop1, nbr1, back1]), ((0, 0), (0, 32 - hop1.shape[0]), (0, 0)))
    dma = pltpu.SemaphoreType.DMA
    return pl.pallas_call(
        grads_kernel,
        out_shape=jax.ShapeDtypeStruct((4, 3 * width), f32),
        in_specs=[pl.BlockSpec(memory_space=pltpu.VMEM)] * 3,
        out_specs=pl.BlockSpec(memory_space=pltpu.VMEM),
        scratch_shapes=[
            pltpu.VMEM((rows, width), bf16), pltpu.VMEM((rows, width), bf16), pltpu.VMEM((3, 32, width), bf16),
            pltpu.VMEM((2, 512, 1024), bf16), pltpu.VMEM((2, 512, 64), bf16), pltpu.VMEM((2, 512, 64), bf16),
            pltpu.VMEM((2, 3, 128, 1536), bf16), pltpu.VMEM((2, 3, 128, 1536), bf16), pltpu.VMEM((2, 128, 1536), f32),
            pltpu.VMEM((2, 3, 32, 1536), bf16), pltpu.VMEM((2, 3, 32, 1536), bf16), pltpu.VMEM((32, 1536), f32),
            pltpu.VMEM((8, 16, 768), f32), pltpu.VMEM((8, 16, 768), bf16), pltpu.VMEM((7, 16, 768), bf16),
            dma((3,)), dma((3,)), dma((2, 3)), dma((2, 3)), dma((2, 3)), dma((2, 3)), dma((7,)), dma((7,)),
        ],
        compiler_params=pltpu.CompilerParams(collective_id=3, has_side_effects=True, vmem_limit_bytes=50 * 1024 * 1024),
        name="grads_scatter",
    )(fetched, back_fetch, small)


from jax.sharding import PartitionSpec as P

CAP, SLOTS = 12, 16
N_FEAT = NZ * NY * NC


def dot_tn(a, b):
    return lax.dot_general(a, b, (((0,), (0,)), ((), ())), preferred_element_type=jnp.float32)


def iota(shape, dim):
    return lax.broadcasted_iota(jnp.int32, shape, dim)


def fetch_kernel(
    owner_ref, row_ref, table_ref, l1_ref, fetched_ref, weights_ref,
    w, reqs, rin, rep_out, rep_in,
    q_send, q_recv, a_send, a_recv, z_send, z_recv, y_send, y_recv, x_send, x_recv, c_send, c_recv, out_sem,
):
    f32, bf16 = jnp.float32, jnp.bfloat16
    z, y, c, x = coords()
    me = lax.axis_index("feat")
    partner = device_at(z, y, 1 - c, x)
    xs = [device_at(z, y, c, (x + k) % NX) for k in range(NX)]
    ys = [device_at(z, (y + k) % NY, c, x) for k in range(NY)]
    zs = [device_at((z + k) % NZ, y, c, x) for k in range(NZ)]
    barrier = pltpu.get_barrier_semaphore()

    def greet(k, carry):
        pl.semaphore_signal(barrier, inc=1, device_id=((me + k) % N_FEAT, x), device_id_type=MESH)
        return carry

    lax.fori_loop(1, N_FEAT, greet, 0)
    for dev in xs[1:]:
        pl.semaphore_signal(barrier, inc=1, device_id=dev, device_id_type=MESH)
    pl.semaphore_wait(barrier, N_FEAT - 1 + NX - 1)

    def cols(sec, at):
        return pl.ds(pl.multiple_of(sec * 1024 + at * 256, 256), 256)

    def remote(src, dst, send, recv, dev):
        copy = pltpu.make_async_remote_copy(
            src_ref=src, dst_ref=dst, send_sem=send, recv_sem=recv, device_id=dev, device_id_type=MESH)
        copy.start()
        return copy

    def wait_bytes(ref, sem):
        pltpu.make_async_copy(ref, ref, sem).wait()

    for sec in range(3):
        for k in (4, 3, 5, 2, 6, 1, 7):
            remote(l1_ref.at[:, cols(sec, x)], w.at[z, y, c, :, cols(sec, x)], z_send.at[sec], z_recv.at[sec], zs[k])
    for sec in range(3):
        w[z, y, c, :, cols(sec, x)] = l1_ref[:, cols(sec, x)]

    count = owner_ref.shape[0]
    rel = (owner_ref[...] - me + N_FEAT) % N_FEAT
    member = (iota((count, N_FEAT), 1) == rel).astype(bf16)
    before = (iota((count, count), 0) > iota((count, count), 1)).astype(bf16)
    rank = dot(before, member)
    slot = jnp.sum(rank * member.astype(f32), axis=1, keepdims=True).astype(jnp.int32)
    row = row_ref[...]
    lane = iota((count, 128), 1)
    asked = jnp.where(lane == slot, row // 32, 0) + jnp.where(lane == slot + SLOTS, row % 32, 0)
    reqs[...] = dot_tn(member, asked.astype(f32).astype(bf16)).reshape(N_FEAT, 1, 128)

    def ask(k, carry):
        remote(reqs.at[k], rin.at[k], q_send, q_recv, ((me + k) % N_FEAT, x))
        return carry

    lax.fori_loop(1, N_FEAT, ask, 0)
    rin[0] = reqs[0]
    for sec in range(3):
        wait_bytes(w.at[pl.ds(0, NZ - 1), y, c, :, cols(sec, x)], z_recv.at[sec])
        for k in (2, 1, 3):
            part = w.at[:, y, c, :, cols(sec, x)]
            remote(part, part, y_send.at[sec], y_recv.at[sec], ys[k])

    wait_bytes(rin.at[pl.ds(1, N_FEAT - 1)], q_recv)
    wanted = rin[...].reshape(N_FEAT, 128).astype(bf16)
    wide = 8 * SLOTS
    at_row, at_lane = iota((wide, 128), 0) % SLOTS, iota((wide, 128), 1)

    def pick_weights(slots):
        return (32 * (at_lane == slots).astype(jnp.int32) + (at_lane == slots + SLOTS).astype(jnp.int32)).astype(f32)

    main_at = pick_weights(at_row)
    rest_at = [pick_weights(4 * j + at_row - CAP) for j in range(3)]
    is_main = iota((wide, 1), 0) % SLOTS < CAP
    rows = table_ref.shape[0]

    def chunk(g):
        group = (iota((wide, N_FEAT), 1) == g * 8 + iota((wide, N_FEAT), 0) // SLOTS).astype(bf16)
        spread = dot(group, wanted)
        ids = iota((wide, rows), 1).astype(f32)

        def chosen(weights, keep):
            target = jnp.where(keep, jnp.sum(spread * weights, axis=1, keepdims=True), -1.0)
            return (ids == target).astype(bf16)

        main = dot(chosen(main_at, is_main), table_ref[:, 0:768])
        for j in range(3):
            rest = dot(chosen(rest_at[j], jnp.logical_not(is_main)), table_ref[:, 768:1024])
            both = main[:, 256 * j:256 * j + 256] + rest
            rep_out[pl.ds(g * 8, 8), :, 256 * j:256 * j + 256] = both.astype(bf16).reshape(8, SLOTS, 256)

    def reply(k):
        remote(rep_out.at[k], rep_in.at[k], a_send, a_recv, ((me - k + N_FEAT) % N_FEAT, x))

    def serve(g, carry):
        chunk(g)
        for n in range(8):
            reply(g * 8 + n)
        return carry

    chunk(0)
    for n in range(1, 8):
        reply(n)
    lax.fori_loop(1, 8, serve, 0)
    rep_in[0] = rep_out[0]

    across = {}
    for sec in range(3):
        wait_bytes(w.at[:, pl.ds(0, NY - 1), c, :, cols(sec, x)], y_recv.at[sec])
        part = w.at[:, :, c, :, cols(sec, x)]
        for k in (2, 1, 3):
            across[sec, k] = remote(part, part, x_send.at[sec, k - 1], x_recv.at[sec, k - 1], xs[k])
        remote(part, part, c_send.at[sec], c_recv.at[sec], partner)
    for sec in range(3):
        for k in (1, 3, 2):
            across[sec, k].wait_recv()
            part = w.at[:, :, c, :, cols(sec, lax.rem(x - k + NX, NX))]
            remote(part, part, c_send.at[sec], c_recv.at[sec], partner)
    for sec in range(3):
        wait_bytes(w.at[:, :, c, :, pl.ds(sec * 1024, 1024)], c_recv.at[sec])
    out = pltpu.make_async_copy(w, weights_ref, out_sem)
    out.start()

    wait_bytes(rep_in.at[pl.ds(1, N_FEAT - 1)], a_recv)
    total = N_FEAT * SLOTS
    places = iota((count, total), 1)
    base = rel * SLOTS
    answers = rep_in[...].reshape(total, 768)
    fetched_ref[:, 0:768] = dot((places == base + slot).astype(bf16), answers).astype(bf16)
    rest = jnp.zeros((count, 256), f32)
    for j in range(3):
        place = jnp.where(slot // 4 == j, base + CAP + slot % 4, -1)
        rest = rest + dot((places == place).astype(bf16), answers[:, 256 * j:256 * j + 256])
    fetched_ref[:, 768:1024] = rest.astype(bf16)

    out.wait()
    wait_bytes(reqs.at[pl.ds(1, N_FEAT - 1)], q_send)
    wait_bytes(rep_out.at[pl.ds(1, N_FEAT - 1)], a_send)
    for sec in range(3):
        wait_bytes(w.at[pl.ds(0, NZ - 1), y, c, :, cols(sec, x)], z_send.at[sec])
        wait_bytes(w.at[:, pl.ds(0, NY - 1), c, :, cols(sec, x)], y_send.at[sec])
        for k in (1, 2, 3):
            across[sec, k].wait_send()
        wait_bytes(w.at[:, :, c, :, pl.ds(sec * 1024, 1024)], c_send.at[sec])


def fetch_call(owner, row, table, layer_one):
    bf16, f32 = jnp.bfloat16, jnp.float32
    count, width = row.shape[0], table.shape[1]
    dma = pltpu.SemaphoreType.DMA
    fetched, weights = pl.pallas_call(
        fetch_kernel,
        out_shape=(
            jax.ShapeDtypeStruct((count, width), bf16),
            jax.ShapeDtypeStruct((NZ, NY, NC, 16, 3 * width), bf16),
        ),
        in_specs=[pl.BlockSpec(memory_space=pltpu.VMEM)] * 4,
        out_specs=(pl.BlockSpec(memory_space=pltpu.VMEM), pl.BlockSpec(memory_space=pl.ANY)),
        scratch_shapes=[
            pltpu.VMEM((NZ, NY, NC, 16, 3 * width), bf16),
            pltpu.VMEM((N_FEAT, 1, 128), f32), pltpu.VMEM((N_FEAT, 1, 128), f32),
            pltpu.VMEM((N_FEAT, SLOTS, 768), bf16), pltpu.VMEM((N_FEAT, SLOTS, 768), bf16),
            dma, dma, dma, dma, dma((3,)), dma((3,)), dma((3,)), dma((3,)), dma((3, 3)), dma((3, 3)), dma((3,)), dma((3,)), dma,
        ],
        compiler_params=pltpu.CompilerParams(collective_id=1, has_side_effects=True, vmem_limit_bytes=50 * 1024 * 1024),
        name="fetch_rows",
    )(owner, row.reshape(count, 1), table, layer_one)
    return fetched, weights.reshape(N_FEAT * 16, 3 * width)


EPS = 1e-05


def act(values):
    return values * jax.nn.sigmoid(values)


def act_slope(values):
    sig = jax.nn.sigmoid(values)
    return sig * (1.0 + values * (1.0 - sig))


def contract_rows(left, right):
    return lax.dot_general(
        left, right, (((0,), (0,)), ((), ())), preferred_element_type=jnp.float32
    )


def contract_cols(left, right):
    return lax.dot_general(
        left, right, (((1,), (1,)), ((), ())), preferred_element_type=jnp.float32
    )


def on_device(
    table,
    hop2_owner,
    hop2_row,
    hop2_weight,
    hop1_feats,
    hop1_weight,
    target_feats,
    cotangent,
    layer_one,
    layer_two,
):
    f32 = jnp.float32
    bf16 = jnp.bfloat16
    width = table.shape[1]
    sections = lax.axis_size("sect")
    section = lax.axis_index("sect")
    count2 = hop2_row.shape[0]
    count1 = hop1_feats.shape[0]
    fanout = count2 // count1
    targets_dev = target_feats.shape[0]
    per_target = count1 // targets_dev
    fetched, piece = fetch_call(hop2_owner, hop2_row, table, layer_one)
    cols_fetch = fetched
    cols_self = hop1_feats
    acc_fetch = jnp.dot(cols_fetch, piece[:, :width], preferred_element_type=f32)
    acc_self = jnp.dot(cols_self, piece[:, width : 2 * width], preferred_element_type=f32)
    nbr_weight = piece[:, 2 * width :]
    imp2 = hop2_weight.astype(f32).reshape(count1, fanout)
    total2 = jnp.sum(imp2, axis=1)
    trans2 = act(acc_fetch).reshape(count1, fanout, width)
    nbr1 = (jnp.sum(imp2[:, :, None] * trans2, axis=1) / total2[:, None]).astype(bf16)
    pre1 = acc_self + jnp.dot(nbr1, nbr_weight, preferred_element_type=f32)
    gated1 = act(pre1)
    scale1 = lax.rsqrt(jnp.mean(gated1 * gated1, axis=-1) + EPS)
    norm1 = gated1 * scale1[:, None]
    h_one = norm1.astype(bf16)
    q_two = layer_two[:, :width]
    v_self = layer_two[:, width : 2 * width]
    v_nbr = layer_two[:, 2 * width :]
    pre_hop1 = jnp.dot(h_one, q_two, preferred_element_type=f32)
    imp1 = hop1_weight.astype(f32).reshape(targets_dev, per_target)
    trans1 = act(pre_hop1).reshape(targets_dev, per_target, width)
    numer = jnp.sum(imp1[:, :, None] * trans1, axis=1)
    partial_total = jnp.sum(imp1, axis=1)
    share = targets_dev // sections
    numer_all, total_all = lax.psum((numer, partial_total), "sect")
    nbr2 = (numer_all / total_all[:, None]).astype(bf16)
    pre2 = jnp.dot(target_feats, v_self, preferred_element_type=f32) + jnp.dot(
        nbr2, v_nbr, preferred_element_type=f32
    )
    gated2 = act(pre2)
    scale2 = lax.rsqrt(jnp.mean(gated2 * gated2, axis=-1) + EPS)
    norm2 = gated2 * scale2[:, None]
    cot = cotangent.astype(f32)
    dg2 = scale2[:, None] * (cot - norm2 * jnp.mean(cot * norm2, axis=-1, keepdims=True))
    back2 = (dg2 * act_slope(pre2)).astype(bf16)
    emb_all = norm2.astype(bf16)
    back_nbr2 = contract_cols(back2, v_nbr)
    embedding = lax.dynamic_slice_in_dim(emb_all, section * share, share, 0)
    coef1 = imp1 / total_all[:, None]
    slope1 = act_slope(pre_hop1.reshape(targets_dev, per_target, width))
    back_hop1 = (
        (back_nbr2[:, None, :] * coef1[:, :, None] * slope1).reshape(count1, width).astype(bf16)
    )
    back_h1 = contract_cols(back_hop1, q_two)
    dg1 = scale1[:, None] * (back_h1 - norm1 * jnp.mean(back_h1 * norm1, axis=-1, keepdims=True))
    back1 = (dg1 * act_slope(pre1)).astype(bf16)
    back_nbr1 = contract_cols(back1, nbr_weight)
    coef2 = imp2 / total2[:, None]
    slope2 = act_slope(acc_fetch.reshape(count1, fanout, width))
    back_fetch = (
        (back_nbr1[:, None, :] * coef2[:, :, None] * slope2).reshape(count2, width).astype(bf16)
    )
    grads = grads_call(fetched, back_fetch, hop1_feats, nbr1, back1)
    return (embedding, grads)


def solution(mesh):
    return jax.shard_map(
        on_device,
        mesh=mesh,
        in_specs=(
            P("feat", None),
            P(("feat", "sect"), None),
            P(("feat", "sect")),
            P(("feat", "sect")),
            P(("feat", "sect"), None),
            P(("feat", "sect")),
            P("feat", None),
            P("feat", None),
            P("feat", None),
            P(),
        ),
        out_specs=(P(("feat", "sect"), None), P(("feat", "sect"), None)),
        check_vma=False,
    )
```

```python
import types

import jax
import jax.numpy as jnp
from jax import lax
from jax.experimental import pallas as pl
from jax.experimental.pallas import tpu as pltpu
from jax.sharding import PartitionSpec as P

MESH = pl.DeviceIdType.MESH
EPS = 1e-05
NZ, NY, NC, NX = 8, 4, 2, 4
N_FEAT = NZ * NY * NC
CAP, SLOTS = 12, 16
D = 1024
ROWS2, ROWS1, FAN, PER = 400, 20, 20, 5
PAD1, PADT = 32, 16
F32, BF16 = jnp.float32, jnp.bfloat16


def act(values):
    return values * jax.nn.sigmoid(values)


def act_slope(values):
    sig = jax.nn.sigmoid(values)
    return sig * (1.0 + values * (1.0 - sig))


def dot(a, b):
    return lax.dot_general(a, b, (((1,), (0,)), ((), ())), preferred_element_type=F32)


def dot_nt(a, b):
    return lax.dot_general(a, b, (((1,), (1,)), ((), ())), preferred_element_type=F32)


def dot_tn(a, b):
    return lax.dot_general(a, b, (((0,), (0,)), ((), ())), preferred_element_type=F32)


def split(values):
    high = values.astype(BF16)
    return high, (values - high.astype(F32)).astype(BF16)


def iota(shape, dim):
    return lax.broadcasted_iota(jnp.int32, shape, dim)


def coords():
    feat = lax.axis_index("feat")
    return feat // (NY * NC), (feat // NC) % NY, feat % NC, lax.axis_index("sect")


def device_at(z, y, c, x):
    return ((z * NY + y) * NC + c, x)


def remote(src, dst, send, recv, dev):
    copy = pltpu.make_async_remote_copy(
        src_ref=src, dst_ref=dst, send_sem=send, recv_sem=recv, device_id=dev, device_id_type=MESH)
    copy.start()
    return copy


def wait_bytes(ref, sem):
    pltpu.make_async_copy(ref, ref, sem).wait()


def row_pick(first, parity):
    m, lane = iota((D // 2, D), 0), iota((D // 2, D), 1)
    a, b, z, i = m // 128, (m // 32) % 4, (m // 4) % 8, m % 4
    y, x = (b, a) if first == "x" else (a, b)
    return (lane == z * 128 + y * 32 + parity * 16 + x * 4 + i).astype(BF16)


SCRATCH = [
    ("w", (NZ, NY, NC, 16, 3 * D), BF16), ("l2", (D, 3 * D), BF16), ("table", (512, D), BF16),
    ("reqs", (N_FEAT, 1, 128), F32), ("rin", (N_FEAT, 1, 128), F32),
    ("rep_out", (N_FEAT, SLOTS, 768), BF16), ("rep_in", (N_FEAT, SLOTS, 768), BF16),
    ("hop", (PAD1, D), BF16), ("nbr1", (PAD1, D), BF16), ("back1", (PAD1, D), BF16),
    ("hop_o", (PAD1, D), BF16), ("nbr1_o", (PAD1, D), BF16), ("back1_o", (PAD1, D), BF16),
    ("tgt", (PADT, D), BF16), ("cot", (PADT, D), F32),
    ("fetched", (ROWS2, D), BF16), ("fetched_o", (ROWS2, D), BF16),
    ("bf", (ROWS2, D), BF16), ("bf_o", (ROWS2, D), BF16), ("pre", (ROWS2, D), F32),
    ("xt", (2, 512, 1024), BF16), ("ht", (2, 512, 64), BF16), ("nt", (2, 512, 64), BF16),
    ("msg", (8, D + 128), F32), ("msg_in", (NX - 1, 8, D + 128), F32),
    ("emb", (PADT, D), F32),
    ("send1", (3, 2, 3, 128, 512), BF16), ("recv1", (3, 2, 3, 128, 512), BF16), ("acc1", (3, 2, 128, 512), F32),
    ("send2", (3, 2, 3, 32, 512), BF16), ("recv2", (3, 2, 3, 32, 512), BF16),
    ("acc2", (2, 32, 512), F32), ("pk", (3, NZ, 16, 256), F32), ("send3", (3, NZ, 16, 256), BF16),
    ("recv3", (3, NZ - 1, 16, 256), BF16),
]
SEMS = [
    ("load", (3,)), ("own", (3,)), ("q_send", ()), ("q_recv", ()), ("a_send", ()), ("a_recv", ()),
    ("z_send", (3,)), ("z_recv", (3,)), ("y_send", (3,)), ("y_recv", (3,)),
    ("x_send", (3, 4)), ("x_recv", (3, 4)), ("c_send", (3,)), ("c_recv", (3,)),
    ("p_send", (5,)), ("p_recv", (5,)), ("m_send", (3,)), ("m_recv", (3,)),
    ("s1", (3, 2, 3)), ("r1", (3, 2, 3)), ("s2", (3, 2, 3)), ("r2", (3, 2, 3)), ("s3", (3, 7)), ("r3", (3, 7)),
]
INPUTS = ["tab", "table_in", "hop_in", "tgt_in", "cot_in", "l1", "l2_in"]
OUTPUTS = ["emb_out", "grads_out"]


def step_kernel(*refs):
    names = INPUTS + OUTPUTS + [s[0] for s in SCRATCH] + [s[0] for s in SEMS]
    r = types.SimpleNamespace(**dict(zip(names, refs)))
    z, y, c, x = coords()
    me = lax.axis_index("feat")
    partner = device_at(z, y, 1 - c, x)
    xs = [device_at(z, y, c, (x + k) % NX) for k in range(NX)]
    ys = [device_at(z, (y + k) % NY, c, x) for k in range(NY)]
    zs = [device_at((z + k) % NZ, y, c, x) for k in range(NZ)]
    w = r.w

    barrier = pltpu.get_barrier_semaphore()

    def greet(k, carry):
        pl.semaphore_signal(barrier, inc=1, device_id=((me + k) % N_FEAT, x), device_id_type=MESH)
        return carry

    lax.fori_loop(1, N_FEAT, greet, 0)
    for dev in xs[1:]:
        pl.semaphore_signal(barrier, inc=1, device_id=dev, device_id_type=MESH)

    def cols(sec, at):
        return pl.ds(pl.multiple_of(sec * D + at * 256, 256), 256)

    loads = [pltpu.make_async_copy(r.table_in, r.table, r.load.at[0]), pltpu.make_async_copy(r.l2_in, r.l2, r.load.at[1])]
    for copy in loads:
        copy.start()
    owns = [pltpu.make_async_copy(r.l1.at[:, cols(sec, x)], w.at[z, y, c, :, cols(sec, x)], r.own.at[sec]) for sec in range(3)]
    for copy in owns:
        copy.start()

    count = ROWS2
    rel = (r.tab[:, 0:1] - me + N_FEAT) % N_FEAT
    row = r.tab[:, 1:2]
    member = (iota((count, N_FEAT), 1) == rel).astype(BF16)
    before = (iota((count, count), 0) > iota((count, count), 1)).astype(BF16)
    slot = jnp.sum(dot(before, member) * member.astype(F32), axis=1, keepdims=True).astype(jnp.int32)
    lane = iota((count, 128), 1)
    asked = jnp.where(lane == slot, row // 32, 0) + jnp.where(lane == slot + SLOTS, row % 32, 0)
    r.reqs[...] = dot_tn(member, asked.astype(F32).astype(BF16)).reshape(N_FEAT, 1, 128)
    r.rin[0] = r.reqs[0]

    pl.semaphore_wait(barrier, N_FEAT - 1 + NX - 1)

    def ask(k, carry):
        remote(r.reqs.at[k], r.rin.at[k], r.q_send, r.q_recv, ((me + k) % N_FEAT, x))
        return carry

    lax.fori_loop(1, N_FEAT, ask, 0)
    for sec in range(3):
        for k in (4, 3, 5, 2, 6, 1, 7):
            remote(r.l1.at[:, cols(sec, x)], w.at[z, y, c, :, cols(sec, x)], r.z_send.at[sec], r.z_recv.at[sec], zs[k])

    r.hop[...] = jnp.zeros_like(r.hop)
    r.hop[0:ROWS1, :] = r.hop_in[...]
    r.tgt[...] = jnp.zeros_like(r.tgt)
    r.tgt[0:4, :] = r.tgt_in[...]
    r.cot[...] = jnp.zeros_like(r.cot)
    r.cot[0:4, :] = r.cot_in[...].astype(F32)
    swaps = [remote(r.hop, r.hop_o, r.p_send.at[0], r.p_recv.at[0], partner)]

    for sec in range(3):
        wait_bytes(w.at[pl.ds(0, NZ - 1), y, c, :, cols(sec, x)], r.z_recv.at[sec])
        owns[sec].wait()
        for k in (2, 1, 3):
            part = w.at[:, y, c, :, cols(sec, x)]
            remote(part, part, r.y_send.at[sec], r.y_recv.at[sec], ys[k])

    loads[0].wait()
    wait_bytes(r.rin.at[pl.ds(1, N_FEAT - 1)], r.q_recv)
    wanted = r.rin[...].reshape(N_FEAT, 128).astype(BF16)
    wide = 8 * SLOTS
    at_row, at_lane = iota((wide, 128), 0) % SLOTS, iota((wide, 128), 1)

    def pick_weights(slots):
        return (32 * (at_lane == slots).astype(jnp.int32) + (at_lane == slots + SLOTS).astype(jnp.int32)).astype(F32)

    main_at = pick_weights(at_row)
    rest_at = [pick_weights(4 * j + at_row - CAP) for j in range(3)]
    is_main = iota((wide, 1), 0) % SLOTS < CAP

    def chunk(g):
        group = (iota((wide, N_FEAT), 1) == g * 8 + iota((wide, N_FEAT), 0) // SLOTS).astype(BF16)
        spread = dot(group, wanted)
        ids = iota((wide, 512), 1).astype(F32)

        def chosen(weights, keep):
            target = jnp.where(keep, jnp.sum(spread * weights, axis=1, keepdims=True), -1.0)
            return (ids == target).astype(BF16)

        main = dot(chosen(main_at, is_main), r.table[:, 0:768])
        for j in range(3):
            rest = dot(chosen(rest_at[j], jnp.logical_not(is_main)), r.table[:, 768:1024])
            both = main[:, 256 * j:256 * j + 256] + rest
            r.rep_out[pl.ds(g * 8, 8), :, 256 * j:256 * j + 256] = both.astype(BF16).reshape(8, SLOTS, 256)

    def reply(k):
        remote(r.rep_out.at[k], r.rep_in.at[k], r.a_send, r.a_recv, ((me - k + N_FEAT) % N_FEAT, x))

    def serve(g, carry):
        chunk(g)
        for n in range(8):
            reply(g * 8 + n)
        return carry

    across = {}

    def along_x(sec):
        wait_bytes(w.at[:, pl.ds(0, NY - 1), c, :, cols(sec, x)], r.y_recv.at[sec])
        part = w.at[:, :, c, :, cols(sec, x)]
        for n, k in enumerate((1, 3)):
            across[sec, n] = remote(part, part, r.x_send.at[sec, n], r.x_recv.at[sec, n], xs[k])
        remote(part, part, r.c_send.at[sec], r.c_recv.at[sec], partner)

    chunk(0)
    for n in range(1, 8):
        reply(n)
    lax.fori_loop(1, 3, serve, 0)
    along_x(0)
    lax.fori_loop(3, 5, serve, 0)
    along_x(1)
    lax.fori_loop(5, 8, serve, 0)
    along_x(2)
    r.rep_in[0] = r.rep_out[0]

    for sec in range(3):
        for n, k in enumerate((1, 3)):
            across[sec, n].wait_recv()
            at = cols(sec, (x - k + NX) % NX)
            half = w.at[pl.ds(4 * n, 4), :, c, :, at]
            across[sec, 2 + n] = remote(half, half, r.x_send.at[sec, 2 + n], r.x_recv.at[sec, 2 + n], xs[k])
            part = w.at[:, :, c, :, at]
            remote(part, part, r.c_send.at[sec], r.c_recv.at[sec], partner)
        for n in range(2):
            across[sec, 2 + n].wait_recv()
            half = w.at[pl.ds(4 * n, 4), :, c, :, cols(sec, (x + 2) % NX)]
            remote(half, half, r.c_send.at[sec], r.c_recv.at[sec], partner)
    for sec in range(3):
        wait_bytes(w.at[:, :, c, :, pl.ds(sec * D, D)], r.c_recv.at[sec])
    loads[1].wait()

    def one(sec):
        return w[:, :, :, :, sec * D:sec * D + D].reshape(D, D)

    def two(sec):
        return r.l2[:, sec * D:sec * D + D]

    pre1_self = dot(r.hop[...], one(1))
    pre2_self = dot(r.tgt[...], two(1))
    swaps[0].wait_recv()
    for part, first in enumerate("xy"):
        pick = row_pick(first, c)
        r.ht[part, :, 0:32] = dot_nt(pick, r.hop[...]).astype(BF16)
        r.ht[part, :, 32:64] = dot_nt(pick, r.hop_o[...]).astype(BF16)

    wait_bytes(r.rep_in.at[pl.ds(1, N_FEAT - 1)], r.a_recv)
    total = N_FEAT * SLOTS
    places = iota((count, total), 1)
    base = rel * SLOTS
    answers = r.rep_in[...].reshape(total, 768)
    r.fetched[:, 0:768] = dot((places == base + slot).astype(BF16), answers).astype(BF16)
    rest = jnp.zeros((count, 256), F32)
    for j in range(3):
        place = jnp.where(slot // 4 == j, base + CAP + slot % 4, -1)
        rest = rest + dot((places == place).astype(BF16), answers[:, 256 * j:256 * j + 256])
    r.fetched[:, 768:1024] = rest.astype(BF16)
    swaps.append(remote(r.fetched, r.fetched_o, r.p_send.at[1], r.p_recv.at[1], partner))

    r.pre[...] = dot(r.fetched[...], one(0))
    of_node = jnp.where(iota((count, PAD1), 0) // FAN == iota((count, PAD1), 1), r.tab[:, 2:3], 0).astype(F32).astype(BF16)
    total2 = jnp.maximum(dot_tn(of_node, jnp.ones((count, 128), BF16))[:, 0:1], 1.0)
    high, low = split(act(r.pre[...]))
    r.nbr1[...] = ((dot_tn(of_node, high) + dot_tn(of_node, low)) / total2).astype(BF16)
    swaps.append(remote(r.nbr1, r.nbr1_o, r.p_send.at[2], r.p_recv.at[2], partner))
    pre1 = pre1_self + dot(r.nbr1[...], one(2))
    gated1 = act(pre1)
    scale1 = lax.rsqrt(jnp.mean(gated1 * gated1, axis=-1, keepdims=True) + EPS)
    norm1 = gated1 * scale1

    pre_hop1 = dot(norm1.astype(BF16), two(0))
    of_target = jnp.where(iota((PAD1, PADT), 0) // PER == iota((PAD1, PADT), 1), r.tab[0:PAD1, 3:4], 0).astype(F32).astype(BF16)
    high, low = split(act(pre_hop1))
    numer = dot_tn(of_target, high) + dot_tn(of_target, low)
    weight = dot_tn(of_target, jnp.ones((PAD1, 128), BF16))
    r.msg[:, 0:D] = numer[0:8]
    r.msg[:, D:D + 128] = weight[0:8]
    sums = [remote(r.msg, r.msg_in.at[k - 1], r.m_send.at[k - 1], r.m_recv.at[k - 1], xs[k]) for k in (1, 2, 3)]
    swaps[1].wait_recv()
    swaps[2].wait_recv()
    for part, first in enumerate("xy"):
        pick = row_pick(first, c)
        r.xt[part, :, 0:count] = dot_nt(pick, r.fetched[...]).astype(BF16)
        r.xt[part, :, 512:512 + count] = dot_nt(pick, r.fetched_o[...]).astype(BF16)
        r.nt[part, :, 0:32] = dot_nt(pick, r.nbr1[...]).astype(BF16)
        r.nt[part, :, 32:64] = dot_nt(pick, r.nbr1_o[...]).astype(BF16)
    for copy in sums:
        copy.wait_recv()
    summed = r.msg[...] + r.msg_in[0] + r.msg_in[1] + r.msg_in[2]
    summed = jnp.concatenate([summed, jnp.zeros((PADT - 8, D + 128), F32)], axis=0)
    total1 = jnp.maximum(summed[:, D:D + 1], 1.0)
    nbr2 = (summed[:, 0:D] / total1).astype(BF16)
    pre2 = pre2_self + dot(nbr2, two(2))
    gated2 = act(pre2)
    scale2 = lax.rsqrt(jnp.mean(gated2 * gated2, axis=-1, keepdims=True) + EPS)
    norm2 = gated2 * scale2
    r.emb[...] = norm2
    cot = r.cot[...]
    back2 = (scale2 * (cot - norm2 * jnp.mean(cot * norm2, axis=-1, keepdims=True)) * act_slope(pre2)).astype(BF16)
    back_nbr2 = dot_nt(back2, two(2))
    high, low = split(back_nbr2 / total1)
    back_hop1 = ((dot(of_target, high) + dot(of_target, low)) * act_slope(pre_hop1)).astype(BF16)
    back_h1 = dot_nt(back_hop1, two(0))
    back1 = (scale1 * (back_h1 - norm1 * jnp.mean(back_h1 * norm1, axis=-1, keepdims=True)) * act_slope(pre1)).astype(BF16)
    r.back1[...] = back1
    swaps.append(remote(r.back1, r.back1_o, r.p_send.at[3], r.p_recv.at[3], partner))
    r.emb_out[...] = r.emb[pl.ds(x, 1), :].astype(BF16)

    first, second, third = {}, {}, {}

    def start_first(sec, value):
        for k in (2, 1, 3, 0):
            for part in range(2):
                at = lax.rem((x if part == 0 else y) + k, 4)
                v = value(part, pl.ds(pl.multiple_of(at * 128, 128), 128), slice(512 * part, 512 * part + 512))
                if k == 0:
                    r.acc1[sec, part] = v
                else:
                    r.send1[sec, part, k - 1] = v.astype(BF16)
                    first[sec, part, k] = remote(
                        r.send1.at[sec, part, k - 1], r.recv1.at[sec, part, k - 1], r.s1.at[sec, part, k - 1],
                        r.r1.at[sec, part, k - 1], (xs, ys)[part][k])

    def start_second(sec):
        for part in range(2):
            for k in (1, 3, 2):
                first[sec, part, k].wait_recv()
            r.acc1[sec, part] = (
                r.acc1[sec, part] + r.recv1[sec, part, 0].astype(F32) + r.recv1[sec, part, 1].astype(F32)
                + r.recv1[sec, part, 2].astype(F32))
            for k in (2, 1, 3):
                at = lax.rem((y if part == 0 else x) + k, 4)
                r.send2[sec, part, k - 1] = r.acc1[sec, part, pl.ds(pl.multiple_of(at * 32, 32), 32), :].astype(BF16)
                second[sec, part, k] = remote(
                    r.send2.at[sec, part, k - 1], r.recv2.at[sec, part, k - 1], r.s2.at[sec, part, k - 1],
                    r.r2.at[sec, part, k - 1], (ys, xs)[part][k])

    def start_third(sec):
        for part in range(2):
            for k in (1, 3, 2):
                second[sec, part, k].wait_recv()
            at = y if part == 0 else x
            r.acc2[part] = (
                r.acc1[sec, part, pl.ds(pl.multiple_of(at * 32, 32), 32), :] + r.recv2[sec, part, 0].astype(F32)
                + r.recv2[sec, part, 1].astype(F32) + r.recv2[sec, part, 2].astype(F32))
            for zz in range(NZ):
                for h in range(2):
                    q = 2 * part + h
                    r.pk[sec, zz, 4 * q:4 * q + 4, :] = r.acc2[part, 4 * zz:4 * zz + 4, 256 * h:256 * h + 256]
        r.send3[sec] = r.pk[sec].astype(BF16)
        for k in (4, 3, 5, 2, 6, 1, 7):
            third[sec, k] = remote(
                r.send3.at[sec, lax.rem(z + k, NZ)], r.recv3.at[sec, k - 1], r.s3.at[sec, k - 1], r.r3.at[sec, k - 1], zs[k])

    def finish(sec):
        value = r.pk[sec, z]
        for k in (1, 7, 2, 6, 3, 5, 4):
            third[sec, k].wait_recv()
            value = value + r.recv3[sec, k - 1].astype(F32)
        r.pk[sec, 0] = value
        for q in range(4):
            r.grads_out[:, sec * D + 256 * q:sec * D + 256 * q + 256] = r.pk[sec, 0, 4 * q:4 * q + 4, :]

    back_nbr1 = dot_nt(r.back1[...], one(2)) / total2
    swaps[3].wait_recv()

    def self_block(part, rws, cls):
        back = jnp.concatenate([r.back1[:, cls], r.back1_o[:, cls]], axis=0)
        return dot(r.ht[part, rws, :], back)

    def nbr_block(part, rws, cls):
        back = jnp.concatenate([r.back1[:, cls], r.back1_o[:, cls]], axis=0)
        return dot(r.nt[part, rws, :], back)

    def fetch_block(part, rws, cls):
        return dot(r.xt[part, rws, 0:count], r.bf[:, cls]) + dot(r.xt[part, rws, 512:512 + count], r.bf_o[:, cls])

    start_first(1, self_block)
    start_first(2, nbr_block)
    high, low = split(back_nbr1)
    r.bf[...] = ((dot(of_node, high) + dot(of_node, low)) * act_slope(r.pre[...])).astype(BF16)
    swaps.append(remote(r.bf, r.bf_o, r.p_send.at[4], r.p_recv.at[4], partner))
    swaps[4].wait_recv()
    start_first(0, fetch_block)
    start_second(1)
    start_second(2)
    start_third(1)
    start_third(2)
    start_second(0)
    finish(1)
    finish(2)
    start_third(0)
    finish(0)

    wait_bytes(r.reqs.at[pl.ds(1, N_FEAT - 1)], r.q_send)
    wait_bytes(r.rep_out.at[pl.ds(1, N_FEAT - 1)], r.a_send)
    for sec in range(3):
        wait_bytes(w.at[pl.ds(0, NZ - 1), y, c, :, cols(sec, x)], r.z_send.at[sec])
        wait_bytes(w.at[:, pl.ds(0, NY - 1), c, :, cols(sec, x)], r.y_send.at[sec])
        wait_bytes(w.at[:, :, c, :, pl.ds(sec * D, D)], r.c_send.at[sec])
    for copy in list(across.values()) + swaps + sums + list(first.values()) + list(second.values()) + list(third.values()):
        copy.wait_send()


def on_device(
    table, hop2_owner, hop2_row, hop2_weight, hop1_feats, hop1_weight, target_feats, cotangent, layer_one, layer_two,
):
    count = hop2_row.shape[0]
    tab = jnp.stack(
        [hop2_owner[:, 0], hop2_row, hop2_weight, jnp.pad(hop1_weight, (0, count - hop1_weight.shape[0]))], axis=1)
    vmem, anywhere = pl.BlockSpec(memory_space=pltpu.VMEM), pl.BlockSpec(memory_space=pl.ANY)
    return pl.pallas_call(
        step_kernel,
        out_shape=(jax.ShapeDtypeStruct((1, D), BF16), jax.ShapeDtypeStruct((4, 3 * D), F32)),
        in_specs=[vmem, anywhere, vmem, vmem, vmem, anywhere, anywhere],
        out_specs=(vmem, vmem),
        scratch_shapes=[pltpu.VMEM(s, t) for _, s, t in SCRATCH] + [pltpu.SemaphoreType.DMA(s) for _, s in SEMS],
        compiler_params=pltpu.CompilerParams(collective_id=1, has_side_effects=True, vmem_limit_bytes=56 * 1024 * 1024),
        name="step",
    )(tab, table, hop1_feats, target_feats, cotangent, layer_one, layer_two)


def solution(mesh):
    both = P(("feat", "sect"), None)
    flat = P(("feat", "sect"))
    feat = P("feat", None)
    return jax.shard_map(
        on_device,
        mesh=mesh,
        in_specs=(feat, both, flat, flat, both, flat, feat, feat, feat, P()),
        out_specs=(both, both),
        check_vma=False,
    )
```

```python
import types

import jax
import jax.numpy as jnp
from jax import lax
from jax.experimental import pallas as pl
from jax.experimental.pallas import tpu as pltpu
from jax.sharding import PartitionSpec as P

MESH = pl.DeviceIdType.MESH
EPS = 1e-05
NZ, NY, NC, NX = 8, 4, 2, 4
N_FEAT = NZ * NY * NC
CAP, SLOTS = 12, 16
VM = 54
D = 1024
ROWS2, ROWS1, FAN, PER = 400, 20, 20, 5
PAD1, PADT = 32, 16
F32, BF16 = jnp.float32, jnp.bfloat16


def act(values):
    return values * jax.nn.sigmoid(values)


def act_slope(values):
    sig = jax.nn.sigmoid(values)
    return sig * (1.0 + values * (1.0 - sig))


def dot(a, b):
    return lax.dot_general(a, b, (((1,), (0,)), ((), ())), preferred_element_type=F32)


def dot_nt(a, b):
    return lax.dot_general(a, b, (((1,), (1,)), ((), ())), preferred_element_type=F32)


def dot_tn(a, b):
    return lax.dot_general(a, b, (((0,), (0,)), ((), ())), preferred_element_type=F32)


def split(values):
    high = values.astype(BF16)
    return high, (values - high.astype(F32)).astype(BF16)


def iota(shape, dim):
    return lax.broadcasted_iota(jnp.int32, shape, dim)


def coords():
    feat = lax.axis_index("feat")
    return feat // (NY * NC), (feat // NC) % NY, feat % NC, lax.axis_index("sect")


def device_at(z, y, c, x):
    return ((z * NY + y) * NC + c, x)


def remote(src, dst, send, recv, dev):
    copy = pltpu.make_async_remote_copy(
        src_ref=src, dst_ref=dst, send_sem=send, recv_sem=recv, device_id=dev, device_id_type=MESH)
    copy.start()
    return copy


def wait_bytes(ref, sem):
    pltpu.make_async_copy(ref, ref, sem).wait()


def row_pick(first, parity):
    m, lane = iota((D // 2, D), 0), iota((D // 2, D), 1)
    a, b, z, i = m // 128, (m // 32) % 4, (m // 4) % 8, m % 4
    y, x = (b, a) if first == "x" else (a, b)
    return (lane == z * 128 + y * 32 + parity * 16 + x * 4 + i).astype(BF16)


SCRATCH = [
    ("w", (NZ, NY, NC, 16, 3 * D), BF16), ("l2", (D, 3 * D), BF16), ("table", (512, D), BF16),
    ("rows", (16, ROWS2), F32), ("reqs", (N_FEAT, 1, 128), F32), ("rin", (N_FEAT, 1, 128), F32),
    ("rep_out", (N_FEAT, SLOTS, 768), BF16), ("rep_in", (N_FEAT, SLOTS, 768), BF16),
    ("hop", (PAD1, D), BF16), ("nbr1", (PAD1, D), BF16), ("back1", (PAD1, D), BF16),
    ("hop_o", (PAD1, D), BF16), ("nbr1_o", (PAD1, D), BF16), ("back1_o", (PAD1, D), BF16),
    ("tgt", (PADT, D), BF16), ("cot", (PADT, D), F32),
    ("fetched", (ROWS2, D), BF16), ("fetched_o", (ROWS2, D), BF16),
    ("bf", (ROWS2, D), BF16), ("bf_o", (ROWS2, D), BF16), ("pre", (ROWS2, D), F32),
    ("xt", (2, 512, 1024), BF16), ("ht", (2, 512, 64), BF16), ("nt", (2, 512, 64), BF16),
    ("msg", (8, D + 128), F32), ("msg_in", (NX - 1, 8, D + 128), F32),
    ("emb", (PADT, D), F32),
    ("send1", (3, 2, 3, 128, 512), BF16), ("recv1", (3, 2, 3, 128, 512), BF16), ("acc1", (3, 2, 128, 512), F32),
    ("send2", (3, 2, 3, 32, 512), BF16), ("recv2", (3, 2, 3, 32, 512), BF16),
    ("acc2", (2, 32, 512), F32), ("pk", (3, NZ, 16, 256), F32), ("send3", (3, NZ, 16, 256), BF16),
    ("recv3", (3, NZ - 1, 16, 256), BF16),
]
SEMS = [
    ("load", (3,)), ("own", (3,)), ("q_send", ()), ("q_recv", ()), ("a_send", ()), ("a_recv", ()),
    ("z_send", (3,)), ("z_recv", (3,)), ("y_send", (3,)), ("y_recv", (3,)),
    ("x_send", (3, 4)), ("x_recv", (3, 4)), ("c_send", (3,)), ("c_recv", (3,)),
    ("p_send", (5,)), ("p_recv", (5,)), ("m_send", (3,)), ("m_recv", (3,)),
    ("s1", (3, 2, 3)), ("r1", (3, 2, 3)), ("s2", (3, 2, 3)), ("r2", (3, 2, 3)), ("s3", (3, 7)), ("r3", (3, 7)),
]
INPUTS = ["owner", "row", "weight2", "weight1", "table_in", "hop_in", "tgt_in", "cot_in", "l1", "l2_in"]
OUTPUTS = ["emb_out", "grads_out"]


def step_kernel(*refs):
    names = INPUTS + OUTPUTS + [s[0] for s in SCRATCH] + [s[0] for s in SEMS]
    r = types.SimpleNamespace(**dict(zip(names, refs)))
    z, y, c, x = coords()
    me = lax.axis_index("feat")
    partner = device_at(z, y, 1 - c, x)
    xs = [device_at(z, y, c, (x + k) % NX) for k in range(NX)]
    ys = [device_at(z, (y + k) % NY, c, x) for k in range(NY)]
    zs = [device_at((z + k) % NZ, y, c, x) for k in range(NZ)]
    w = r.w

    barrier = pltpu.get_barrier_semaphore()

    def greet(k, carry):
        pl.semaphore_signal(barrier, inc=1, device_id=((me + k) % N_FEAT, x), device_id_type=MESH)
        return carry

    lax.fori_loop(1, N_FEAT, greet, 0)
    for dev in xs[1:]:
        pl.semaphore_signal(barrier, inc=1, device_id=dev, device_id_type=MESH)

    def cols(sec, at):
        return pl.ds(pl.multiple_of(sec * D + at * 256, 256), 256)

    loads = [pltpu.make_async_copy(r.table_in, r.table, r.load.at[0]), pltpu.make_async_copy(r.l2_in, r.l2, r.load.at[1])]
    for copy in loads:
        copy.start()
    owns = [pltpu.make_async_copy(r.l1.at[:, cols(sec, x)], w.at[z, y, c, :, cols(sec, x)], r.own.at[sec]) for sec in range(3)]
    for copy in owns:
        copy.start()

    count = ROWS2
    r.rows[...] = jnp.zeros_like(r.rows)
    r.rows[0:1, :] = r.owner[...].astype(F32)
    r.rows[1:2, :] = (r.row[...] // 32).astype(F32)
    r.rows[2:3, :] = (r.row[...] % 32).astype(F32)
    r.rows[3:4, :] = r.weight2[...].astype(F32)
    r.rows[4:5, 0:ROWS1] = r.weight1[...].astype(F32)
    eye = (iota((16, 128), 0) == iota((16, 128), 1)).astype(BF16)
    columns = dot_tn(r.rows[...].astype(BF16), eye).astype(jnp.int32)
    weight2, weight1 = columns[:, 3:4], columns[0:PAD1, 4:5]
    owner = columns[:, 0:1]
    rel = ((owner // NC + NY - y) % NY * NC + (owner + NC - c) % NC) * NZ + (owner // (NY * NC) + NZ - z) % NZ
    member = (iota((count, N_FEAT), 1) == rel).astype(BF16)
    before = (iota((count, count), 0) > iota((count, count), 1)).astype(BF16)
    slot = jnp.sum(dot(before, member) * member.astype(F32), axis=1, keepdims=True).astype(jnp.int32)
    lane = iota((count, 128), 1)
    asked = jnp.where(lane == slot, columns[:, 1:2], 0) + jnp.where(lane == slot + SLOTS, columns[:, 2:3], 0)
    r.reqs[...] = dot_tn(member, asked.astype(F32).astype(BF16)).reshape(N_FEAT, 1, 128)
    r.rin[0] = r.reqs[0]

    pl.semaphore_wait(barrier, N_FEAT - 1 + NX - 1)

    def ask(k, carry):
        dev = device_at((z + k) % NZ, (y + k // (NZ * NC)) % NY, (c + k // NZ) % NC, x)
        remote(r.reqs.at[k], r.rin.at[k], r.q_send, r.q_recv, dev)
        return carry

    lax.fori_loop(1, N_FEAT, ask, 0)
    for sec in range(3):
        for k in (4, 3, 5, 2, 6, 1, 7):
            remote(r.l1.at[:, cols(sec, x)], w.at[z, y, c, :, cols(sec, x)], r.z_send.at[sec], r.z_recv.at[sec], zs[k])

    r.hop[...] = jnp.zeros_like(r.hop)
    r.hop[0:ROWS1, :] = r.hop_in[...]
    r.tgt[...] = jnp.zeros_like(r.tgt)
    r.tgt[0:4, :] = r.tgt_in[...]
    r.cot[...] = jnp.zeros_like(r.cot)
    r.cot[0:4, :] = r.cot_in[...].astype(F32)
    swaps = [remote(r.hop, r.hop_o, r.p_send.at[0], r.p_recv.at[0], partner)]

    for sec in range(3):
        wait_bytes(w.at[pl.ds(0, NZ - 1), y, c, :, cols(sec, x)], r.z_recv.at[sec])
        owns[sec].wait()
        for k in (2, 1, 3):
            part = w.at[:, y, c, :, cols(sec, x)]
            remote(part, part, r.y_send.at[sec], r.y_recv.at[sec], ys[k])

    loads[0].wait()
    wait_bytes(r.rin.at[pl.ds(1, N_FEAT - 1)], r.q_recv)
    wanted = r.rin[...].reshape(N_FEAT, 128).astype(BF16)
    wide = 8 * SLOTS
    at_row, at_lane = iota((wide, 128), 0) % SLOTS, iota((wide, 128), 1)

    def pick_weights(slots):
        return (32 * (at_lane == slots).astype(jnp.int32) + (at_lane == slots + SLOTS).astype(jnp.int32)).astype(F32)

    main_at = pick_weights(at_row)
    rest_at = [pick_weights(4 * j + at_row - CAP) for j in range(3)]
    is_main = iota((wide, 1), 0) % SLOTS < CAP

    def chunk(g):
        group = (iota((wide, N_FEAT), 1) == g * 8 + iota((wide, N_FEAT), 0) // SLOTS).astype(BF16)
        spread = dot(group, wanted)
        ids = iota((wide, 512), 1).astype(F32)

        def chosen(weights, keep):
            target = jnp.where(keep, jnp.sum(spread * weights, axis=1, keepdims=True), -1.0)
            return (ids == target).astype(BF16)

        main = dot(chosen(main_at, is_main), r.table[:, 0:768])
        for j in range(3):
            rest = dot(chosen(rest_at[j], jnp.logical_not(is_main)), r.table[:, 768:1024])
            both = main[:, 256 * j:256 * j + 256] + rest
            r.rep_out[pl.ds(g * 8, 8), :, 256 * j:256 * j + 256] = both.astype(BF16).reshape(8, SLOTS, 256)

    def reply(k):
        dev = device_at((z + NZ - k % NZ) % NZ, (y + NY - k // (NZ * NC)) % NY, (c + NC - k // NZ % NC) % NC, x)
        remote(r.rep_out.at[k], r.rep_in.at[k], r.a_send, r.a_recv, dev)

    def serve(g, carry):
        chunk(g)
        for n in (4, 3, 5, 2, 6, 1, 7, 0):
            reply(g * 8 + n)
        return carry

    across = {}

    def along_x(sec):
        wait_bytes(w.at[:, pl.ds(0, NY - 1), c, :, cols(sec, x)], r.y_recv.at[sec])
        part = w.at[:, :, c, :, cols(sec, x)]
        for n, k in enumerate((1, 3)):
            across[sec, n] = remote(part, part, r.x_send.at[sec, n], r.x_recv.at[sec, n], xs[k])
        remote(part, part, r.c_send.at[sec], r.c_recv.at[sec], partner)

    chunk(0)
    for n in (4, 3, 5, 2, 6, 1, 7):
        reply(n)
    lax.fori_loop(1, 3, serve, 0)
    along_x(0)
    lax.fori_loop(3, 5, serve, 0)
    along_x(1)
    lax.fori_loop(5, 8, serve, 0)
    along_x(2)
    r.rep_in[0] = r.rep_out[0]

    for sec in range(3):
        for n, k in enumerate((1, 3)):
            across[sec, n].wait_recv()
            at = cols(sec, (x - k + NX) % NX)
            half = w.at[pl.ds(4 * n, 4), :, c, :, at]
            across[sec, 2 + n] = remote(half, half, r.x_send.at[sec, 2 + n], r.x_recv.at[sec, 2 + n], xs[k])
            part = w.at[:, :, c, :, at]
            remote(part, part, r.c_send.at[sec], r.c_recv.at[sec], partner)
    for sec in range(3):
        for n in range(2):
            across[sec, 2 + n].wait_recv()
            half = w.at[pl.ds(4 * n, 4), :, c, :, cols(sec, (x + 2) % NX)]
            remote(half, half, r.c_send.at[sec], r.c_recv.at[sec], partner)
    for sec in range(3):
        wait_bytes(w.at[:, :, c, :, pl.ds(sec * D, D)], r.c_recv.at[sec])
    loads[1].wait()

    def one(sec):
        return w[:, :, :, :, sec * D:sec * D + D].reshape(D, D)

    def two(sec):
        return r.l2[:, sec * D:sec * D + D]

    pre1_self = dot(r.hop[...], one(1))
    pre2_self = dot(r.tgt[...], two(1))
    swaps[0].wait_recv()
    for part, axis in enumerate("xy"):
        pick = row_pick(axis, c)
        r.ht[part, :, 0:32] = dot_nt(pick, r.hop[...]).astype(BF16)
        r.ht[part, :, 32:64] = dot_nt(pick, r.hop_o[...]).astype(BF16)

    wait_bytes(r.rep_in.at[pl.ds(1, N_FEAT - 1)], r.a_recv)
    total = N_FEAT * SLOTS
    places = iota((count, total), 1)
    base = rel * SLOTS
    answers = r.rep_in[...].reshape(total, 768)
    r.fetched[:, 0:768] = dot((places == base + slot).astype(BF16), answers).astype(BF16)
    rest = jnp.zeros((count, 256), F32)
    for j in range(3):
        place = jnp.where(slot // 4 == j, base + CAP + slot % 4, -1)
        rest = rest + dot((places == place).astype(BF16), answers[:, 256 * j:256 * j + 256])
    r.fetched[:, 768:1024] = rest.astype(BF16)
    swaps.append(remote(r.fetched, r.fetched_o, r.p_send.at[1], r.p_recv.at[1], partner))

    r.pre[...] = dot(r.fetched[...], one(0))
    of_node = jnp.where(iota((count, PAD1), 0) // FAN == iota((count, PAD1), 1), weight2, 0).astype(F32).astype(BF16)
    total2 = jnp.maximum(dot_tn(of_node, jnp.ones((count, 128), BF16))[:, 0:1], 1.0)
    high, low = split(act(r.pre[...]))
    r.nbr1[...] = ((dot_tn(of_node, high) + dot_tn(of_node, low)) / total2).astype(BF16)
    swaps.append(remote(r.nbr1, r.nbr1_o, r.p_send.at[2], r.p_recv.at[2], partner))
    pre1 = pre1_self + dot(r.nbr1[...], one(2))
    gated1 = act(pre1)
    scale1 = lax.rsqrt(jnp.mean(gated1 * gated1, axis=-1, keepdims=True) + EPS)
    norm1 = gated1 * scale1

    pre_hop1 = dot(norm1.astype(BF16), two(0))
    of_target = jnp.where(iota((PAD1, PADT), 0) // PER == iota((PAD1, PADT), 1), weight1, 0).astype(F32).astype(BF16)
    high, low = split(act(pre_hop1))
    numer = dot_tn(of_target, high) + dot_tn(of_target, low)
    weight = dot_tn(of_target, jnp.ones((PAD1, 128), BF16))
    r.msg[:, 0:D] = numer[0:8]
    r.msg[:, D:D + 128] = weight[0:8]
    sums = [remote(r.msg, r.msg_in.at[k - 1], r.m_send.at[k - 1], r.m_recv.at[k - 1], xs[k]) for k in (1, 2, 3)]
    swaps[1].wait_recv()
    swaps[2].wait_recv()
    for part, axis in enumerate("xy"):
        pick = row_pick(axis, c)
        r.xt[part, :, 0:count] = dot_nt(pick, r.fetched[...]).astype(BF16)
        r.xt[part, :, 512:512 + count] = dot_nt(pick, r.fetched_o[...]).astype(BF16)
        r.nt[part, :, 0:32] = dot_nt(pick, r.nbr1[...]).astype(BF16)
        r.nt[part, :, 32:64] = dot_nt(pick, r.nbr1_o[...]).astype(BF16)
    for copy in sums:
        copy.wait_recv()
    summed = r.msg[...] + r.msg_in[0] + r.msg_in[1] + r.msg_in[2]
    summed = jnp.concatenate([summed, jnp.zeros((PADT - 8, D + 128), F32)], axis=0)
    total1 = jnp.maximum(summed[:, D:D + 1], 1.0)
    nbr2 = (summed[:, 0:D] / total1).astype(BF16)
    pre2 = pre2_self + dot(nbr2, two(2))
    gated2 = act(pre2)
    scale2 = lax.rsqrt(jnp.mean(gated2 * gated2, axis=-1, keepdims=True) + EPS)
    norm2 = gated2 * scale2
    r.emb[...] = norm2
    cot = r.cot[...]
    back2 = (scale2 * (cot - norm2 * jnp.mean(cot * norm2, axis=-1, keepdims=True)) * act_slope(pre2)).astype(BF16)
    back_nbr2 = dot_nt(back2, two(2))
    high, low = split(back_nbr2 / total1)
    back_hop1 = ((dot(of_target, high) + dot(of_target, low)) * act_slope(pre_hop1)).astype(BF16)
    back_h1 = dot_nt(back_hop1, two(0))
    back1 = (scale1 * (back_h1 - norm1 * jnp.mean(back_h1 * norm1, axis=-1, keepdims=True)) * act_slope(pre1)).astype(BF16)
    r.back1[...] = back1
    swaps.append(remote(r.back1, r.back1_o, r.p_send.at[3], r.p_recv.at[3], partner))
    r.emb_out[...] = r.emb[pl.ds(x, 1), :].astype(BF16)

    first, second, third = {}, {}, {}

    def start_first(sec, value):
        for k in (2, 1, 3, 0):
            for part in range(2):
                at = lax.rem((x if part == 0 else y) + k, 4)
                v = value(part, pl.ds(pl.multiple_of(at * 128, 128), 128), slice(512 * part, 512 * part + 512))
                if k == 0:
                    r.acc1[sec, part] = v
                else:
                    r.send1[sec, part, k - 1] = v.astype(BF16)
                    first[sec, part, k] = remote(
                        r.send1.at[sec, part, k - 1], r.recv1.at[sec, part, k - 1], r.s1.at[sec, part, k - 1],
                        r.r1.at[sec, part, k - 1], (xs, ys)[part][k])

    def start_second(sec):
        for part in range(2):
            for k in (1, 3, 2):
                first[sec, part, k].wait_recv()
            r.acc1[sec, part] = (
                r.acc1[sec, part] + r.recv1[sec, part, 0].astype(F32) + r.recv1[sec, part, 1].astype(F32)
                + r.recv1[sec, part, 2].astype(F32))
            for k in (2, 1, 3):
                at = lax.rem((y if part == 0 else x) + k, 4)
                r.send2[sec, part, k - 1] = r.acc1[sec, part, pl.ds(pl.multiple_of(at * 32, 32), 32), :].astype(BF16)
                second[sec, part, k] = remote(
                    r.send2.at[sec, part, k - 1], r.recv2.at[sec, part, k - 1], r.s2.at[sec, part, k - 1],
                    r.r2.at[sec, part, k - 1], (ys, xs)[part][k])

    def start_third(sec):
        for part in range(2):
            for k in (1, 3, 2):
                second[sec, part, k].wait_recv()
            at = y if part == 0 else x
            r.acc2[part] = (
                r.acc1[sec, part, pl.ds(pl.multiple_of(at * 32, 32), 32), :] + r.recv2[sec, part, 0].astype(F32)
                + r.recv2[sec, part, 1].astype(F32) + r.recv2[sec, part, 2].astype(F32))
            for zz in range(NZ):
                for h in range(2):
                    q = 2 * part + h
                    r.pk[sec, zz, 4 * q:4 * q + 4, :] = r.acc2[part, 4 * zz:4 * zz + 4, 256 * h:256 * h + 256]
        r.send3[sec] = r.pk[sec].astype(BF16)
        for k in (4, 3, 5, 2, 6, 1, 7):
            third[sec, k] = remote(
                r.send3.at[sec, lax.rem(z + k, NZ)], r.recv3.at[sec, k - 1], r.s3.at[sec, k - 1], r.r3.at[sec, k - 1], zs[k])

    def finish(sec):
        value = r.pk[sec, z]
        for k in (1, 7, 2, 6, 3, 5, 4):
            third[sec, k].wait_recv()
            value = value + r.recv3[sec, k - 1].astype(F32)
        r.pk[sec, 0] = value
        for q in range(4):
            r.grads_out[:, sec * D + 256 * q:sec * D + 256 * q + 256] = r.pk[sec, 0, 4 * q:4 * q + 4, :]

    back_nbr1 = dot_nt(r.back1[...], one(2)) / total2
    swaps[3].wait_recv()

    def self_block(part, rws, cls):
        back = jnp.concatenate([r.back1[:, cls], r.back1_o[:, cls]], axis=0)
        return dot(r.ht[part, rws, :], back)

    def nbr_block(part, rws, cls):
        back = jnp.concatenate([r.back1[:, cls], r.back1_o[:, cls]], axis=0)
        return dot(r.nt[part, rws, :], back)

    def fetch_block(part, rws, cls):
        return dot(r.xt[part, rws, 0:count], r.bf[:, cls]) + dot(r.xt[part, rws, 512:512 + count], r.bf_o[:, cls])

    start_first(1, self_block)
    start_first(2, nbr_block)
    high, low = split(back_nbr1)
    r.bf[...] = ((dot(of_node, high) + dot(of_node, low)) * act_slope(r.pre[...])).astype(BF16)
    swaps.append(remote(r.bf, r.bf_o, r.p_send.at[4], r.p_recv.at[4], partner))
    swaps[4].wait_recv()
    start_first(0, fetch_block)
    start_second(1)
    start_second(2)
    start_second(0)
    start_third(1)
    start_third(2)
    start_third(0)
    finish(1)
    finish(2)
    finish(0)

    wait_bytes(r.reqs.at[pl.ds(1, N_FEAT - 1)], r.q_send)
    wait_bytes(r.rep_out.at[pl.ds(1, N_FEAT - 1)], r.a_send)
    for sec in range(3):
        wait_bytes(w.at[pl.ds(0, NZ - 1), y, c, :, cols(sec, x)], r.z_send.at[sec])
        wait_bytes(w.at[:, pl.ds(0, NY - 1), c, :, cols(sec, x)], r.y_send.at[sec])
        wait_bytes(w.at[:, :, c, :, pl.ds(sec * D, D)], r.c_send.at[sec])
    for copy in list(across.values()) + swaps + sums + list(first.values()) + list(second.values()) + list(third.values()):
        copy.wait_send()


def on_device(
    table, hop2_owner, hop2_row, hop2_weight, hop1_feats, hop1_weight, target_feats, cotangent, layer_one, layer_two,
):
    vmem, anywhere = pl.BlockSpec(memory_space=pltpu.VMEM), pl.BlockSpec(memory_space=pl.ANY)
    return pl.pallas_call(
        step_kernel,
        out_shape=(jax.ShapeDtypeStruct((1, D), BF16), jax.ShapeDtypeStruct((4, 3 * D), F32)),
        in_specs=[vmem, vmem, vmem, vmem, anywhere, vmem, vmem, vmem, anywhere, anywhere],
        out_specs=(vmem, vmem),
        scratch_shapes=[pltpu.VMEM(s, t) for _, s, t in SCRATCH] + [pltpu.SemaphoreType.DMA(s) for _, s in SEMS],
        compiler_params=pltpu.CompilerParams(collective_id=1, has_side_effects=True, vmem_limit_bytes=VM * 1024 * 1024),
        name="step",
    )(
        hop2_owner.reshape(1, ROWS2), hop2_row.reshape(1, ROWS2), hop2_weight.reshape(1, ROWS2), hop1_weight.reshape(1, ROWS1), table, hop1_feats, target_feats, cotangent, layer_one, layer_two)


def solution(mesh):
    both = P(("feat", "sect"), None)
    flat = P(("feat", "sect"))
    feat = P("feat", None)
    return jax.shard_map(
        on_device,
        mesh=mesh,
        in_specs=(feat, both, flat, flat, both, flat, feat, feat, feat, P()),
        out_specs=(both, both),
        check_vma=False,
    )
```

```python
import types

import jax
import jax.numpy as jnp
from jax import lax
from jax.experimental import pallas as pl
from jax.experimental.pallas import tpu as pltpu
from jax.sharding import PartitionSpec as P

MESH = pl.DeviceIdType.MESH
EPS = 1e-05
NZ, NY, NC, NX = 8, 4, 2, 4
N_FEAT = NZ * NY * NC
CAP, SLOTS = 12, 16
VM = 54
D = 1024
ROWS2, ROWS1, FAN, PER = 400, 20, 20, 5
PAD1, PADT = 32, 16
F32, BF16 = jnp.float32, jnp.bfloat16


def act(values):
    return values * jax.nn.sigmoid(values)


def act_slope(values):
    sig = jax.nn.sigmoid(values)
    return sig * (1.0 + values * (1.0 - sig))


def dot(a, b):
    return lax.dot_general(a, b, (((1,), (0,)), ((), ())), preferred_element_type=F32)


def dot_nt(a, b):
    return lax.dot_general(a, b, (((1,), (1,)), ((), ())), preferred_element_type=F32)


def dot_tn(a, b):
    return lax.dot_general(a, b, (((0,), (0,)), ((), ())), preferred_element_type=F32)


def split(values):
    high = values.astype(BF16)
    return high, (values - high.astype(F32)).astype(BF16)


def iota(shape, dim):
    return lax.broadcasted_iota(jnp.int32, shape, dim)


def coords():
    feat = lax.axis_index("feat")
    return feat // (NY * NC), (feat // NC) % NY, feat % NC, lax.axis_index("sect")


def device_at(z, y, c, x):
    return ((z * NY + y) * NC + c, x)


def remote(src, dst, send, recv, dev):
    copy = pltpu.make_async_remote_copy(
        src_ref=src, dst_ref=dst, send_sem=send, recv_sem=recv, device_id=dev, device_id_type=MESH)
    copy.start()
    return copy


def wait_bytes(ref, sem):
    pltpu.make_async_copy(ref, ref, sem).wait()


def row_pick(first, parity):
    m, lane = iota((D // 2, D), 0), iota((D // 2, D), 1)
    a, b, z, i = m // 128, (m // 32) % 4, (m // 4) % 8, m % 4
    y, x = (b, a) if first == "x" else (a, b)
    return (lane == z * 128 + y * 32 + parity * 16 + x * 4 + i).astype(BF16)


def line_pick(axis, c, y, x):
    m, lane = iota((128, D), 0), iota((128, D), 1)
    b, z, i = m // 32, (m // 4) % 8, m % 4
    y, x = (b, x) if axis == "x" else (y, b)
    return (lane == z * 128 + y * 32 + c * 16 + x * 4 + i).astype(BF16)


SCRATCH = [
    ("w", (NZ, NY, NC, 16, 3 * D), BF16), ("l2", (D, 3 * D), BF16), ("table", (512, D), BF16),
    ("rows", (16, ROWS2), F32), ("reqs", (N_FEAT, 1, 128), F32), ("rin", (N_FEAT, 1, 128), F32),
    ("rep_out", (N_FEAT, SLOTS, 768), BF16), ("rep_in", (N_FEAT, SLOTS, 768), BF16),
    ("hop", (PAD1, D), BF16), ("nbr1", (PAD1, D), BF16), ("back1", (PAD1, D), BF16),
    ("hop8", (2, 4, PAD1, D), BF16), ("nbr8", (2, 4, PAD1, D), BF16), ("back8", (2, 2, 4, PAD1, D), BF16),
    ("tgt", (PADT, D), BF16), ("cot", (PADT, D), F32),
    ("fetched", (ROWS2, D), BF16), ("fetched_o", (ROWS2, D), BF16),
    ("bf", (ROWS2, D), BF16), ("bf_o", (ROWS2, D), BF16), ("pre", (ROWS2, D), F32),
    ("xt", (2, 512, 1024), BF16), ("ht", (128, 256), BF16), ("nt", (128, 256), BF16),
    ("msg", (8, D + 128), F32), ("msg_in", (NX - 1, 8, D + 128), F32),
    ("emb", (PADT, D), F32),
    ("send1", (2, 3, 128, 512), BF16), ("recv1", (2, 3, 128, 512), BF16), ("acc1", (2, 128, 512), F32),
    ("send2", (2, 3, 32, 512), BF16), ("recv2", (2, 3, 32, 512), BF16),
    ("line", (2, 128, D), F32), ("send_l", (2, 3, 32, D), BF16), ("recv_l", (2, 3, 32, D), BF16),
    ("acc2", (2, 32, 512), F32), ("accl", (32, D), F32), ("pk", (3, NZ, 16, 256), F32), ("send3", (3, NZ, 16, 256), BF16),
    ("recv3", (3, NZ - 1, 16, 256), BF16),
]
SEMS = [
    ("load", (3,)), ("own", (3,)), ("q_send", ()), ("q_recv", ()), ("a_send", ()), ("a_recv", (4,)),
    ("z_send", (3,)), ("z_recv", (3,)), ("y_send", (3,)), ("y_recv", (3,)),
    ("x_send", (3, 4)), ("x_recv", (3, 4)), ("c_send", (3,)), ("c_recv", (3,)),
    ("p_send", (2,)), ("p_recv", (2,)), ("m_send", (3,)), ("m_recv", (3,)),
    ("s1", (2, 3)), ("r1", (2, 3)), ("s2", (2, 3)), ("r2", (2, 3)), ("sl", (2, 3)), ("rl", (2, 3)),
    ("h_send", (4,)), ("h_recv", (4,)), ("n_send", (4,)), ("n_recv", (4,)), ("b_send", (2, 4)), ("b_recv", (2, 4)), ("s3", (3, 7)), ("r3", (3, 7)),
]
INPUTS = ["owner", "row", "weight2", "weight1", "table_in", "hop_in", "tgt_in", "cot_in", "l1", "l2_in"]
OUTPUTS = ["emb_out", "grads_out"]


def step_kernel(*refs):
    names = INPUTS + OUTPUTS + [s[0] for s in SCRATCH] + [s[0] for s in SEMS]
    r = types.SimpleNamespace(**dict(zip(names, refs)))
    z, y, c, x = coords()
    me = lax.axis_index("feat")
    partner = device_at(z, y, 1 - c, x)
    xs = [device_at(z, y, c, (x + k) % NX) for k in range(NX)]
    ys = [device_at(z, (y + k) % NY, c, x) for k in range(NY)]
    zs = [device_at((z + k) % NZ, y, c, x) for k in range(NZ)]
    w = r.w

    barrier = pltpu.get_barrier_semaphore()

    def greet(k, carry):
        pl.semaphore_signal(barrier, inc=1, device_id=((me + k) % N_FEAT, x), device_id_type=MESH)
        return carry

    lax.fori_loop(1, N_FEAT, greet, 0)
    for dev in xs[1:]:
        pl.semaphore_signal(barrier, inc=1, device_id=dev, device_id_type=MESH)

    def cols(sec, at):
        return pl.ds(pl.multiple_of(sec * D + at * 256, 256), 256)

    loads = [pltpu.make_async_copy(r.table_in, r.table, r.load.at[0]), pltpu.make_async_copy(r.l2_in, r.l2, r.load.at[1])]
    for copy in loads:
        copy.start()
    owns = [pltpu.make_async_copy(r.l1.at[:, cols(sec, x)], w.at[z, y, c, :, cols(sec, x)], r.own.at[sec]) for sec in range(3)]
    for copy in owns:
        copy.start()

    count = ROWS2
    r.rows[...] = jnp.zeros_like(r.rows)
    r.rows[0:1, :] = r.owner[...].astype(F32)
    r.rows[1:2, :] = (r.row[...] // 32).astype(F32)
    r.rows[2:3, :] = (r.row[...] % 32).astype(F32)
    r.rows[3:4, :] = r.weight2[...].astype(F32)
    r.rows[4:5, 0:ROWS1] = r.weight1[...].astype(F32)
    eye = (iota((16, 128), 0) == iota((16, 128), 1)).astype(BF16)
    columns = dot_tn(r.rows[...].astype(BF16), eye).astype(jnp.int32)
    weight2, weight1 = columns[:, 3:4], columns[0:PAD1, 4:5]
    owner = columns[:, 0:1]
    rel = ((owner // NC + NY - y) % NY * NC + (owner + NC - c) % NC) * NZ + (owner // (NY * NC) + NZ - z) % NZ
    member = (iota((count, N_FEAT), 1) == rel).astype(BF16)
    before = (iota((count, count), 0) > iota((count, count), 1)).astype(BF16)
    slot = jnp.sum(dot(before, member) * member.astype(F32), axis=1, keepdims=True).astype(jnp.int32)
    lane = iota((count, 128), 1)
    asked = jnp.where(lane == slot, columns[:, 1:2], 0) + jnp.where(lane == slot + SLOTS, columns[:, 2:3], 0)
    r.reqs[...] = dot_tn(member, asked.astype(F32).astype(BF16)).reshape(N_FEAT, 1, 128)
    r.rin[0] = r.reqs[0]

    pl.semaphore_wait(barrier, N_FEAT - 1 + NX - 1)

    def ask(k, carry):
        dev = device_at((z + k) % NZ, (y + k // (NZ * NC)) % NY, (c + k // NZ) % NC, x)
        remote(r.reqs.at[k], r.rin.at[k], r.q_send, r.q_recv, dev)
        return carry

    lax.fori_loop(1, N_FEAT, ask, 0)
    for sec in range(3):
        for k in (4, 3, 5, 2, 6, 1, 7):
            remote(r.l1.at[:, cols(sec, x)], w.at[z, y, c, :, cols(sec, x)], r.z_send.at[sec], r.z_recv.at[sec], zs[k])

    r.hop[...] = jnp.zeros_like(r.hop)
    r.hop[0:ROWS1, :] = r.hop_in[...]
    r.tgt[...] = jnp.zeros_like(r.tgt)
    r.tgt[0:4, :] = r.tgt_in[...]
    r.cot[...] = jnp.zeros_like(r.cot)
    r.cot[0:4, :] = r.cot_in[...].astype(F32)

    def to_line(buf, send, recv, devs):
        return [remote(buf.at[0, 0], buf.at[0, k], send.at[k - 1], recv.at[k - 1], devs[k]) for k in (2, 1, 3)]

    def to_partner(copies, buf, send, recv):
        for copy in copies:
            copy.wait_recv()
        copies.append(remote(buf.at[0], buf.at[1], send.at[3], recv.at[3], partner))

    r.hop8[0, 0] = r.hop[...]
    hop_copies = to_line(r.hop8, r.h_send, r.h_recv, xs)
    swaps = []

    for sec in range(3):
        wait_bytes(w.at[pl.ds(0, NZ - 1), y, c, :, cols(sec, x)], r.z_recv.at[sec])
        owns[sec].wait()
        for k in (2, 1, 3):
            part = w.at[:, y, c, :, cols(sec, x)]
            remote(part, part, r.y_send.at[sec], r.y_recv.at[sec], ys[k])

    loads[0].wait()
    wait_bytes(r.rin.at[pl.ds(1, N_FEAT - 1)], r.q_recv)
    wanted = r.rin[...].reshape(N_FEAT, 128).astype(BF16)
    wide = 8 * SLOTS
    at_row, at_lane = iota((wide, 128), 0) % SLOTS, iota((wide, 128), 1)

    def pick_weights(slots):
        return (32 * (at_lane == slots).astype(jnp.int32) + (at_lane == slots + SLOTS).astype(jnp.int32)).astype(F32)

    main_at = pick_weights(at_row)
    rest_at = [pick_weights(4 * j + at_row - CAP) for j in range(3)]
    is_main = iota((wide, 1), 0) % SLOTS < CAP

    def chunk(g):
        group = (iota((wide, N_FEAT), 1) == g * 8 + iota((wide, N_FEAT), 0) // SLOTS).astype(BF16)
        spread = dot(group, wanted)
        ids = iota((wide, 512), 1).astype(F32)

        def chosen(weights, keep):
            target = jnp.where(keep, jnp.sum(spread * weights, axis=1, keepdims=True), -1.0)
            return (ids == target).astype(BF16)

        main = dot(chosen(main_at, is_main), r.table[:, 0:768])
        for j in range(3):
            rest = dot(chosen(rest_at[j], jnp.logical_not(is_main)), r.table[:, 768:1024])
            both = main[:, 256 * j:256 * j + 256] + rest
            r.rep_out[pl.ds(g * 8, 8), :, 256 * j:256 * j + 256] = both.astype(BF16).reshape(8, SLOTS, 256)

    def reply(k):
        dev = device_at((z + NZ - k % NZ) % NZ, (y + NY - k // (NZ * NC)) % NY, (c + NC - k // NZ % NC) % NC, x)
        remote(r.rep_out.at[k], r.rep_in.at[k], r.a_send, r.a_recv.at[k // 16], dev)

    def serve(g, carry):
        chunk(g)
        for n in (4, 3, 5, 2, 6, 1, 7, 0):
            reply(g * 8 + n)
        return carry

    across = {}

    def along_x(sec):
        wait_bytes(w.at[:, pl.ds(0, NY - 1), c, :, cols(sec, x)], r.y_recv.at[sec])
        part = w.at[:, :, c, :, cols(sec, x)]
        for n, k in enumerate((1, 3)):
            across[sec, n] = remote(part, part, r.x_send.at[sec, n], r.x_recv.at[sec, n], xs[k])
        remote(part, part, r.c_send.at[sec], r.c_recv.at[sec], partner)

    chunk(0)
    for n in (4, 3, 5, 2, 6, 1, 7):
        reply(n)
    lax.fori_loop(1, 3, serve, 0)
    along_x(0)
    lax.fori_loop(3, 5, serve, 0)
    along_x(1)
    lax.fori_loop(5, 8, serve, 0)
    along_x(2)
    r.rep_in[0] = r.rep_out[0]

    for sec in range(3):
        for n, k in enumerate((1, 3)):
            across[sec, n].wait_recv()
            at = cols(sec, (x - k + NX) % NX)
            half = w.at[pl.ds(4 * n, 4), :, c, :, at]
            across[sec, 2 + n] = remote(half, half, r.x_send.at[sec, 2 + n], r.x_recv.at[sec, 2 + n], xs[k])
            part = w.at[:, :, c, :, at]
            remote(part, part, r.c_send.at[sec], r.c_recv.at[sec], partner)
    def unpack(part):
        low = max(16 * part, 1)
        wait_bytes(r.rep_in.at[pl.ds(low, 16 * part + 16 - low)], r.a_recv.at[part])
        answers = r.rep_in[16 * part:16 * part + 16].reshape(256, 768)
        places = iota((count, 256), 1) + 256 * part
        base = rel * SLOTS
        main = dot((places == base + slot).astype(BF16), answers)
        rest = jnp.zeros((count, 256), F32)
        for j in range(3):
            place = jnp.where(slot // 4 == j, base + CAP + slot % 4, -1)
            rest = rest + dot((places == place).astype(BF16), answers[:, 256 * j:256 * j + 256])
        if part:
            main, rest = main + r.pre[:, 0:768], rest + r.pre[:, 768:1024]
        r.pre[:, 0:768] = main
        r.pre[:, 768:1024] = rest

    unpack(0)
    for sec in range(3):
        for n in range(2):
            across[sec, 2 + n].wait_recv()
            half = w.at[pl.ds(4 * n, 4), :, c, :, cols(sec, (x + 2) % NX)]
            remote(half, half, r.c_send.at[sec], r.c_recv.at[sec], partner)
    unpack(1)
    for sec in range(3):
        wait_bytes(w.at[:, :, c, :, pl.ds(sec * D, D)], r.c_recv.at[sec])
    loads[1].wait()

    def one(sec):
        return w[:, :, :, :, sec * D:sec * D + D].reshape(D, D)

    def two(sec):
        return r.l2[:, sec * D:sec * D + D]

    to_partner(hop_copies, r.hop8, r.h_send, r.h_recv)
    pre1_self = dot(r.hop[...], one(1))
    pre2_self = dot(r.tgt[...], two(1))
    hop_copies[3].wait_recv()
    r.ht[...] = dot_nt(line_pick("x", c, y, x), r.hop8[...].reshape(256, D)).astype(BF16)
    unpack(2)
    unpack(3)
    r.fetched[...] = r.pre[...].astype(BF16)
    swaps.append(remote(r.fetched, r.fetched_o, r.p_send.at[0], r.p_recv.at[0], partner))

    pre = dot(r.fetched[...], one(0))
    sig = jax.nn.sigmoid(pre)
    high, low = split(pre * sig)
    r.pre[...] = sig * (1.0 + pre * (1.0 - sig))
    of_node = jnp.where(iota((count, PAD1), 0) // FAN == iota((count, PAD1), 1), weight2, 0).astype(F32).astype(BF16)
    total2 = jnp.maximum(dot_tn(of_node, jnp.ones((count, 128), BF16))[:, 0:1], 1.0)
    r.nbr1[...] = ((dot_tn(of_node, high) + dot_tn(of_node, low)) / total2).astype(BF16)
    r.nbr8[0, 0] = r.nbr1[...]
    nbr_copies = to_line(r.nbr8, r.n_send, r.n_recv, ys)
    pre1 = pre1_self + dot(r.nbr1[...], one(2))
    gated1 = act(pre1)
    scale1 = lax.rsqrt(jnp.mean(gated1 * gated1, axis=-1, keepdims=True) + EPS)
    norm1 = gated1 * scale1

    pre_hop1 = dot(norm1.astype(BF16), two(0))
    of_target = jnp.where(iota((PAD1, PADT), 0) // PER == iota((PAD1, PADT), 1), weight1, 0).astype(F32).astype(BF16)
    high, low = split(act(pre_hop1))
    numer = dot_tn(of_target, high) + dot_tn(of_target, low)
    weight = dot_tn(of_target, jnp.ones((PAD1, 128), BF16))
    r.msg[:, 0:D] = numer[0:8]
    r.msg[:, D:D + 128] = weight[0:8]
    sums = [remote(r.msg, r.msg_in.at[k - 1], r.m_send.at[k - 1], r.m_recv.at[k - 1], xs[k]) for k in (1, 2, 3)]
    to_partner(nbr_copies, r.nbr8, r.n_send, r.n_recv)
    swaps[0].wait_recv()
    for part, axis in enumerate("xy"):
        pick = row_pick(axis, c)
        r.xt[part, :, 0:count] = dot_nt(pick, r.fetched[...]).astype(BF16)
        r.xt[part, :, 512:512 + count] = dot_nt(pick, r.fetched_o[...]).astype(BF16)
    nbr_copies[3].wait_recv()
    r.nt[...] = dot_nt(line_pick("y", c, y, x), r.nbr8[...].reshape(256, D)).astype(BF16)
    for copy in sums:
        copy.wait_recv()
    summed = r.msg[...] + r.msg_in[0] + r.msg_in[1] + r.msg_in[2]
    summed = jnp.concatenate([summed, jnp.zeros((PADT - 8, D + 128), F32)], axis=0)
    total1 = jnp.maximum(summed[:, D:D + 1], 1.0)
    nbr2 = (summed[:, 0:D] / total1).astype(BF16)
    pre2 = pre2_self + dot(nbr2, two(2))
    gated2 = act(pre2)
    scale2 = lax.rsqrt(jnp.mean(gated2 * gated2, axis=-1, keepdims=True) + EPS)
    norm2 = gated2 * scale2
    r.emb[...] = norm2
    cot = r.cot[...]
    back2 = (scale2 * (cot - norm2 * jnp.mean(cot * norm2, axis=-1, keepdims=True)) * act_slope(pre2)).astype(BF16)
    back_nbr2 = dot_nt(back2, two(2))
    high, low = split(back_nbr2 / total1)
    back_hop1 = ((dot(of_target, high) + dot(of_target, low)) * act_slope(pre_hop1)).astype(BF16)
    back_h1 = dot_nt(back_hop1, two(0))
    back1 = (scale1 * (back_h1 - norm1 * jnp.mean(back_h1 * norm1, axis=-1, keepdims=True)) * act_slope(pre1)).astype(BF16)
    r.back1[...] = back1
    back_copies = []
    for n, devs in enumerate((xs, ys)):
        r.back8[n, 0, 0] = back1
        back_copies.append(to_line(r.back8.at[n], r.b_send.at[n], r.b_recv.at[n], devs))
    r.emb_out[...] = r.emb[pl.ds(x, 1), :]

    first, second, third, lines = {}, {}, {}, {}

    def start_first(value):
        for k in (2, 1, 3, 0):
            for part in range(2):
                at = lax.rem((x if part == 0 else y) + k, 4)
                v = value(part, pl.ds(pl.multiple_of(at * 128, 128), 128), slice(512 * part, 512 * part + 512))
                if k == 0:
                    r.acc1[part] = v
                else:
                    r.send1[part, k - 1] = v.astype(BF16)
                    first[part, k] = remote(
                        r.send1.at[part, k - 1], r.recv1.at[part, k - 1], r.s1.at[part, k - 1], r.r1.at[part, k - 1],
                        (xs, ys)[part][k])

    def start_second():
        for part in range(2):
            for k in (1, 3, 2):
                first[part, k].wait_recv()
            r.acc1[part] = (
                r.acc1[part] + r.recv1[part, 0].astype(F32) + r.recv1[part, 1].astype(F32) + r.recv1[part, 2].astype(F32))
            for k in (2, 1, 3):
                at = lax.rem((y if part == 0 else x) + k, 4)
                r.send2[part, k - 1] = r.acc1[part, pl.ds(pl.multiple_of(at * 32, 32), 32), :].astype(BF16)
                second[part, k] = remote(
                    r.send2.at[part, k - 1], r.recv2.at[part, k - 1], r.s2.at[part, k - 1], r.r2.at[part, k - 1],
                    (ys, xs)[part][k])

    def start_line(n, rows):
        back_copies[n][3].wait_recv()
        r.line[n] = dot(rows, r.back8[n].reshape(256, D))
        for k in (2, 1, 3):
            at = lax.rem((y if n == 0 else x) + k, 4)
            r.send_l[n, k - 1] = r.line[n, pl.ds(pl.multiple_of(at * 32, 32), 32), :].astype(BF16)
            lines[n, k] = remote(
                r.send_l.at[n, k - 1], r.recv_l.at[n, k - 1], r.sl.at[n, k - 1], r.rl.at[n, k - 1], (ys, xs)[n][k])

    def start_third(sec):
        r.send3[sec] = r.pk[sec].astype(BF16)
        for k in (4, 3, 5, 2, 6, 1, 7):
            third[sec, k] = remote(
                r.send3.at[sec, lax.rem(z + k, NZ)], r.recv3.at[sec, k - 1], r.s3.at[sec, k - 1], r.r3.at[sec, k - 1], zs[k])

    def third_of_line(n):
        for k in (1, 3, 2):
            lines[n, k].wait_recv()
        own = pl.ds(pl.multiple_of((y if n == 0 else x) * 32, 32), 32)
        r.accl[...] = (
            r.line[n, own, :] + r.recv_l[n, 0].astype(F32) + r.recv_l[n, 1].astype(F32) + r.recv_l[n, 2].astype(F32))
        for zz in range(NZ):
            for q in range(4):
                r.pk[n + 1, zz, 4 * q:4 * q + 4, :] = r.accl[4 * zz:4 * zz + 4, 256 * q:256 * q + 256]
        start_third(n + 1)

    def third_of_fetch():
        for part in range(2):
            for k in (1, 3, 2):
                second[part, k].wait_recv()
            at = y if part == 0 else x
            r.acc2[part] = (
                r.acc1[part, pl.ds(pl.multiple_of(at * 32, 32), 32), :] + r.recv2[part, 0].astype(F32)
                + r.recv2[part, 1].astype(F32) + r.recv2[part, 2].astype(F32))
            for zz in range(NZ):
                for h in range(2):
                    q = 2 * part + h
                    r.pk[0, zz, 4 * q:4 * q + 4, :] = r.acc2[part, 4 * zz:4 * zz + 4, 256 * h:256 * h + 256]
        start_third(0)

    def finish(sec):
        value = r.pk[sec, z]
        for k in (1, 7, 2, 6, 3, 5, 4):
            third[sec, k].wait_recv()
            value = value + r.recv3[sec, k - 1].astype(F32)
        r.pk[sec, 0] = value
        for q in range(4):
            r.grads_out[:, sec * D + 256 * q:sec * D + 256 * q + 256] = r.pk[sec, 0, 4 * q:4 * q + 4, :]

    back_nbr1 = dot_nt(r.back1[...], one(2)) / total2
    of_node = jnp.concatenate([of_node, of_node], axis=1)
    r.bf[...] = (dot(of_node, jnp.concatenate(split(back_nbr1), axis=0)) * r.pre[...]).astype(BF16)
    swaps.append(remote(r.bf, r.bf_o, r.p_send.at[1], r.p_recv.at[1], partner))
    for n in range(2):
        to_partner(back_copies[n], r.back8.at[n], r.b_send.at[n], r.b_recv.at[n])

    def fetch_block(part, rws, cls):
        return dot(r.xt[part, rws, 0:count], r.bf[:, cls]) + dot(r.xt[part, rws, 512:512 + count], r.bf_o[:, cls])

    swaps[1].wait_recv()
    start_first(fetch_block)
    start_line(0, r.ht[...])
    start_line(1, r.nt[...])
    start_second()
    third_of_line(0)
    third_of_line(1)
    third_of_fetch()
    finish(1)
    finish(2)
    finish(0)

    wait_bytes(r.reqs.at[pl.ds(1, N_FEAT - 1)], r.q_send)
    wait_bytes(r.rep_out.at[pl.ds(1, N_FEAT - 1)], r.a_send)
    for sec in range(3):
        wait_bytes(w.at[pl.ds(0, NZ - 1), y, c, :, cols(sec, x)], r.z_send.at[sec])
        wait_bytes(w.at[:, pl.ds(0, NY - 1), c, :, cols(sec, x)], r.y_send.at[sec])
        wait_bytes(w.at[:, :, c, :, pl.ds(sec * D, D)], r.c_send.at[sec])
    for copy in list(across.values()) + swaps + sums + hop_copies + nbr_copies + back_copies[0] + back_copies[1]:
        copy.wait_send()
    for copy in list(first.values()) + list(second.values()) + list(lines.values()) + list(third.values()):
        copy.wait_send()


def on_device(
    table, hop2_owner, hop2_row, hop2_weight, hop1_feats, hop1_weight, target_feats, cotangent, layer_one, layer_two,
):
    vmem, anywhere = pl.BlockSpec(memory_space=pltpu.VMEM), pl.BlockSpec(memory_space=pl.ANY)
    emb, grads = pl.pallas_call(
        step_kernel,
        out_shape=(jax.ShapeDtypeStruct((1, D), F32), jax.ShapeDtypeStruct((4, 3 * D), F32)),
        in_specs=[vmem, vmem, vmem, vmem, anywhere, vmem, vmem, vmem, anywhere, anywhere],
        out_specs=(vmem, vmem),
        scratch_shapes=[pltpu.VMEM(s, t) for _, s, t in SCRATCH] + [pltpu.SemaphoreType.DMA(s) for _, s in SEMS],
        compiler_params=pltpu.CompilerParams(collective_id=1, has_side_effects=True, vmem_limit_bytes=VM * 1024 * 1024),
        name="step",
    )(
        hop2_owner.reshape(1, ROWS2), hop2_row.reshape(1, ROWS2), hop2_weight.reshape(1, ROWS2), hop1_weight.reshape(1, ROWS1), table, hop1_feats, target_feats, cotangent, layer_one, layer_two)

    def hand_over(emb_ref, grads_ref, emb_out, grads_out):
        emb_out[...] = emb_ref[...].astype(BF16)
        grads_out[...] = grads_ref[...]

    return pl.pallas_call(
        hand_over,
        out_shape=(jax.ShapeDtypeStruct((1, D), BF16), jax.ShapeDtypeStruct((4, 3 * D), F32)),
        in_specs=[vmem, vmem],
        out_specs=(vmem, vmem),
        name="hand_over",
    )(emb, grads)


def solution(mesh):
    both = P(("feat", "sect"), None)
    flat = P(("feat", "sect"))
    feat = P("feat", None)
    return jax.shard_map(
        on_device,
        mesh=mesh,
        in_specs=(feat, both, flat, flat, both, flat, feat, feat, feat, P()),
        out_specs=(both, both),
        check_vma=False,
    )
```

```python
import types

import jax
import jax.numpy as jnp
from jax import lax
from jax.experimental import pallas as pl
from jax.experimental.pallas import tpu as pltpu
from jax.sharding import PartitionSpec as P

MESH = pl.DeviceIdType.MESH
EPS = 1e-05
NZ, NY, NC, NX = 8, 4, 2, 4
N_FEAT = NZ * NY * NC
CAP, SLOTS = 12, 16
VM = 54
D = 1024
ROWS2, ROWS1, FAN, PER = 400, 20, 20, 5
PAD1, PADT = 32, 16
F32, BF16 = jnp.float32, jnp.bfloat16


def act(values):
    return values * jax.nn.sigmoid(values)


def act_slope(values):
    sig = jax.nn.sigmoid(values)
    return sig * (1.0 + values * (1.0 - sig))


def dot(a, b):
    return lax.dot_general(a, b, (((1,), (0,)), ((), ())), preferred_element_type=F32)


def dot_nt(a, b):
    return lax.dot_general(a, b, (((1,), (1,)), ((), ())), preferred_element_type=F32)


def dot_tn(a, b):
    return lax.dot_general(a, b, (((0,), (0,)), ((), ())), preferred_element_type=F32)


def split(values):
    high = values.astype(BF16)
    return high, (values - high.astype(F32)).astype(BF16)


def iota(shape, dim):
    return lax.broadcasted_iota(jnp.int32, shape, dim)


def coords():
    feat = lax.axis_index("feat")
    return feat // (NY * NC), (feat // NC) % NY, feat % NC, lax.axis_index("sect")


def device_at(z, y, c, x):
    return ((z * NY + y) * NC + c, x)


def remote(src, dst, send, recv, dev):
    copy = pltpu.make_async_remote_copy(
        src_ref=src, dst_ref=dst, send_sem=send, recv_sem=recv, device_id=dev, device_id_type=MESH)
    copy.start()
    return copy


def wait_bytes(ref, sem):
    pltpu.make_async_copy(ref, ref, sem).wait()


def row_pick(first, parity):
    m, lane = iota((D // 2, D), 0), iota((D // 2, D), 1)
    a, b, z, i = m // 128, (m // 32) % 4, (m // 4) % 8, m % 4
    y, x = (b, a) if first == "x" else (a, b)
    return (lane == z * 128 + y * 32 + parity * 16 + x * 4 + i).astype(BF16)


def line_pick(axis, c, y, x):
    m, lane = iota((128, D), 0), iota((128, D), 1)
    b, z, i = m // 32, (m // 4) % 8, m % 4
    y, x = (b, x) if axis == "x" else (y, b)
    return (lane == z * 128 + y * 32 + c * 16 + x * 4 + i).astype(BF16)


SCRATCH = [
    ("w", (NZ, NY, NC, 16, 3 * D), BF16), ("l2", (D, 3 * D), BF16), ("table", (512, D), BF16),
    ("owner", (1, ROWS2), jnp.int32), ("row", (1, ROWS2), jnp.int32), ("weight2", (1, ROWS2), jnp.int32),
    ("weight1", (1, ROWS1), jnp.int32), ("rows", (16, ROWS2), F32), ("reqs", (N_FEAT, 1, 128), F32), ("rin", (N_FEAT, 1, 128), F32),
    ("rep_out", (N_FEAT, SLOTS, 768), BF16), ("rep_in", (N_FEAT, SLOTS, 768), BF16),
    ("hop", (PAD1, D), BF16), ("nbr1", (PAD1, D), BF16), ("back1", (PAD1, D), BF16),
    ("hop8", (2, 4, PAD1, D), BF16), ("nbr8", (2, 4, PAD1, D), BF16), ("back8", (2, 2, 4, PAD1, D), BF16),
    ("tgt", (PADT, D), BF16), ("cot", (PADT, D), F32),
    ("fetched", (ROWS2, D), BF16), ("fetched_o", (ROWS2, D), BF16),
    ("bf", (2, ROWS2, 512), BF16), ("bf_o", (2, ROWS2, 512), BF16), ("mine", (2, 512, 512), F32), ("pre", (ROWS2, D), F32),
    ("xt", (2, 512, 1024), BF16), ("ht", (128, 256), BF16), ("nt", (128, 256), BF16),
    ("msg", (4, D + 128), F32), ("msg_in", (NX - 1, 4, D + 128), F32),
    ("emb", (PADT, D), F32), ("summed", (PADT, D + 128), F32),
    ("send1", (2, 3, 128, 512), BF16), ("recv1", (2, 3, 128, 512), BF16), ("acc1", (2, 128, 512), F32),
    ("send2", (2, 3, 32, 512), BF16), ("recv2", (2, 3, 32, 512), BF16),
    ("line", (2, 128, D), F32), ("send_l", (2, 3, 32, D), BF16), ("recv_l", (2, 3, 32, D), BF16),
    ("acc2", (2, 32, 512), F32), ("accl", (32, D), F32), ("pk", (3, NZ, 16, 256), F32), ("send3", (3, NZ, 16, 256), BF16),
    ("recv3", (3, NZ - 1, 16, 256), BF16),
]
SEMS = [
    ("load", (2,)), ("index", (4,)), ("own", (3,)), ("q_send", ()), ("q_recv", ()), ("a_send", ()), ("a_recv", (4,)),
    ("z_send", (3,)), ("z_recv", (3,)), ("y_send", (3,)), ("y_recv", (3,)),
    ("x_send", (3, 4)), ("x_recv", (3, 4)), ("c_send", (3,)), ("c_recv", (3,)),
    ("p_send", (3,)), ("p_recv", (3,)), ("m_send", (3,)), ("m_recv", (3,)),
    ("s1", (2, 3)), ("r1", (2, 3)), ("s2", (2, 3)), ("r2", (2, 3)), ("sl", (2, 3)), ("rl", (2, 3)),
    ("h_send", (4,)), ("h_recv", (4,)), ("n_send", (4,)), ("n_recv", (4,)), ("b_send", (2, 4)), ("b_recv", (2, 4)), ("s3", (3, 7)), ("r3", (3, 7)),
]
INPUTS = ["owner_in", "row_in", "weight2_in", "weight1_in", "table_in", "hop_in", "tgt_in", "cot_in", "l1", "l2_in"]
OUTPUTS = ["emb_out", "grads_out"]


def step_kernel(*refs):
    names = INPUTS + OUTPUTS + [s[0] for s in SCRATCH] + [s[0] for s in SEMS]
    r = types.SimpleNamespace(**dict(zip(names, refs)))
    z, y, c, x = coords()
    me = lax.axis_index("feat")
    partner = device_at(z, y, 1 - c, x)
    xs = [device_at(z, y, c, (x + k) % NX) for k in range(NX)]
    ys = [device_at(z, (y + k) % NY, c, x) for k in range(NY)]
    zs = [device_at((z + k) % NZ, y, c, x) for k in range(NZ)]
    w = r.w

    numbers = [
        pltpu.make_async_copy(src, dst, r.index.at[n]) for n, (src, dst) in enumerate([
            (r.owner_in, r.owner), (r.row_in, r.row), (r.weight2_in, r.weight2), (r.weight1_in, r.weight1)])]
    for copy in numbers:
        copy.start()

    barrier = pltpu.get_barrier_semaphore()

    def greet(k, carry):
        pl.semaphore_signal(barrier, inc=1, device_id=((me + k) % N_FEAT, x), device_id_type=MESH)
        return carry

    lax.fori_loop(1, N_FEAT, greet, 0)
    for dev in xs[1:]:
        pl.semaphore_signal(barrier, inc=1, device_id=dev, device_id_type=MESH)

    def cols(sec, at):
        return pl.ds(pl.multiple_of(sec * D + at * 256, 256), 256)

    loads = [pltpu.make_async_copy(r.table_in, r.table, r.load.at[0]), pltpu.make_async_copy(r.l2_in, r.l2, r.load.at[1])]
    for copy in loads:
        copy.start()
    owns = [pltpu.make_async_copy(r.l1.at[:, cols(sec, x)], w.at[z, y, c, :, cols(sec, x)], r.own.at[sec]) for sec in range(3)]
    for copy in owns:
        copy.start()

    count = ROWS2
    r.rows[...] = jnp.zeros_like(r.rows)
    for copy in numbers:
        copy.wait()
    r.rows[0:1, :] = r.owner[...].astype(F32)
    r.rows[1:2, :] = (r.row[...] // 32).astype(F32)
    r.rows[2:3, :] = (r.row[...] % 32).astype(F32)
    r.rows[3:4, :] = r.weight2[...].astype(F32)
    r.rows[4:5, 0:ROWS1] = r.weight1[...].astype(F32)
    eye = (iota((16, 128), 0) == iota((16, 128), 1)).astype(BF16)
    columns = dot_tn(r.rows[...].astype(BF16), eye).astype(jnp.int32)
    weight2, weight1 = columns[:, 3:4], columns[0:PAD1, 4:5]
    owner = columns[:, 0:1]
    rel = ((owner // NC + NY - y) % NY * NC + (owner + NC - c) % NC) * NZ + (owner // (NY * NC) + NZ - z) % NZ
    member = (iota((count, N_FEAT), 1) == rel).astype(BF16)
    before = (iota((count, count), 0) > iota((count, count), 1)).astype(BF16)
    slot = jnp.sum(dot(before, member) * member.astype(F32), axis=1, keepdims=True).astype(jnp.int32)
    lane = iota((count, 128), 1)
    asked = jnp.where(lane == slot, columns[:, 1:2], 0) + jnp.where(lane == slot + SLOTS, columns[:, 2:3], 0)
    r.reqs[...] = dot_tn(member, asked.astype(F32).astype(BF16)).reshape(N_FEAT, 1, 128)
    r.rin[0] = r.reqs[0]

    pl.semaphore_wait(barrier, N_FEAT - 1 + NX - 1)

    def ask(k, carry):
        dev = device_at((z + k) % NZ, (y + k // (NZ * NC)) % NY, (c + k // NZ) % NC, x)
        remote(r.reqs.at[k], r.rin.at[k], r.q_send, r.q_recv, dev)
        return carry

    lax.fori_loop(1, N_FEAT, ask, 0)
    for sec in range(3):
        for k in (4, 3, 5, 2, 6, 1, 7):
            remote(r.l1.at[:, cols(sec, x)], w.at[z, y, c, :, cols(sec, x)], r.z_send.at[sec], r.z_recv.at[sec], zs[k])

    r.hop[...] = jnp.zeros_like(r.hop)
    r.hop[0:ROWS1, :] = r.hop_in[...]
    r.tgt[...] = jnp.zeros_like(r.tgt)
    r.tgt[0:4, :] = r.tgt_in[...]
    r.cot[...] = jnp.zeros_like(r.cot)
    r.cot[0:4, :] = r.cot_in[...].astype(F32)

    def to_line(buf, send, recv, devs):
        return [remote(buf.at[0, 0], buf.at[0, k], send.at[k - 1], recv.at[k - 1], devs[k]) for k in (2, 1, 3)]

    def to_partner(copies, buf, send, recv):
        for copy in copies:
            copy.wait_recv()
        copies.append(remote(buf.at[0], buf.at[1], send.at[3], recv.at[3], partner))

    r.hop8[0, 0] = r.hop[...]
    hop_copies = to_line(r.hop8, r.h_send, r.h_recv, xs)
    swaps = []

    for sec in range(3):
        wait_bytes(w.at[pl.ds(0, NZ - 1), y, c, :, cols(sec, x)], r.z_recv.at[sec])
        owns[sec].wait()
        for k in (2, 1, 3):
            part = w.at[:, y, c, :, cols(sec, x)]
            remote(part, part, r.y_send.at[sec], r.y_recv.at[sec], ys[k])

    loads[0].wait()
    wait_bytes(r.rin.at[pl.ds(1, N_FEAT - 1)], r.q_recv)
    wanted = r.rin[...].reshape(N_FEAT, 128).astype(BF16)
    wide = 8 * SLOTS
    at_row, at_lane = iota((wide, 128), 0) % SLOTS, iota((wide, 128), 1)

    def pick_weights(slots):
        return (32 * (at_lane == slots).astype(jnp.int32) + (at_lane == slots + SLOTS).astype(jnp.int32)).astype(F32)

    main_at = pick_weights(at_row)
    rest_at = [pick_weights(4 * j + at_row - CAP) for j in range(3)]
    is_main = iota((wide, 1), 0) % SLOTS < CAP

    def chunk(g):
        group = (iota((wide, N_FEAT), 1) == g * 8 + iota((wide, N_FEAT), 0) // SLOTS).astype(BF16)
        spread = dot(group, wanted)
        ids = iota((wide, 512), 1).astype(F32)

        def chosen(weights, keep):
            target = jnp.where(keep, jnp.sum(spread * weights, axis=1, keepdims=True), -1.0)
            return (ids == target).astype(BF16)

        main = dot(chosen(main_at, is_main), r.table[:, 0:768])
        for j in range(3):
            rest = dot(chosen(rest_at[j], jnp.logical_not(is_main)), r.table[:, 768:1024])
            both = main[:, 256 * j:256 * j + 256] + rest
            r.rep_out[pl.ds(g * 8, 8), :, 256 * j:256 * j + 256] = both.astype(BF16).reshape(8, SLOTS, 256)

    def reply(k):
        dev = device_at((z + NZ - k % NZ) % NZ, (y + NY - k // (NZ * NC)) % NY, (c + NC - k // NZ % NC) % NC, x)
        remote(r.rep_out.at[k], r.rep_in.at[k], r.a_send, r.a_recv.at[k // 16], dev)

    def serve(g, carry):
        chunk(g)
        for n in (4, 3, 5, 2, 6, 1, 7, 0):
            reply(g * 8 + n)
        return carry

    across = {}

    def along_x(sec):
        wait_bytes(w.at[:, pl.ds(0, NY - 1), c, :, cols(sec, x)], r.y_recv.at[sec])
        part = w.at[:, :, c, :, cols(sec, x)]
        for n, k in enumerate((1, 3)):
            across[sec, n] = remote(part, part, r.x_send.at[sec, n], r.x_recv.at[sec, n], xs[k])
        remote(part, part, r.c_send.at[sec], r.c_recv.at[sec], partner)

    chunk(0)
    for n in (4, 3, 5, 2, 6, 1, 7):
        reply(n)
    lax.fori_loop(1, 3, serve, 0)
    along_x(0)
    lax.fori_loop(3, 5, serve, 0)
    along_x(1)
    lax.fori_loop(5, 8, serve, 0)
    along_x(2)
    r.rep_in[0] = r.rep_out[0]

    for sec in range(3):
        for n, k in enumerate((1, 3)):
            across[sec, n].wait_recv()
            at = cols(sec, (x - k + NX) % NX)
            half = w.at[pl.ds(4 * n, 4), :, c, :, at]
            across[sec, 2 + n] = remote(half, half, r.x_send.at[sec, 2 + n], r.x_recv.at[sec, 2 + n], xs[k])
            part = w.at[:, :, c, :, at]
            remote(part, part, r.c_send.at[sec], r.c_recv.at[sec], partner)
    def unpack(part):
        low = max(16 * part, 1)
        wait_bytes(r.rep_in.at[pl.ds(low, 16 * part + 16 - low)], r.a_recv.at[part])
        answers = r.rep_in[16 * part:16 * part + 16].reshape(256, 768)
        places = iota((count, 256), 1) + 256 * part
        base = rel * SLOTS
        main = dot((places == base + slot).astype(BF16), answers)
        rest = jnp.zeros((count, 256), F32)
        for j in range(3):
            place = jnp.where(slot // 4 == j, base + CAP + slot % 4, -1)
            rest = rest + dot((places == place).astype(BF16), answers[:, 256 * j:256 * j + 256])
        if part:
            main, rest = main + r.pre[:, 0:768], rest + r.pre[:, 768:1024]
        r.pre[:, 0:768] = main
        r.pre[:, 768:1024] = rest

    unpack(0)
    for sec in range(3):
        for n in range(2):
            across[sec, 2 + n].wait_recv()
            half = w.at[pl.ds(4 * n, 4), :, c, :, cols(sec, (x + 2) % NX)]
            remote(half, half, r.c_send.at[sec], r.c_recv.at[sec], partner)
    unpack(1)
    for sec in range(3):
        wait_bytes(w.at[:, :, c, :, pl.ds(sec * D, D)], r.c_recv.at[sec])
    loads[1].wait()

    def one(sec):
        return w[:, :, :, :, sec * D:sec * D + D].reshape(D, D)

    def two(sec):
        return r.l2[:, sec * D:sec * D + D]

    to_partner(hop_copies, r.hop8, r.h_send, r.h_recv)
    pre1_self = dot(r.hop[...], one(1))
    pre2_self = dot(r.tgt[...], two(1))
    hop_copies[3].wait_recv()
    r.ht[...] = dot_nt(line_pick("x", c, y, x), r.hop8[...].reshape(256, D)).astype(BF16)
    unpack(2)
    unpack(3)
    r.fetched[...] = r.pre[...].astype(BF16)
    swaps.append(remote(r.fetched, r.fetched_o, r.p_send.at[0], r.p_recv.at[0], partner))

    of_node = jnp.where(iota((count, PAD1), 0) // FAN == iota((count, PAD1), 1), weight2, 0).astype(F32).astype(BF16)
    total2 = jnp.maximum(dot_tn(of_node, jnp.ones((count, 128), BF16))[:, 0:1], 1.0)
    for n in range(4):
        at = slice(256 * n, 256 * n + 256)
        pre = dot(r.fetched[...], w[:, :, :, :, at].reshape(D, 256))
        sig = jax.nn.sigmoid(pre)
        high, low = split(pre * sig)
        r.pre[:, at] = sig * (1.0 + pre * (1.0 - sig))
        r.nbr1[:, at] = ((dot_tn(of_node, high) + dot_tn(of_node, low)) / total2).astype(BF16)
    r.nbr8[0, 0] = r.nbr1[...]
    nbr_copies = to_line(r.nbr8, r.n_send, r.n_recv, ys)
    pre1 = pre1_self + dot(r.nbr1[...], one(2))
    gated1 = act(pre1)
    scale1 = lax.rsqrt(jnp.mean(gated1 * gated1, axis=-1, keepdims=True) + EPS)
    norm1 = gated1 * scale1

    pre_hop1 = dot(norm1.astype(BF16), two(0))
    of_target = jnp.where(iota((PAD1, PADT), 0) // PER == iota((PAD1, PADT), 1), weight1, 0).astype(F32).astype(BF16)
    high, low = split(act(pre_hop1))
    numer = dot_tn(of_target, high) + dot_tn(of_target, low)
    weight = dot_tn(of_target, jnp.ones((PAD1, 128), BF16))
    r.msg[:, 0:D] = numer[0:4]
    r.msg[:, D:D + 128] = weight[0:4]
    sums = [remote(r.msg, r.msg_in.at[k - 1], r.m_send.at[k - 1], r.m_recv.at[k - 1], xs[k]) for k in (1, 2, 3)]
    to_partner(nbr_copies, r.nbr8, r.n_send, r.n_recv)
    swaps[0].wait_recv()
    for part, axis in enumerate("xy"):
        pick = row_pick(axis, c)
        r.xt[part, :, 0:count] = dot_nt(pick, r.fetched[...]).astype(BF16)
        r.xt[part, :, 512:512 + count] = dot_nt(pick, r.fetched_o[...]).astype(BF16)
    nbr_copies[3].wait_recv()
    r.nt[...] = dot_nt(line_pick("y", c, y, x), r.nbr8[...].reshape(256, D)).astype(BF16)
    for copy in sums:
        copy.wait_recv()
    r.summed[...] = jnp.zeros_like(r.summed)
    r.summed[0:4, :] = r.msg[...] + r.msg_in[0] + r.msg_in[1] + r.msg_in[2]
    summed = r.summed[...]
    total1 = jnp.maximum(summed[:, D:D + 1], 1.0)
    nbr2 = (summed[:, 0:D] / total1).astype(BF16)
    pre2 = pre2_self + dot(nbr2, two(2))
    gated2 = act(pre2)
    scale2 = lax.rsqrt(jnp.mean(gated2 * gated2, axis=-1, keepdims=True) + EPS)
    norm2 = gated2 * scale2
    r.emb[...] = norm2
    cot = r.cot[...]
    back2 = (scale2 * (cot - norm2 * jnp.mean(cot * norm2, axis=-1, keepdims=True)) * act_slope(pre2)).astype(BF16)
    back_nbr2 = dot_nt(back2, two(2))
    high, low = split(back_nbr2 / total1)
    back_hop1 = ((dot(of_target, high) + dot(of_target, low)) * act_slope(pre_hop1)).astype(BF16)
    back_h1 = dot_nt(back_hop1, two(0))
    back1 = (scale1 * (back_h1 - norm1 * jnp.mean(back_h1 * norm1, axis=-1, keepdims=True)) * act_slope(pre1)).astype(BF16)
    r.back1[...] = back1
    back_copies = []
    for n, devs in enumerate((xs, ys)):
        r.back8[n, 0, 0] = back1
        back_copies.append(to_line(r.back8.at[n], r.b_send.at[n], r.b_recv.at[n], devs))
    r.emb_out[...] = r.emb[pl.ds(x, 1), :]

    first, second, third, lines = {}, {}, {}, {}

    def start_first(k):
        for part in range(2):
            at = pl.ds(pl.multiple_of(lax.rem((x if part == 0 else y) + k, 4) * 128, 128), 128)
            v = r.mine[part, at, :] + dot(r.xt[part, at, 512:512 + count], r.bf_o[part])
            if k == 0:
                r.acc1[part] = v
            else:
                r.send1[part, k - 1] = v.astype(BF16)
                first[part, k] = remote(
                    r.send1.at[part, k - 1], r.recv1.at[part, k - 1], r.s1.at[part, k - 1], r.r1.at[part, k - 1],
                    (xs, ys)[part][k])

    def start_second():
        for part in range(2):
            for k in (1, 3, 2):
                first[part, k].wait_recv()
            r.acc1[part] = (
                r.acc1[part] + r.recv1[part, 0].astype(F32) + r.recv1[part, 1].astype(F32) + r.recv1[part, 2].astype(F32))
            for k in (2, 1, 3):
                at = lax.rem((y if part == 0 else x) + k, 4)
                r.send2[part, k - 1] = r.acc1[part, pl.ds(pl.multiple_of(at * 32, 32), 32), :].astype(BF16)
                second[part, k] = remote(
                    r.send2.at[part, k - 1], r.recv2.at[part, k - 1], r.s2.at[part, k - 1], r.r2.at[part, k - 1],
                    (ys, xs)[part][k])

    def start_line(n, rows):
        back_copies[n][3].wait_recv()
        r.line[n] = dot(rows, r.back8[n].reshape(256, D))
        for k in (2, 1, 3):
            at = lax.rem((y if n == 0 else x) + k, 4)
            r.send_l[n, k - 1] = r.line[n, pl.ds(pl.multiple_of(at * 32, 32), 32), :].astype(BF16)
            lines[n, k] = remote(
                r.send_l.at[n, k - 1], r.recv_l.at[n, k - 1], r.sl.at[n, k - 1], r.rl.at[n, k - 1], (ys, xs)[n][k])

    def start_third(sec):
        r.send3[sec] = r.pk[sec].astype(BF16)
        for k in (4, 3, 5, 2, 6, 1, 7):
            third[sec, k] = remote(
                r.send3.at[sec, lax.rem(z + k, NZ)], r.recv3.at[sec, k - 1], r.s3.at[sec, k - 1], r.r3.at[sec, k - 1], zs[k])

    def third_of_line(n):
        for k in (1, 3, 2):
            lines[n, k].wait_recv()
        own = pl.ds(pl.multiple_of((y if n == 0 else x) * 32, 32), 32)
        r.accl[...] = (
            r.line[n, own, :] + r.recv_l[n, 0].astype(F32) + r.recv_l[n, 1].astype(F32) + r.recv_l[n, 2].astype(F32))
        for zz in range(NZ):
            for q in range(4):
                r.pk[n + 1, zz, 4 * q:4 * q + 4, :] = r.accl[4 * zz:4 * zz + 4, 256 * q:256 * q + 256]
        start_third(n + 1)

    def third_of_fetch():
        for part in range(2):
            for k in (1, 3, 2):
                second[part, k].wait_recv()
            at = y if part == 0 else x
            r.acc2[part] = (
                r.acc1[part, pl.ds(pl.multiple_of(at * 32, 32), 32), :] + r.recv2[part, 0].astype(F32)
                + r.recv2[part, 1].astype(F32) + r.recv2[part, 2].astype(F32))
            for zz in range(NZ):
                for h in range(2):
                    q = 2 * part + h
                    r.pk[0, zz, 4 * q:4 * q + 4, :] = r.acc2[part, 4 * zz:4 * zz + 4, 256 * h:256 * h + 256]
        start_third(0)

    def finish(sec):
        value = r.pk[sec, z]
        for k in (1, 7, 2, 6, 3, 5, 4):
            third[sec, k].wait_recv()
            value = value + r.recv3[sec, k - 1].astype(F32)
        r.pk[sec, 0] = value
        for q in range(4):
            r.grads_out[:, sec * D + 256 * q:sec * D + 256 * q + 256] = r.pk[sec, 0, 4 * q:4 * q + 4, :]

    back_nbr1 = dot_nt(r.back1[...], one(2)) / total2
    of_node = jnp.concatenate([of_node, of_node], axis=1)
    terms = jnp.concatenate(split(back_nbr1), axis=0)
    for part in range(2):
        at = slice(512 * part, 512 * part + 512)
        r.bf[part] = (dot(of_node, terms[:, at]) * r.pre[:, at]).astype(BF16)
        swaps.append(remote(r.bf.at[part], r.bf_o.at[part], r.p_send.at[1 + part], r.p_recv.at[1 + part], partner))
    for part in range(2):
        r.mine[part] = dot(r.xt[part, :, 0:count], r.bf[part])
    swaps[1].wait_recv()
    swaps[2].wait_recv()
    start_first(2)
    for n in range(2):
        to_partner(back_copies[n], r.back8.at[n], r.b_send.at[n], r.b_recv.at[n])
    start_first(1)
    start_first(3)
    start_line(0, r.ht[...])
    start_line(1, r.nt[...])
    start_first(0)
    start_second()
    third_of_line(0)
    third_of_line(1)
    third_of_fetch()
    finish(1)
    finish(2)
    finish(0)

    wait_bytes(r.reqs.at[pl.ds(1, N_FEAT - 1)], r.q_send)
    wait_bytes(r.rep_out.at[pl.ds(1, N_FEAT - 1)], r.a_send)
    for sec in range(3):
        wait_bytes(w.at[pl.ds(0, NZ - 1), y, c, :, cols(sec, x)], r.z_send.at[sec])
        wait_bytes(w.at[:, pl.ds(0, NY - 1), c, :, cols(sec, x)], r.y_send.at[sec])
        wait_bytes(w.at[:, :, c, :, pl.ds(sec * D, D)], r.c_send.at[sec])
    for copy in list(across.values()) + swaps + sums + hop_copies + nbr_copies + back_copies[0] + back_copies[1]:
        copy.wait_send()
    for copy in list(first.values()) + list(second.values()) + list(lines.values()) + list(third.values()):
        copy.wait_send()


def on_device(
    table, hop2_owner, hop2_row, hop2_weight, hop1_feats, hop1_weight, target_feats, cotangent, layer_one, layer_two,
):
    vmem, anywhere = pl.BlockSpec(memory_space=pltpu.VMEM), pl.BlockSpec(memory_space=pl.ANY)
    emb, grads = pl.pallas_call(
        step_kernel,
        out_shape=(jax.ShapeDtypeStruct((1, D), F32), jax.ShapeDtypeStruct((4, 3 * D), F32)),
        in_specs=[anywhere, anywhere, anywhere, anywhere, anywhere, vmem, vmem, vmem, anywhere, anywhere],
        out_specs=(vmem, vmem),
        scratch_shapes=[pltpu.VMEM(s, t) for _, s, t in SCRATCH] + [pltpu.SemaphoreType.DMA(s) for _, s in SEMS],
        compiler_params=pltpu.CompilerParams(collective_id=1, has_side_effects=True, vmem_limit_bytes=VM * 1024 * 1024),
        name="step",
    )(
        hop2_owner.reshape(1, ROWS2), hop2_row.reshape(1, ROWS2), hop2_weight.reshape(1, ROWS2), hop1_weight.reshape(1, ROWS1), table, hop1_feats, target_feats, cotangent, layer_one, layer_two)

    def hand_over(emb_ref, grads_ref, emb_out, grads_out):
        emb_out[...] = emb_ref[...].astype(BF16)
        grads_out[...] = grads_ref[...]

    return pl.pallas_call(
        hand_over,
        out_shape=(jax.ShapeDtypeStruct((1, D), BF16), jax.ShapeDtypeStruct((4, 3 * D), F32)),
        in_specs=[vmem, vmem],
        out_specs=(vmem, vmem),
        name="hand_over",
    )(emb, grads)


def solution(mesh):
    both = P(("feat", "sect"), None)
    flat = P(("feat", "sect"))
    feat = P("feat", None)
    return jax.shard_map(
        on_device,
        mesh=mesh,
        in_specs=(feat, both, flat, flat, both, flat, feat, feat, feat, P()),
        out_specs=(both, both),
        check_vma=False,
    )
```

```python
import types

import jax
import jax.numpy as jnp
from jax import lax
from jax.experimental import pallas as pl
from jax.experimental.pallas import tpu as pltpu
from jax.sharding import PartitionSpec as P

MESH = pl.DeviceIdType.MESH
EPS = 1e-05
NZ, NY, NC, NX = 8, 4, 2, 4
N_FEAT = NZ * NY * NC
CAP, SLOTS = 12, 16
VM = 54
D = 1024
ROWS2, ROWS1, FAN, PER = 400, 20, 20, 5
PAD1, PADT = 32, 16
F32, BF16 = jnp.float32, jnp.bfloat16


def act(values):
    return values * jax.nn.sigmoid(values)


def act_slope(values):
    sig = jax.nn.sigmoid(values)
    return sig * (1.0 + values * (1.0 - sig))


def dot(a, b):
    return lax.dot_general(a, b, (((1,), (0,)), ((), ())), preferred_element_type=F32)


def dot_nt(a, b):
    return lax.dot_general(a, b, (((1,), (1,)), ((), ())), preferred_element_type=F32)


def dot_tn(a, b):
    return lax.dot_general(a, b, (((0,), (0,)), ((), ())), preferred_element_type=F32)


def split(values):
    high = values.astype(BF16)
    return high, (values - high.astype(F32)).astype(BF16)


def iota(shape, dim):
    return lax.broadcasted_iota(jnp.int32, shape, dim)


def coords():
    feat = lax.axis_index("feat")
    return feat // (NY * NC), (feat // NC) % NY, feat % NC, lax.axis_index("sect")


def device_at(z, y, c, x):
    return ((z * NY + y) * NC + c, x)


def remote(src, dst, send, recv, dev):
    copy = pltpu.make_async_remote_copy(
        src_ref=src, dst_ref=dst, send_sem=send, recv_sem=recv, device_id=dev, device_id_type=MESH)
    copy.start()
    return copy


def wait_bytes(ref, sem):
    pltpu.make_async_copy(ref, ref, sem).wait()


def row_pick(first, parity):
    m, lane = iota((D // 2, D), 0), iota((D // 2, D), 1)
    a, b, z, i = m // 128, (m // 32) % 4, (m // 4) % 8, m % 4
    y, x = (b, a) if first == "x" else (a, b)
    return (lane == z * 128 + y * 32 + parity * 16 + x * 4 + i).astype(BF16)


def line_pick(axis, c, y, x):
    m, lane = iota((128, D), 0), iota((128, D), 1)
    b, z, i = m // 32, (m // 4) % 8, m % 4
    y, x = (b, x) if axis == "x" else (y, b)
    return (lane == z * 128 + y * 32 + c * 16 + x * 4 + i).astype(BF16)


SCRATCH = [
    ("w", (NZ, NY, NC, 16, 3 * D), BF16), ("l2", (D, 3 * D), BF16), ("table", (512, D), BF16),
    ("owner", (1, ROWS2), jnp.int32), ("row", (1, ROWS2), jnp.int32), ("weight2", (1, ROWS2), jnp.int32),
    ("weight1", (1, ROWS1), jnp.int32), ("rows", (16, ROWS2), F32), ("reqs", (N_FEAT, 1, 128), F32), ("rin", (N_FEAT, 1, 128), F32),
    ("rep_out", (N_FEAT, SLOTS, 768), BF16), ("rep_in", (N_FEAT, SLOTS, 768), BF16),
    ("hop", (PAD1, D), BF16), ("nbr1", (PAD1, D), BF16), ("back1", (PAD1, D), BF16),
    ("hop8", (2, 4, PAD1, D), BF16), ("nbr8", (2, 4, PAD1, D), BF16), ("back8", (2, 2, 4, PAD1, D), BF16),
    ("tgt", (PADT, D), BF16), ("cot", (PADT, D), F32),
    ("fetched", (ROWS2, D), BF16), ("fetched_o", (ROWS2, D), BF16),
    ("bf", (2, ROWS2, 512), BF16), ("bf_o", (2, ROWS2, 512), BF16), ("mine", (2, 512, 512), F32), ("pre", (ROWS2, D), F32),
    ("vt", (D, D), BF16), ("qt", (D, D), BF16), ("pick", (2, 512, D), BF16), ("xt", (2, 512, 1024), BF16), ("ht", (128, 256), BF16), ("nt", (128, 256), BF16),
    ("msg", (4, D + 128), F32), ("msg_in", (NX - 1, 4, D + 128), F32),
    ("emb", (PADT, D), F32), ("summed", (PADT, D + 128), F32),
    ("send1", (2, 3, 128, 512), BF16), ("recv1", (2, 3, 128, 512), BF16), ("acc1", (2, 128, 512), F32),
    ("send2", (2, 3, 32, 512), BF16), ("recv2", (2, 3, 32, 512), BF16),
    ("line", (2, 128, D), F32), ("send_l", (2, 3, 32, D), BF16), ("recv_l", (2, 3, 32, D), BF16),
    ("acc2", (2, 32, 512), F32), ("accl", (32, D), F32), ("pk", (3, NZ, 16, 256), F32), ("send3", (3, NZ, 16, 256), BF16),
    ("recv3", (3, NZ - 1, 16, 256), BF16),
]
SEMS = [
    ("load", (2,)), ("index", (4,)), ("own", (3,)), ("q_send", ()), ("q_recv", ()), ("a_send", ()), ("a_recv", (4,)),
    ("z_send", (3,)), ("z_recv", (3,)), ("y_send", (3,)), ("y_recv", (3,)),
    ("x_send", (3, 4)), ("x_recv", (3, 4)), ("c_send", (3,)), ("c_recv", (3,)),
    ("p_send", (3,)), ("p_recv", (3,)), ("m_send", (3,)), ("m_recv", (3,)),
    ("s1", (2, 3)), ("r1", (2, 3)), ("s2", (2, 3)), ("r2", (2, 3)), ("sl", (2, 3)), ("rl", (2, 3)),
    ("h_send", (4,)), ("h_recv", (4,)), ("n_send", (4,)), ("n_recv", (4,)), ("b_send", (2, 4)), ("b_recv", (2, 4)), ("s3", (3, 7)), ("r3", (3, 7)),
]
INPUTS = ["owner_in", "row_in", "weight2_in", "weight1_in", "table_in", "hop_in", "tgt_in", "cot_in", "l1", "l2_in"]
OUTPUTS = ["emb_out", "grads_out"]


def step_kernel(*refs):
    names = INPUTS + OUTPUTS + [s[0] for s in SCRATCH] + [s[0] for s in SEMS]
    r = types.SimpleNamespace(**dict(zip(names, refs)))
    z, y, c, x = coords()
    me = lax.axis_index("feat")
    partner = device_at(z, y, 1 - c, x)
    xs = [device_at(z, y, c, (x + k) % NX) for k in range(NX)]
    ys = [device_at(z, (y + k) % NY, c, x) for k in range(NY)]
    zs = [device_at((z + k) % NZ, y, c, x) for k in range(NZ)]
    w = r.w

    numbers = [
        pltpu.make_async_copy(src, dst, r.index.at[n]) for n, (src, dst) in enumerate([
            (r.owner_in, r.owner), (r.row_in, r.row), (r.weight2_in, r.weight2), (r.weight1_in, r.weight1)])]
    for copy in numbers:
        copy.start()

    barrier = pltpu.get_barrier_semaphore()

    def greet(k, carry):
        pl.semaphore_signal(barrier, inc=1, device_id=((me + k) % N_FEAT, x), device_id_type=MESH)
        return carry

    lax.fori_loop(1, N_FEAT, greet, 0)
    for dev in xs[1:]:
        pl.semaphore_signal(barrier, inc=1, device_id=dev, device_id_type=MESH)

    def cols(sec, at):
        return pl.ds(pl.multiple_of(sec * D + at * 256, 256), 256)

    loads = [pltpu.make_async_copy(r.table_in, r.table, r.load.at[0]), pltpu.make_async_copy(r.l2_in, r.l2, r.load.at[1])]
    for copy in loads:
        copy.start()
    owns = [pltpu.make_async_copy(r.l1.at[:, cols(sec, x)], w.at[z, y, c, :, cols(sec, x)], r.own.at[sec]) for sec in range(3)]
    for copy in owns:
        copy.start()

    count = ROWS2
    r.rows[...] = jnp.zeros_like(r.rows)
    for copy in numbers:
        copy.wait()
    r.rows[0:1, :] = r.owner[...].astype(F32)
    r.rows[1:2, :] = (r.row[...] // 32).astype(F32)
    r.rows[2:3, :] = (r.row[...] % 32).astype(F32)
    r.rows[3:4, :] = r.weight2[...].astype(F32)
    r.rows[4:5, 0:ROWS1] = r.weight1[...].astype(F32)
    eye = (iota((16, 128), 0) == iota((16, 128), 1)).astype(BF16)
    columns = dot_tn(r.rows[...].astype(BF16), eye).astype(jnp.int32)
    weight2, weight1 = columns[:, 3:4], columns[0:PAD1, 4:5]
    owner = columns[:, 0:1]
    rel = ((owner // NC + NY - y) % NY * NC + (owner + NC - c) % NC) * NZ + (owner // (NY * NC) + NZ - z) % NZ
    member = (iota((count, N_FEAT), 1) == rel).astype(BF16)
    before = (iota((count, count), 0) > iota((count, count), 1)).astype(BF16)
    slot = jnp.sum(dot(before, member) * member.astype(F32), axis=1, keepdims=True).astype(jnp.int32)
    lane = iota((count, 128), 1)
    asked = jnp.where(lane == slot, columns[:, 1:2], 0) + jnp.where(lane == slot + SLOTS, columns[:, 2:3], 0)
    r.reqs[...] = dot_tn(member, asked.astype(F32).astype(BF16)).reshape(N_FEAT, 1, 128)
    r.rin[0] = r.reqs[0]

    pl.semaphore_wait(barrier, N_FEAT - 1 + NX - 1)

    def ask(k, carry):
        dev = device_at((z + k) % NZ, (y + k // (NZ * NC)) % NY, (c + k // NZ) % NC, x)
        remote(r.reqs.at[k], r.rin.at[k], r.q_send, r.q_recv, dev)
        return carry

    lax.fori_loop(1, N_FEAT, ask, 0)
    for sec in range(3):
        for k in (4, 3, 5, 2, 6, 1, 7):
            remote(r.l1.at[:, cols(sec, x)], w.at[z, y, c, :, cols(sec, x)], r.z_send.at[sec], r.z_recv.at[sec], zs[k])

    r.hop[...] = jnp.zeros_like(r.hop)
    r.hop[0:ROWS1, :] = r.hop_in[...]
    r.tgt[...] = jnp.zeros_like(r.tgt)
    r.tgt[0:4, :] = r.tgt_in[...]
    r.cot[...] = jnp.zeros_like(r.cot)
    r.cot[0:4, :] = r.cot_in[...].astype(F32)

    def to_line(buf, send, recv, devs):
        return [remote(buf.at[0, 0], buf.at[0, k], send.at[k - 1], recv.at[k - 1], devs[k]) for k in (2, 1, 3)]

    def to_partner(copies, buf, send, recv):
        for copy in copies:
            copy.wait_recv()
        copies.append(remote(buf.at[0], buf.at[1], send.at[3], recv.at[3], partner))

    r.hop8[0, 0] = r.hop[...]
    hop_copies = to_line(r.hop8, r.h_send, r.h_recv, xs)
    swaps = []

    for sec in range(3):
        wait_bytes(w.at[pl.ds(0, NZ - 1), y, c, :, cols(sec, x)], r.z_recv.at[sec])
        owns[sec].wait()
        for k in (2, 1, 3):
            part = w.at[:, y, c, :, cols(sec, x)]
            remote(part, part, r.y_send.at[sec], r.y_recv.at[sec], ys[k])

    loads[0].wait()
    wait_bytes(r.rin.at[pl.ds(1, N_FEAT - 1)], r.q_recv)
    wanted = r.rin[...].reshape(N_FEAT, 128).astype(BF16)
    wide = 8 * SLOTS
    at_row, at_lane = iota((wide, 128), 0) % SLOTS, iota((wide, 128), 1)

    def pick_weights(slots):
        return (32 * (at_lane == slots).astype(jnp.int32) + (at_lane == slots + SLOTS).astype(jnp.int32)).astype(F32)

    main_at = pick_weights(at_row)
    rest_at = [pick_weights(4 * j + at_row - CAP) for j in range(3)]
    is_main = iota((wide, 1), 0) % SLOTS < CAP

    def chunk(g):
        group = (iota((wide, N_FEAT), 1) == g * 8 + iota((wide, N_FEAT), 0) // SLOTS).astype(BF16)
        spread = dot(group, wanted)
        ids = iota((wide, 512), 1).astype(F32)

        def chosen(weights, keep):
            target = jnp.where(keep, jnp.sum(spread * weights, axis=1, keepdims=True), -1.0)
            return (ids == target).astype(BF16)

        main = dot(chosen(main_at, is_main), r.table[:, 0:768])
        for j in range(3):
            rest = dot(chosen(rest_at[j], jnp.logical_not(is_main)), r.table[:, 768:1024])
            both = main[:, 256 * j:256 * j + 256] + rest
            r.rep_out[pl.ds(g * 8, 8), :, 256 * j:256 * j + 256] = both.astype(BF16).reshape(8, SLOTS, 256)

    def reply(k):
        dev = device_at((z + NZ - k % NZ) % NZ, (y + NY - k // (NZ * NC)) % NY, (c + NC - k // NZ % NC) % NC, x)
        remote(r.rep_out.at[k], r.rep_in.at[k], r.a_send, r.a_recv.at[k // 16], dev)

    def serve(g, carry):
        chunk(g)
        for n in (4, 3, 5, 2, 6, 1, 7, 0):
            reply(g * 8 + n)
        return carry

    across = {}

    def along_x(sec):
        wait_bytes(w.at[:, pl.ds(0, NY - 1), c, :, cols(sec, x)], r.y_recv.at[sec])
        part = w.at[:, :, c, :, cols(sec, x)]
        for n, k in enumerate((1, 3)):
            across[sec, n] = remote(part, part, r.x_send.at[sec, n], r.x_recv.at[sec, n], xs[k])
        remote(part, part, r.c_send.at[sec], r.c_recv.at[sec], partner)

    chunk(0)
    for n in (4, 3, 5, 2, 6, 1, 7):
        reply(n)
    lax.fori_loop(1, 3, serve, 0)
    along_x(0)
    lax.fori_loop(3, 5, serve, 0)
    along_x(1)
    lax.fori_loop(5, 8, serve, 0)
    along_x(2)
    r.rep_in[0] = r.rep_out[0]
    r.pick[0] = row_pick("x", c)
    r.pick[1] = row_pick("y", c)
    loads[1].wait()
    r.vt[...] = r.l2[:, 2 * D:3 * D].T
    r.qt[...] = r.l2[:, 0:D].T

    for sec in range(3):
        for n, k in enumerate((1, 3)):
            across[sec, n].wait_recv()
            at = cols(sec, (x - k + NX) % NX)
            half = w.at[pl.ds(4 * n, 4), :, c, :, at]
            across[sec, 2 + n] = remote(half, half, r.x_send.at[sec, 2 + n], r.x_recv.at[sec, 2 + n], xs[k])
            part = w.at[:, :, c, :, at]
            remote(part, part, r.c_send.at[sec], r.c_recv.at[sec], partner)
    def unpack(part):
        low = max(16 * part, 1)
        wait_bytes(r.rep_in.at[pl.ds(low, 16 * part + 16 - low)], r.a_recv.at[part])
        answers = r.rep_in[16 * part:16 * part + 16].reshape(256, 768)
        places = iota((count, 256), 1) + 256 * part
        base = rel * SLOTS
        main = dot((places == base + slot).astype(BF16), answers)
        rest = jnp.zeros((count, 256), F32)
        for j in range(3):
            place = jnp.where(slot // 4 == j, base + CAP + slot % 4, -1)
            rest = rest + dot((places == place).astype(BF16), answers[:, 256 * j:256 * j + 256])
        if part:
            main, rest = main + r.pre[:, 0:768], rest + r.pre[:, 768:1024]
        r.pre[:, 0:768] = main
        r.pre[:, 768:1024] = rest

    unpack(0)
    for sec in range(3):
        for n in range(2):
            across[sec, 2 + n].wait_recv()
            half = w.at[pl.ds(4 * n, 4), :, c, :, cols(sec, (x + 2) % NX)]
            remote(half, half, r.c_send.at[sec], r.c_recv.at[sec], partner)
    unpack(1)
    for sec in range(3):
        wait_bytes(w.at[:, :, c, :, pl.ds(sec * D, D)], r.c_recv.at[sec])

    def one(sec):
        return w[:, :, :, :, sec * D:sec * D + D].reshape(D, D)

    def two(sec):
        return r.l2[:, sec * D:sec * D + D]

    to_partner(hop_copies, r.hop8, r.h_send, r.h_recv)
    pre1_self = dot(r.hop[...], one(1))
    pre2_self = dot(r.tgt[...], two(1))
    hop_copies[3].wait_recv()
    r.ht[...] = dot_nt(line_pick("x", c, y, x), r.hop8[...].reshape(256, D)).astype(BF16)
    unpack(2)
    unpack(3)
    r.fetched[...] = r.pre[...].astype(BF16)
    swaps.append(remote(r.fetched, r.fetched_o, r.p_send.at[0], r.p_recv.at[0], partner))

    of_node = jnp.where(iota((count, PAD1), 0) // FAN == iota((count, PAD1), 1), weight2, 0).astype(F32).astype(BF16)
    total2 = jnp.maximum(dot_tn(of_node, jnp.ones((count, 128), BF16))[:, 0:1], 1.0)
    for n in range(4):
        at = slice(256 * n, 256 * n + 256)
        pre = dot(r.fetched[...], w[:, :, :, :, at].reshape(D, 256))
        sig = jax.nn.sigmoid(pre)
        high, low = split(pre * sig)
        r.pre[:, at] = sig * (1.0 + pre * (1.0 - sig))
        r.nbr1[:, at] = ((dot_tn(of_node, high) + dot_tn(of_node, low)) / total2).astype(BF16)
    r.nbr8[0, 0] = r.nbr1[...]
    nbr_copies = to_line(r.nbr8, r.n_send, r.n_recv, ys)
    pre1 = pre1_self + dot(r.nbr1[...], one(2))
    gated1 = act(pre1)
    scale1 = lax.rsqrt(jnp.mean(gated1 * gated1, axis=-1, keepdims=True) + EPS)
    norm1 = gated1 * scale1

    pre_hop1 = dot(norm1.astype(BF16), two(0))
    of_target = jnp.where(iota((PAD1, PADT), 0) // PER == iota((PAD1, PADT), 1), weight1, 0).astype(F32).astype(BF16)
    high, low = split(act(pre_hop1))
    numer = dot_tn(of_target, high) + dot_tn(of_target, low)
    weight = dot_tn(of_target, jnp.ones((PAD1, 128), BF16))
    r.msg[:, 0:D] = numer[0:4]
    r.msg[:, D:D + 128] = weight[0:4]
    sums = [remote(r.msg, r.msg_in.at[k - 1], r.m_send.at[k - 1], r.m_recv.at[k - 1], xs[k]) for k in (1, 2, 3)]
    slope_hop1 = act_slope(pre_hop1)
    slope1 = act_slope(pre1)
    swaps[0].wait_recv()
    for part in range(2):
        r.xt[part, :, 0:count] = dot_nt(r.pick[part], r.fetched[...]).astype(BF16)
        r.xt[part, :, 512:512 + count] = dot_nt(r.pick[part], r.fetched_o[...]).astype(BF16)
    for copy in sums:
        copy.wait_recv()
    r.summed[...] = jnp.zeros_like(r.summed)
    r.summed[0:4, :] = r.msg[...] + r.msg_in[0] + r.msg_in[1] + r.msg_in[2]
    summed = r.summed[...]
    total1 = jnp.maximum(summed[:, D:D + 1], 1.0)
    nbr2 = (summed[:, 0:D] / total1).astype(BF16)
    pre2 = pre2_self + dot(nbr2, two(2))
    gated2 = act(pre2)
    scale2 = lax.rsqrt(jnp.mean(gated2 * gated2, axis=-1, keepdims=True) + EPS)
    norm2 = gated2 * scale2
    r.emb[...] = norm2
    cot = r.cot[...]
    back2 = (scale2 * (cot - norm2 * jnp.mean(cot * norm2, axis=-1, keepdims=True)) * act_slope(pre2)).astype(BF16)
    back_nbr2 = dot(back2, r.vt[...])
    high, low = split(back_nbr2 / total1)
    back_hop1 = ((dot(of_target, high) + dot(of_target, low)) * slope_hop1).astype(BF16)
    back_h1 = dot(back_hop1, r.qt[...])
    back1 = (scale1 * (back_h1 - norm1 * jnp.mean(back_h1 * norm1, axis=-1, keepdims=True)) * slope1).astype(BF16)
    r.back1[...] = back1
    back_copies = []
    for n, devs in enumerate((xs, ys)):
        r.back8[n, 0, 0] = back1
        back_copies.append(to_line(r.back8.at[n], r.b_send.at[n], r.b_recv.at[n], devs))

    first, second, third, lines = {}, {}, {}, {}

    def start_first(k):
        for part in range(2):
            at = pl.ds(pl.multiple_of(lax.rem((x if part == 0 else y) + k, 4) * 128, 128), 128)
            v = r.mine[part, at, :] + dot(r.xt[part, at, 512:512 + count], r.bf_o[part])
            if k == 0:
                r.acc1[part] = v
            else:
                r.send1[part, k - 1] = v.astype(BF16)
                first[part, k] = remote(
                    r.send1.at[part, k - 1], r.recv1.at[part, k - 1], r.s1.at[part, k - 1], r.r1.at[part, k - 1],
                    (xs, ys)[part][k])

    def start_second():
        for part in range(2):
            for k in (1, 3, 2):
                first[part, k].wait_recv()
            r.acc1[part] = (
                r.acc1[part] + r.recv1[part, 0].astype(F32) + r.recv1[part, 1].astype(F32) + r.recv1[part, 2].astype(F32))
            for k in (2, 1, 3):
                at = lax.rem((y if part == 0 else x) + k, 4)
                r.send2[part, k - 1] = r.acc1[part, pl.ds(pl.multiple_of(at * 32, 32), 32), :].astype(BF16)
                second[part, k] = remote(
                    r.send2.at[part, k - 1], r.recv2.at[part, k - 1], r.s2.at[part, k - 1], r.r2.at[part, k - 1],
                    (ys, xs)[part][k])

    def start_line(n, rows):
        back_copies[n][3].wait_recv()
        r.line[n] = dot(rows, r.back8[n].reshape(256, D))
        for k in (2, 1, 3):
            at = lax.rem((y if n == 0 else x) + k, 4)
            r.send_l[n, k - 1] = r.line[n, pl.ds(pl.multiple_of(at * 32, 32), 32), :].astype(BF16)
            lines[n, k] = remote(
                r.send_l.at[n, k - 1], r.recv_l.at[n, k - 1], r.sl.at[n, k - 1], r.rl.at[n, k - 1], (ys, xs)[n][k])

    def start_third(sec):
        r.send3[sec] = r.pk[sec].astype(BF16)
        for k in (4, 3, 5, 2, 6, 1, 7):
            third[sec, k] = remote(
                r.send3.at[sec, lax.rem(z + k, NZ)], r.recv3.at[sec, k - 1], r.s3.at[sec, k - 1], r.r3.at[sec, k - 1], zs[k])

    def third_of_line(n):
        for k in (1, 3, 2):
            lines[n, k].wait_recv()
        own = pl.ds(pl.multiple_of((y if n == 0 else x) * 32, 32), 32)
        r.accl[...] = (
            r.line[n, own, :] + r.recv_l[n, 0].astype(F32) + r.recv_l[n, 1].astype(F32) + r.recv_l[n, 2].astype(F32))
        for zz in range(NZ):
            for q in range(4):
                r.pk[n + 1, zz, 4 * q:4 * q + 4, :] = r.accl[4 * zz:4 * zz + 4, 256 * q:256 * q + 256]
        start_third(n + 1)

    def third_of_fetch():
        for part in range(2):
            for k in (1, 3, 2):
                second[part, k].wait_recv()
            at = y if part == 0 else x
            r.acc2[part] = (
                r.acc1[part, pl.ds(pl.multiple_of(at * 32, 32), 32), :] + r.recv2[part, 0].astype(F32)
                + r.recv2[part, 1].astype(F32) + r.recv2[part, 2].astype(F32))
            for zz in range(NZ):
                for h in range(2):
                    q = 2 * part + h
                    r.pk[0, zz, 4 * q:4 * q + 4, :] = r.acc2[part, 4 * zz:4 * zz + 4, 256 * h:256 * h + 256]
        start_third(0)

    def finish(sec):
        value = r.pk[sec, z]
        for k in (1, 7, 2, 6, 3, 5, 4):
            third[sec, k].wait_recv()
            value = value + r.recv3[sec, k - 1].astype(F32)
        r.pk[sec, 0] = value
        for q in range(4):
            r.grads_out[:, sec * D + 256 * q:sec * D + 256 * q + 256] = r.pk[sec, 0, 4 * q:4 * q + 4, :]

    back_nbr1 = dot_nt(r.back1[...], one(2)) / total2
    of_node = jnp.concatenate([of_node, of_node], axis=1)
    terms = jnp.concatenate(split(back_nbr1), axis=0)
    for part in range(2):
        at = slice(512 * part, 512 * part + 512)
        r.bf[part] = (dot(of_node, terms[:, at]) * r.pre[:, at]).astype(BF16)
        swaps.append(remote(r.bf.at[part], r.bf_o.at[part], r.p_send.at[1 + part], r.p_recv.at[1 + part], partner))
    to_partner(nbr_copies, r.nbr8, r.n_send, r.n_recv)
    for part in range(2):
        r.mine[part] = dot(r.xt[part, :, 0:count], r.bf[part])
    swaps[1].wait_recv()
    swaps[2].wait_recv()
    start_first(2)
    r.emb_out[...] = r.emb[pl.ds(x, 1), :]
    for n in range(2):
        to_partner(back_copies[n], r.back8.at[n], r.b_send.at[n], r.b_recv.at[n])
    start_first(1)
    start_first(3)
    start_line(0, r.ht[...])
    nbr_copies[3].wait_recv()
    r.nt[...] = dot_nt(line_pick("y", c, y, x), r.nbr8[...].reshape(256, D)).astype(BF16)
    start_line(1, r.nt[...])
    start_first(0)
    start_second()
    third_of_line(0)
    third_of_line(1)
    third_of_fetch()
    finish(1)
    finish(2)
    finish(0)

    wait_bytes(r.reqs.at[pl.ds(1, N_FEAT - 1)], r.q_send)
    wait_bytes(r.rep_out.at[pl.ds(1, N_FEAT - 1)], r.a_send)
    for sec in range(3):
        wait_bytes(w.at[pl.ds(0, NZ - 1), y, c, :, cols(sec, x)], r.z_send.at[sec])
        wait_bytes(w.at[:, pl.ds(0, NY - 1), c, :, cols(sec, x)], r.y_send.at[sec])
        wait_bytes(w.at[:, :, c, :, pl.ds(sec * D, D)], r.c_send.at[sec])
    for copy in list(across.values()) + swaps + sums + hop_copies + nbr_copies + back_copies[0] + back_copies[1]:
        copy.wait_send()
    for copy in list(first.values()) + list(second.values()) + list(lines.values()) + list(third.values()):
        copy.wait_send()


def on_device(
    table, hop2_owner, hop2_row, hop2_weight, hop1_feats, hop1_weight, target_feats, cotangent, layer_one, layer_two,
):
    vmem, anywhere = pl.BlockSpec(memory_space=pltpu.VMEM), pl.BlockSpec(memory_space=pl.ANY)
    emb, grads = pl.pallas_call(
        step_kernel,
        out_shape=(jax.ShapeDtypeStruct((1, D), F32), jax.ShapeDtypeStruct((4, 3 * D), F32)),
        in_specs=[anywhere, anywhere, anywhere, anywhere, anywhere, vmem, vmem, vmem, anywhere, anywhere],
        out_specs=(vmem, vmem),
        scratch_shapes=[pltpu.VMEM(s, t) for _, s, t in SCRATCH] + [pltpu.SemaphoreType.DMA(s) for _, s in SEMS],
        compiler_params=pltpu.CompilerParams(collective_id=1, has_side_effects=True, vmem_limit_bytes=VM * 1024 * 1024),
        name="step",
    )(
        hop2_owner.reshape(1, ROWS2), hop2_row.reshape(1, ROWS2), hop2_weight.reshape(1, ROWS2), hop1_weight.reshape(1, ROWS1), table, hop1_feats, target_feats, cotangent, layer_one, layer_two)

    def hand_over(emb_ref, grads_ref, emb_out, grads_out):
        emb_out[...] = emb_ref[...].astype(BF16)
        grads_out[...] = grads_ref[...]

    return pl.pallas_call(
        hand_over,
        out_shape=(jax.ShapeDtypeStruct((1, D), BF16), jax.ShapeDtypeStruct((4, 3 * D), F32)),
        in_specs=[vmem, vmem],
        out_specs=(vmem, vmem),
        name="hand_over",
    )(emb, grads)


def solution(mesh):
    both = P(("feat", "sect"), None)
    flat = P(("feat", "sect"))
    feat = P("feat", None)
    return jax.shard_map(
        on_device,
        mesh=mesh,
        in_specs=(feat, both, flat, flat, both, flat, feat, feat, feat, P()),
        out_specs=(both, both),
        check_vma=False,
    )
```

```python
import types

import jax
import jax.numpy as jnp
from jax import lax
from jax.experimental import pallas as pl
from jax.experimental.pallas import tpu as pltpu
from jax.sharding import PartitionSpec as P

MESH = pl.DeviceIdType.MESH
EPS = 1e-05
NZ, NY, NC, NX = 8, 4, 2, 4
N_FEAT = NZ * NY * NC
CAP, SLOTS = 12, 16
VM = 54
D = 1024
ROWS2, ROWS1, FAN, PER = 400, 20, 20, 5
PAD1, PADT = 32, 16
F32, BF16 = jnp.float32, jnp.bfloat16


def act(values):
    return values * jax.nn.sigmoid(values)


def act_slope(values):
    sig = jax.nn.sigmoid(values)
    return sig * (1.0 + values * (1.0 - sig))


def dot(a, b):
    return lax.dot_general(a, b, (((1,), (0,)), ((), ())), preferred_element_type=F32)


def dot_nt(a, b):
    return lax.dot_general(a, b, (((1,), (1,)), ((), ())), preferred_element_type=F32)


def dot_tn(a, b):
    return lax.dot_general(a, b, (((0,), (0,)), ((), ())), preferred_element_type=F32)


def split(values):
    high = values.astype(BF16)
    return high, (values - high.astype(F32)).astype(BF16)


def iota(shape, dim):
    return lax.broadcasted_iota(jnp.int32, shape, dim)


def coords():
    feat = lax.axis_index("feat")
    return feat // (NY * NC), (feat // NC) % NY, feat % NC, lax.axis_index("sect")


def device_at(z, y, c, x):
    return ((z * NY + y) * NC + c, x)


def remote(src, dst, send, recv, dev):
    copy = pltpu.make_async_remote_copy(
        src_ref=src, dst_ref=dst, send_sem=send, recv_sem=recv, device_id=dev, device_id_type=MESH)
    copy.start()
    return copy


def wait_bytes(ref, sem):
    pltpu.make_async_copy(ref, ref, sem).wait()


def row_pick(first, parity):
    m, lane = iota((D // 2, D), 0), iota((D // 2, D), 1)
    a, b, z, i = m // 128, (m // 32) % 4, (m // 4) % 8, m % 4
    y, x = (b, a) if first == "x" else (a, b)
    return (lane == z * 128 + y * 32 + parity * 16 + x * 4 + i).astype(BF16)


def line_pick(axis, c, y, x):
    m, lane = iota((128, D), 0), iota((128, D), 1)
    b, z, i = m // 32, (m // 4) % 8, m % 4
    y, x = (b, x) if axis == "x" else (y, b)
    return (lane == z * 128 + y * 32 + c * 16 + x * 4 + i).astype(BF16)


SCRATCH = [
    ("w", (NZ, NY, NC, 16, 3 * D), BF16), ("l2", (D, 3 * D), BF16), ("table", (512, D), BF16),
    ("owner", (1, ROWS2), jnp.int32), ("row", (1, ROWS2), jnp.int32), ("weight2", (1, ROWS2), jnp.int32),
    ("weight1", (1, ROWS1), jnp.int32), ("rows", (16, ROWS2), F32), ("reqs", (N_FEAT, 1, 128), F32), ("rin", (N_FEAT, 1, 128), F32),
    ("rep_out", (N_FEAT, SLOTS, 768), BF16), ("rep_in", (N_FEAT, SLOTS, 768), BF16),
    ("hop", (PAD1, D), BF16), ("nbr1", (PAD1, D), BF16), ("back1", (PAD1, D), BF16),
    ("hop8", (2, 4, PAD1, D), BF16), ("nbr8", (2, 4, PAD1, D), BF16), ("back8", (2, 2, 4, PAD1, D), BF16),
    ("tgt", (PADT, D), BF16), ("cot", (PADT, D), F32),
    ("fetched", (ROWS2, D), BF16), ("fetched_o", (ROWS2, D), BF16),
    ("bf", (2, ROWS2, 512), BF16), ("bf_o", (2, ROWS2, 512), BF16), ("mine", (2, 512, 512), F32), ("pre", (ROWS2, D), F32),
    ("vt", (D, D), BF16), ("qt", (D, D), BF16), ("pick", (2, 512, D), BF16), ("xt", (2, 512, 1024), BF16), ("ht", (128, 256), BF16), ("nt", (128, 256), BF16),
    ("msg", (4, D + 128), F32), ("msg_in", (NX - 1, 4, D + 128), F32),
    ("emb", (PADT, D), F32), ("summed", (PADT, D + 128), F32),
    ("send1", (2, 3, 128, 512), BF16), ("recv1", (2, 3, 128, 512), BF16), ("acc1", (2, 128, 512), F32),
    ("send2", (2, 3, 32, 512), BF16), ("recv2", (2, 3, 32, 512), BF16),
    ("line", (2, 128, D), F32), ("send_l", (2, 3, 32, D), BF16), ("recv_l", (2, 3, 32, D), BF16),
    ("acc2", (2, 32, 512), F32), ("accl", (32, D), F32), ("pk", (3, NZ, 16, 256), F32), ("send3", (3, NZ, 16, 256), BF16),
    ("recv3", (3, NZ - 1, 16, 256), BF16),
]
SEMS = [
    ("load", (2,)), ("index", (4,)), ("own", (3,)), ("q_send", ()), ("q_recv", ()), ("a_send", ()), ("a_recv", (4,)),
    ("z_send", (3,)), ("z_recv", (3,)), ("y_send", (3,)), ("y_recv", (3,)),
    ("x_send", (3, 4)), ("x_recv", (3, 4)), ("c_send", (3,)), ("c_recv", (3,)),
    ("p_send", (3,)), ("p_recv", (3,)), ("m_send", (3,)), ("m_recv", (3,)),
    ("s1", (2, 3)), ("r1", (2, 3)), ("s2", (2, 3)), ("r2", (2, 3)), ("sl", (2, 3)), ("rl", (2, 3)),
    ("h_send", (4,)), ("h_recv", (4,)), ("n_send", (4,)), ("n_recv", (4,)), ("b_send", (2, 4)), ("b_recv", (2, 4)), ("s3", (3, 7)), ("r3", (3, 7)),
]
INPUTS = ["owner_in", "row_in", "weight2_in", "weight1_in", "table_in", "hop_in", "tgt_in", "cot_in", "l1", "l2_in"]
OUTPUTS = ["emb_out", "grads_out"]


def step_kernel(*refs):
    names = INPUTS + OUTPUTS + [s[0] for s in SCRATCH] + [s[0] for s in SEMS]
    r = types.SimpleNamespace(**dict(zip(names, refs)))
    z, y, c, x = coords()
    me = lax.axis_index("feat")
    partner = device_at(z, y, 1 - c, x)
    xs = [device_at(z, y, c, (x + k) % NX) for k in range(NX)]
    ys = [device_at(z, (y + k) % NY, c, x) for k in range(NY)]
    zs = [device_at((z + k) % NZ, y, c, x) for k in range(NZ)]
    w = r.w

    numbers = [
        pltpu.make_async_copy(src, dst, r.index.at[n]) for n, (src, dst) in enumerate([
            (r.owner_in, r.owner), (r.row_in, r.row), (r.weight2_in, r.weight2), (r.weight1_in, r.weight1)])]
    for copy in numbers:
        copy.start()

    barrier = pltpu.get_barrier_semaphore()

    def greet(k, carry):
        pl.semaphore_signal(barrier, inc=1, device_id=((me + k) % N_FEAT, x), device_id_type=MESH)
        return carry

    lax.fori_loop(1, N_FEAT, greet, 0)
    for dev in xs[1:]:
        pl.semaphore_signal(barrier, inc=1, device_id=dev, device_id_type=MESH)

    def cols(sec, at):
        return pl.ds(pl.multiple_of(sec * D + at * 256, 256), 256)

    loads = [pltpu.make_async_copy(r.table_in, r.table, r.load.at[0]), pltpu.make_async_copy(r.l2_in, r.l2, r.load.at[1])]
    for copy in loads:
        copy.start()
    owns = [pltpu.make_async_copy(r.l1.at[:, cols(sec, x)], w.at[z, y, c, :, cols(sec, x)], r.own.at[sec]) for sec in range(3)]
    for copy in owns:
        copy.start()

    count = ROWS2
    r.rows[...] = jnp.zeros_like(r.rows)
    for copy in numbers:
        copy.wait()
    r.rows[0:1, :] = r.owner[...].astype(F32)
    r.rows[1:2, :] = (r.row[...] // 32).astype(F32)
    r.rows[2:3, :] = (r.row[...] % 32).astype(F32)
    r.rows[3:4, :] = r.weight2[...].astype(F32)
    r.rows[4:5, 0:ROWS1] = r.weight1[...].astype(F32)
    eye = (iota((16, 128), 0) == iota((16, 128), 1)).astype(BF16)
    columns = dot_tn(r.rows[...].astype(BF16), eye).astype(jnp.int32)
    weight2, weight1 = columns[:, 3:4], columns[0:PAD1, 4:5]
    owner = columns[:, 0:1]
    rel = ((owner // NC + NY - y) % NY * NC + (owner + NC - c) % NC) * NZ + (owner // (NY * NC) + NZ - z) % NZ
    member = (iota((count, N_FEAT), 1) == rel).astype(BF16)
    before = (iota((count, count), 0) > iota((count, count), 1)).astype(BF16)
    slot = jnp.sum(dot(before, member) * member.astype(F32), axis=1, keepdims=True).astype(jnp.int32)
    lane = iota((count, 128), 1)
    asked = jnp.where(lane == slot, columns[:, 1:2], 0) + jnp.where(lane == slot + SLOTS, columns[:, 2:3], 0)
    r.reqs[...] = dot_tn(member, asked.astype(F32).astype(BF16)).reshape(N_FEAT, 1, 128)
    r.rin[0] = r.reqs[0]

    pl.semaphore_wait(barrier, N_FEAT - 1 + NX - 1)

    def ask(k, carry):
        dev = device_at((z + k) % NZ, (y + k // (NZ * NC)) % NY, (c + k // NZ) % NC, x)
        remote(r.reqs.at[k], r.rin.at[k], r.q_send, r.q_recv, dev)
        return carry

    lax.fori_loop(1, N_FEAT, ask, 0)
    for sec in range(3):
        for k in (4, 3, 5, 2, 6, 1, 7):
            remote(r.l1.at[:, cols(sec, x)], w.at[z, y, c, :, cols(sec, x)], r.z_send.at[sec], r.z_recv.at[sec], zs[k])

    r.hop[...] = jnp.zeros_like(r.hop)
    r.hop[0:ROWS1, :] = r.hop_in[...]
    r.tgt[...] = jnp.zeros_like(r.tgt)
    r.tgt[0:4, :] = r.tgt_in[...]
    r.cot[...] = jnp.zeros_like(r.cot)
    r.cot[0:4, :] = r.cot_in[...].astype(F32)

    def to_line(buf, send, recv, devs):
        return [remote(buf.at[0, 0], buf.at[0, k], send.at[k - 1], recv.at[k - 1], devs[k]) for k in (2, 1, 3)]

    def to_partner(copies, buf, send, recv):
        for copy in copies:
            copy.wait_recv()
        copies.append(remote(buf.at[0], buf.at[1], send.at[3], recv.at[3], partner))

    r.hop8[0, 0] = r.hop[...]
    hop_copies = to_line(r.hop8, r.h_send, r.h_recv, xs)
    swaps = []

    for sec in range(3):
        wait_bytes(w.at[pl.ds(0, NZ - 1), y, c, :, cols(sec, x)], r.z_recv.at[sec])
        owns[sec].wait()
        for k in (2, 1, 3):
            part = w.at[:, y, c, :, cols(sec, x)]
            remote(part, part, r.y_send.at[sec], r.y_recv.at[sec], ys[k])

    loads[0].wait()
    wait_bytes(r.rin.at[pl.ds(1, N_FEAT - 1)], r.q_recv)
    wanted = r.rin[...].reshape(N_FEAT, 128).astype(BF16)
    wide = 8 * SLOTS
    at_row, at_lane = iota((wide, 128), 0) % SLOTS, iota((wide, 128), 1)

    def pick_weights(slots):
        return (32 * (at_lane == slots).astype(jnp.int32) + (at_lane == slots + SLOTS).astype(jnp.int32)).astype(F32)

    main_at = pick_weights(at_row)
    rest_at = [pick_weights(4 * j + at_row - CAP) for j in range(3)]
    is_main = iota((wide, 1), 0) % SLOTS < CAP

    def chunk(g):
        group = (iota((wide, N_FEAT), 1) == g * 8 + iota((wide, N_FEAT), 0) // SLOTS).astype(BF16)
        spread = dot(group, wanted)
        ids = iota((wide, 512), 1).astype(F32)

        def chosen(weights, keep):
            target = jnp.where(keep, jnp.sum(spread * weights, axis=1, keepdims=True), -1.0)
            return (ids == target).astype(BF16)

        main = dot(chosen(main_at, is_main), r.table[:, 0:768])
        for j in range(3):
            rest = dot(chosen(rest_at[j], jnp.logical_not(is_main)), r.table[:, 768:1024])
            both = main[:, 256 * j:256 * j + 256] + rest
            r.rep_out[pl.ds(g * 8, 8), :, 256 * j:256 * j + 256] = both.astype(BF16).reshape(8, SLOTS, 256)

    def reply(k):
        dev = device_at((z + NZ - k % NZ) % NZ, (y + NY - k // (NZ * NC)) % NY, (c + NC - k // NZ % NC) % NC, x)
        remote(r.rep_out.at[k], r.rep_in.at[k], r.a_send, r.a_recv.at[k // 16], dev)

    def serve(g, carry):
        chunk(g)
        for n in (4, 3, 5, 2, 6, 1, 7, 0):
            reply(g * 8 + n)
        return carry

    across = {}

    def along_x(sec):
        wait_bytes(w.at[:, pl.ds(0, NY - 1), c, :, cols(sec, x)], r.y_recv.at[sec])
        part = w.at[:, :, c, :, cols(sec, x)]
        for n, k in enumerate((1, 3)):
            across[sec, n] = remote(part, part, r.x_send.at[sec, n], r.x_recv.at[sec, n], xs[k])
        remote(part, part, r.c_send.at[sec], r.c_recv.at[sec], partner)

    chunk(0)
    for n in (4, 3, 5, 2, 6, 1, 7):
        reply(n)
    lax.fori_loop(1, 3, serve, 0)
    along_x(0)
    lax.fori_loop(3, 5, serve, 0)
    along_x(1)
    lax.fori_loop(5, 8, serve, 0)
    along_x(2)
    r.rep_in[0] = r.rep_out[0]
    r.pick[0] = row_pick("x", c)
    r.pick[1] = row_pick("y", c)
    loads[1].wait()
    r.vt[...] = r.l2[:, 2 * D:3 * D].T
    r.qt[...] = r.l2[:, 0:D].T

    for sec in range(3):
        for n, k in enumerate((1, 3)):
            across[sec, n].wait_recv()
            at = cols(sec, (x - k + NX) % NX)
            half = w.at[pl.ds(4 * n, 4), :, c, :, at]
            across[sec, 2 + n] = remote(half, half, r.x_send.at[sec, 2 + n], r.x_recv.at[sec, 2 + n], xs[k])
            part = w.at[:, :, c, :, at]
            remote(part, part, r.c_send.at[sec], r.c_recv.at[sec], partner)
    def unpack(part):
        low = max(16 * part, 1)
        wait_bytes(r.rep_in.at[pl.ds(low, 16 * part + 16 - low)], r.a_recv.at[part])
        answers = r.rep_in[16 * part:16 * part + 16].reshape(256, 768)
        places = iota((count, 256), 1) + 256 * part
        base = rel * SLOTS
        main = dot((places == base + slot).astype(BF16), answers)
        rest = jnp.zeros((count, 256), F32)
        for j in range(3):
            place = jnp.where(slot // 4 == j, base + CAP + slot % 4, -1)
            rest = rest + dot((places == place).astype(BF16), answers[:, 256 * j:256 * j + 256])
        if part:
            main, rest = main + r.pre[:, 0:768], rest + r.pre[:, 768:1024]
        r.pre[:, 0:768] = main
        r.pre[:, 768:1024] = rest

    unpack(0)
    for sec in range(3):
        for n in range(2):
            across[sec, 2 + n].wait_recv()
            half = w.at[pl.ds(4 * n, 4), :, c, :, cols(sec, (x + 2) % NX)]
            remote(half, half, r.c_send.at[sec], r.c_recv.at[sec], partner)
    unpack(1)
    for sec in range(3):
        wait_bytes(w.at[:, :, c, :, pl.ds(sec * D, D)], r.c_recv.at[sec])

    def one(sec):
        return w[:, :, :, :, sec * D:sec * D + D].reshape(D, D)

    def two(sec):
        return r.l2[:, sec * D:sec * D + D]

    to_partner(hop_copies, r.hop8, r.h_send, r.h_recv)
    pre1_self = dot(r.hop[...], one(1))
    pre2_self = dot(r.tgt[...], two(1))
    hop_copies[3].wait_recv()
    r.ht[...] = dot_nt(line_pick("x", c, y, x), r.hop8[...].reshape(256, D)).astype(BF16)
    of_node = jnp.where(iota((count, PAD1), 0) // FAN == iota((count, PAD1), 1), weight2, 0).astype(F32).astype(BF16)
    at_node = jnp.where(iota((PAD1, count), 1) // FAN == iota((PAD1, count), 0), r.weight2[...], 0).astype(F32)
    total2 = jnp.maximum(jnp.sum(at_node, axis=1, keepdims=True), 1.0)
    at_node = at_node.astype(BF16)
    unpack(2)
    unpack(3)
    r.fetched[...] = r.pre[...].astype(BF16)
    swaps.append(remote(r.fetched, r.fetched_o, r.p_send.at[0], r.p_recv.at[0], partner))

    for n in range(4):
        at = slice(256 * n, 256 * n + 256)
        pre = dot(r.fetched[...], w[:, :, :, :, at].reshape(D, 256))
        sig = jax.nn.sigmoid(pre)
        high, low = split(pre * sig)
        r.pre[:, at] = sig * (1.0 + pre * (1.0 - sig))
        r.nbr1[:, at] = ((dot(at_node, high) + dot(at_node, low)) / total2).astype(BF16)
    r.nbr8[0, 0] = r.nbr1[...]
    nbr_copies = to_line(r.nbr8, r.n_send, r.n_recv, ys)
    pre1 = pre1_self + dot(r.nbr1[...], one(2))
    gated1 = act(pre1)
    scale1 = lax.rsqrt(jnp.mean(gated1 * gated1, axis=-1, keepdims=True) + EPS)
    norm1 = gated1 * scale1

    pre_hop1 = dot(norm1.astype(BF16), two(0))
    of_target = jnp.where(iota((PAD1, PADT), 0) // PER == iota((PAD1, PADT), 1), weight1, 0).astype(F32).astype(BF16)
    high, low = split(act(pre_hop1))
    numer = dot_tn(of_target, high) + dot_tn(of_target, low)
    weight = dot_tn(of_target, jnp.ones((PAD1, 128), BF16))
    r.msg[:, 0:D] = numer[0:4]
    r.msg[:, D:D + 128] = weight[0:4]
    sums = [remote(r.msg, r.msg_in.at[k - 1], r.m_send.at[k - 1], r.m_recv.at[k - 1], xs[k]) for k in (1, 2, 3)]
    slope_hop1 = act_slope(pre_hop1)
    slope1 = act_slope(pre1)
    swaps[0].wait_recv()
    for part in range(2):
        r.xt[part, :, 0:count] = dot_nt(r.pick[part], r.fetched[...]).astype(BF16)
        r.xt[part, :, 512:512 + count] = dot_nt(r.pick[part], r.fetched_o[...]).astype(BF16)
    for copy in sums:
        copy.wait_recv()
    r.summed[...] = jnp.zeros_like(r.summed)
    r.summed[0:4, :] = r.msg[...] + r.msg_in[0] + r.msg_in[1] + r.msg_in[2]
    summed = r.summed[...]
    total1 = jnp.maximum(summed[:, D:D + 1], 1.0)
    nbr2 = (summed[:, 0:D] / total1).astype(BF16)
    pre2 = pre2_self + dot(nbr2, two(2))
    gated2 = act(pre2)
    scale2 = lax.rsqrt(jnp.mean(gated2 * gated2, axis=-1, keepdims=True) + EPS)
    norm2 = gated2 * scale2
    r.emb[...] = norm2
    cot = r.cot[...]
    back2 = (scale2 * (cot - norm2 * jnp.mean(cot * norm2, axis=-1, keepdims=True)) * act_slope(pre2)).astype(BF16)
    back_nbr2 = dot(back2, r.vt[...])
    high, low = split(back_nbr2 / total1)
    back_hop1 = ((dot(of_target, high) + dot(of_target, low)) * slope_hop1).astype(BF16)
    back_h1 = dot(back_hop1, r.qt[...])
    back1 = (scale1 * (back_h1 - norm1 * jnp.mean(back_h1 * norm1, axis=-1, keepdims=True)) * slope1).astype(BF16)
    r.back1[...] = back1
    back_copies = []
    for n, devs in enumerate((xs, ys)):
        r.back8[n, 0, 0] = back1
        back_copies.append(to_line(r.back8.at[n], r.b_send.at[n], r.b_recv.at[n], devs))

    first, second, third, lines = {}, {}, {}, {}

    def start_first(k):
        for part in range(2):
            at = pl.ds(pl.multiple_of(lax.rem((x if part == 0 else y) + k, 4) * 128, 128), 128)
            v = r.mine[part, at, :] + dot(r.xt[part, at, 512:512 + count], r.bf_o[part])
            if k == 0:
                r.acc1[part] = v
            else:
                r.send1[part, k - 1] = v.astype(BF16)
                first[part, k] = remote(
                    r.send1.at[part, k - 1], r.recv1.at[part, k - 1], r.s1.at[part, k - 1], r.r1.at[part, k - 1],
                    (xs, ys)[part][k])

    def start_second():
        for part in range(2):
            for k in (1, 3, 2):
                first[part, k].wait_recv()
            r.acc1[part] = (
                r.acc1[part] + r.recv1[part, 0].astype(F32) + r.recv1[part, 1].astype(F32) + r.recv1[part, 2].astype(F32))
            for k in (2, 1, 3):
                at = lax.rem((y if part == 0 else x) + k, 4)
                r.send2[part, k - 1] = r.acc1[part, pl.ds(pl.multiple_of(at * 32, 32), 32), :].astype(BF16)
                second[part, k] = remote(
                    r.send2.at[part, k - 1], r.recv2.at[part, k - 1], r.s2.at[part, k - 1], r.r2.at[part, k - 1],
                    (ys, xs)[part][k])

    def start_line(n, rows):
        back_copies[n][3].wait_recv()
        r.line[n] = dot(rows, r.back8[n].reshape(256, D))
        for k in (2, 1, 3):
            at = lax.rem((y if n == 0 else x) + k, 4)
            r.send_l[n, k - 1] = r.line[n, pl.ds(pl.multiple_of(at * 32, 32), 32), :].astype(BF16)
            lines[n, k] = remote(
                r.send_l.at[n, k - 1], r.recv_l.at[n, k - 1], r.sl.at[n, k - 1], r.rl.at[n, k - 1], (ys, xs)[n][k])

    def start_third(sec):
        r.send3[sec] = r.pk[sec].astype(BF16)
        for k in (4, 3, 5, 2, 6, 1, 7):
            third[sec, k] = remote(
                r.send3.at[sec, lax.rem(z + k, NZ)], r.recv3.at[sec, k - 1], r.s3.at[sec, k - 1], r.r3.at[sec, k - 1], zs[k])

    def third_of_line(n):
        for k in (1, 3, 2):
            lines[n, k].wait_recv()
        own = pl.ds(pl.multiple_of((y if n == 0 else x) * 32, 32), 32)
        r.accl[...] = (
            r.line[n, own, :] + r.recv_l[n, 0].astype(F32) + r.recv_l[n, 1].astype(F32) + r.recv_l[n, 2].astype(F32))
        for zz in range(NZ):
            for q in range(4):
                r.pk[n + 1, zz, 4 * q:4 * q + 4, :] = r.accl[4 * zz:4 * zz + 4, 256 * q:256 * q + 256]
        start_third(n + 1)

    def third_of_fetch():
        for part in range(2):
            for k in (1, 3, 2):
                second[part, k].wait_recv()
            at = y if part == 0 else x
            r.acc2[part] = (
                r.acc1[part, pl.ds(pl.multiple_of(at * 32, 32), 32), :] + r.recv2[part, 0].astype(F32)
                + r.recv2[part, 1].astype(F32) + r.recv2[part, 2].astype(F32))
            for zz in range(NZ):
                for h in range(2):
                    q = 2 * part + h
                    r.pk[0, zz, 4 * q:4 * q + 4, :] = r.acc2[part, 4 * zz:4 * zz + 4, 256 * h:256 * h + 256]
        start_third(0)

    def finish(sec):
        value = r.pk[sec, z]
        for k in (1, 7, 2, 6, 3, 5, 4):
            third[sec, k].wait_recv()
            value = value + r.recv3[sec, k - 1].astype(F32)
        r.pk[sec, 0] = value
        for q in range(4):
            r.grads_out[:, sec * D + 256 * q:sec * D + 256 * q + 256] = r.pk[sec, 0, 4 * q:4 * q + 4, :]

    back_nbr1 = dot_nt(r.back1[...], one(2)) / total2
    of_node = jnp.concatenate([of_node, of_node], axis=1)
    terms = jnp.concatenate(split(back_nbr1), axis=0)
    for part in range(2):
        at = slice(512 * part, 512 * part + 512)
        r.bf[part] = (dot(of_node, terms[:, at]) * r.pre[:, at]).astype(BF16)
        swaps.append(remote(r.bf.at[part], r.bf_o.at[part], r.p_send.at[1 + part], r.p_recv.at[1 + part], partner))
    to_partner(nbr_copies, r.nbr8, r.n_send, r.n_recv)
    for part in range(2):
        r.mine[part] = dot(r.xt[part, :, 0:count], r.bf[part])
    swaps[1].wait_recv()
    swaps[2].wait_recv()
    start_first(2)
    r.emb_out[...] = r.emb[pl.ds(x, 1), :]
    for n in range(2):
        to_partner(back_copies[n], r.back8.at[n], r.b_send.at[n], r.b_recv.at[n])
    start_first(1)
    start_first(3)
    start_line(0, r.ht[...])
    nbr_copies[3].wait_recv()
    r.nt[...] = dot_nt(line_pick("y", c, y, x), r.nbr8[...].reshape(256, D)).astype(BF16)
    start_line(1, r.nt[...])
    start_first(0)
    start_second()
    third_of_line(0)
    third_of_line(1)
    third_of_fetch()
    finish(1)
    finish(2)
    finish(0)

    wait_bytes(r.reqs.at[pl.ds(1, N_FEAT - 1)], r.q_send)
    wait_bytes(r.rep_out.at[pl.ds(1, N_FEAT - 1)], r.a_send)
    for sec in range(3):
        wait_bytes(w.at[pl.ds(0, NZ - 1), y, c, :, cols(sec, x)], r.z_send.at[sec])
        wait_bytes(w.at[:, pl.ds(0, NY - 1), c, :, cols(sec, x)], r.y_send.at[sec])
        wait_bytes(w.at[:, :, c, :, pl.ds(sec * D, D)], r.c_send.at[sec])
    for copy in list(across.values()) + swaps + sums + hop_copies + nbr_copies + back_copies[0] + back_copies[1]:
        copy.wait_send()
    for copy in list(first.values()) + list(second.values()) + list(lines.values()) + list(third.values()):
        copy.wait_send()


def on_device(
    table, hop2_owner, hop2_row, hop2_weight, hop1_feats, hop1_weight, target_feats, cotangent, layer_one, layer_two,
):
    vmem, anywhere = pl.BlockSpec(memory_space=pltpu.VMEM), pl.BlockSpec(memory_space=pl.ANY)
    emb, grads = pl.pallas_call(
        step_kernel,
        out_shape=(jax.ShapeDtypeStruct((1, D), F32), jax.ShapeDtypeStruct((4, 3 * D), F32)),
        in_specs=[anywhere, anywhere, anywhere, anywhere, anywhere, vmem, vmem, vmem, anywhere, anywhere],
        out_specs=(vmem, vmem),
        scratch_shapes=[pltpu.VMEM(s, t) for _, s, t in SCRATCH] + [pltpu.SemaphoreType.DMA(s) for _, s in SEMS],
        compiler_params=pltpu.CompilerParams(collective_id=1, has_side_effects=True, vmem_limit_bytes=VM * 1024 * 1024),
        name="step",
    )(
        hop2_owner.reshape(1, ROWS2), hop2_row.reshape(1, ROWS2), hop2_weight.reshape(1, ROWS2), hop1_weight.reshape(1, ROWS1), table, hop1_feats, target_feats, cotangent, layer_one, layer_two)

    def hand_over(emb_ref, grads_ref, emb_out, grads_out):
        emb_out[...] = emb_ref[...].astype(BF16)
        grads_out[...] = grads_ref[...]

    return pl.pallas_call(
        hand_over,
        out_shape=(jax.ShapeDtypeStruct((1, D), BF16), jax.ShapeDtypeStruct((4, 3 * D), F32)),
        in_specs=[vmem, vmem],
        out_specs=(vmem, vmem),
        name="hand_over",
    )(emb, grads)


def solution(mesh):
    both = P(("feat", "sect"), None)
    flat = P(("feat", "sect"))
    feat = P("feat", None)
    return jax.shard_map(
        on_device,
        mesh=mesh,
        in_specs=(feat, both, flat, flat, both, flat, feat, feat, feat, P()),
        out_specs=(both, both),
        check_vma=False,
    )
```
